32 devices in a mesh: tm: 4 (over y, x), tmpl: 8 (over z, core).
Axes of the slice: x: 2, y: 2, z: 4, core: 2. Of those that a mesh axis runs over, the one named last changes fastest.
Arguments:
- strain: float32 [65536], P(('tm', 'tmpl')), may hold values from -40 to 40, as said below
- templates: bfloat16 [2, 128, 2048], P(None, 'tmpl', 'tm'), may hold values from -6 to 6
- cutoff: int32 [128], P('tmpl'), may hold values from 512 to 2048
Outputs:
- snr_peak: float32 [32, 128], P('tm', 'tmpl')
The draws below stay inside these ranges and needn't reach their ends.
Inputs may be any that keep to these rules, and one draw needn't show every extreme that they name: `strain`: one contiguous record of 65536 samples.
All inputs are finite; a program needn't handle non-finite values.
Results may differ from the reference program's by a relative error of at most 0.00098.
Values may be sent and summed in bfloat16 or wider, within the bound.
No kernel may reach another device: no remote copies, remote signals or barrier semaphores. Data moves between devices by JAX's collectives and lax.ppermute only.
A program may use at most 64 MiB of HBM per device.

```python
import math
import jax
import jax.numpy as jnp
from jax import lax

NFFT = 4096
BINS = 2048
HOP = 2048
SEGS = 32
SAMPLES = 65536
TEMPLATES = 128


def draw_strain(key, part):
    key = jax.random.fold_in(key, 11)
    subkeys = jax.random.split(key, 4)
    sample = jnp.arange(SAMPLES, dtype=jnp.int32)
    random_noise = jnp.clip(jax.random.normal(subkeys[0], (SAMPLES,), jnp.float32), -6.0, 6.0)
    growth = 2.0
    line_bins = jax.random.randint(subkeys[1], (8, 1), 1, BINS, dtype=jnp.int32)
    line_amps = jnp.exp(jax.random.uniform(subkeys[2], (8, 1), jnp.float32, math.log(0.01), math.log(0.1)))
    line_phase = jax.random.uniform(subkeys[3], (8, 1), jnp.float32, -math.pi, math.pi)
    line_cycle = (line_bins * (sample % NFFT)[None, :] % NFFT).astype(jnp.float32)
    line_sum = jnp.sum(line_amps * jnp.cos(2.0 * math.pi * line_cycle / NFFT + line_phase), axis=0)
    amplitude = 1.0 + growth * sample.astype(jnp.float32) / SAMPLES
    return amplitude * (random_noise + line_sum)


def set_ends(values, key, least, largest):
    place = [jax.random.randint(jax.random.fold_in(key, axis), (), 0, length) for axis, length in enumerate(values.shape)]
    widest = values.shape.index(max(values.shape))
    beside = place[:widest] + [(place[widest] + 1) % values.shape[widest]] + place[widest + 1:]
    return values.at[tuple(place)].set(least).at[tuple(beside)].set(largest)


def block_scale(stream_key, dims, cuts, low, top_value):
    factor_of = 1.0
    for axis_at, shards_of in cuts:
        steps = jax.random.uniform(jax.random.fold_in(jax.random.fold_in(stream_key, 6), axis_at), (shards_of,), jnp.float32, low / len(cuts), top_value / len(cuts))
        factor_of = factor_of * jnp.repeat(jnp.exp(steps), dims[axis_at] // shards_of).reshape((-1,) + (1,) * (len(dims) - 1 - axis_at))
    return factor_of


def gaussian(own_key, shape, scale, limit, pieces=(), held_as=jnp.bfloat16):
    level = block_scale(own_key, shape, pieces, -0.22, 0.18) if pieces else 1.0
    array = jax.random.normal(own_key, shape, jnp.float32) * scale * level
    return jnp.minimum(jnp.maximum(array, -limit), limit).astype(held_as)


def setup_inputs(seed: int = 0) -> dict:
    splits = jax.random.split(jax.random.key(seed), 4)
    return {
        "strain": draw_strain(jax.random.fold_in(splits[3], 71), 0),
        "templates": gaussian(splits[1], (2, TEMPLATES, BINS), 1.0, 6.0, ((1, 8), (2, 4))),
        "cutoff": set_ends(jax.random.randint(splits[2], (TEMPLATES,), BINS // 4, BINS + 1), jax.random.fold_in(splits[2], 1), BINS // 4, BINS).astype(jnp.int32),
    }


def hann_window():
    sample = jnp.arange(NFFT, dtype=jnp.float32)
    return 0.5 - 0.5 * jnp.cos(2.0 * jnp.pi * sample / NFFT)

def reference(strain, templates, cutoff):
    window = hann_window()
    norm_window = jnp.sum(window * window)
    extended = jnp.concatenate([strain, strain[:HOP]]).reshape(SEGS + 1, HOP)
    frames = jnp.concatenate([extended[:-1], extended[1:]], axis=1) * window
    spectrum = jnp.fft.rfft(frames, axis=1)[:, :BINS]
    spec_real = jnp.real(spectrum)
    spec_imag = jnp.imag(spectrum)
    total_power = lax.optimization_barrier(jnp.sum(spec_real * spec_real + spec_imag * spec_imag, axis=0))
    density = total_power / (SEGS * norm_window) + 1e-06
    white_real = (spec_real / density).astype(jnp.bfloat16).astype(jnp.float32)
    white_imag = (spec_imag / density).astype(jnp.bfloat16).astype(jnp.float32)
    tmpl_real = templates[0].astype(jnp.float32)
    tmpl_imag = templates[1].astype(jnp.float32)
    bin_ids = jnp.arange(BINS, dtype=jnp.int32)
    keep_mask = (bin_ids[None, :] < cutoff[:, None]).astype(jnp.float32)
    norm_squares = lax.optimization_barrier(jnp.sum(keep_mask * (tmpl_real * tmpl_real + tmpl_imag * tmpl_imag) / density, axis=1))

    def one_template(index):
        row_real = tmpl_real[index][None, :]
        row_imag = tmpl_imag[index][None, :]
        row_keep = keep_mask[index][None, :]
        prod_real = ((row_real * white_real + row_imag * white_imag) * row_keep).astype(jnp.bfloat16)
        prod_imag = ((row_real * white_imag - row_imag * white_real) * row_keep).astype(jnp.bfloat16)
        prod_real = lax.optimization_barrier(prod_real).astype(jnp.float32)
        prod_imag = lax.optimization_barrier(prod_imag).astype(jnp.float32)
        complex_rows = prod_real + 1j * prod_imag
        padded = jnp.pad(complex_rows, ((0, 0), (0, NFFT - BINS)))
        series = jnp.fft.ifft(padded, axis=1) * NFFT
        return lax.optimization_barrier(jnp.max(jnp.abs(series), axis=1))
    peak_values = lax.map(one_template, jnp.arange(TEMPLATES, dtype=jnp.int32))
    norm_scale = jnp.sqrt(norm_squares) * jnp.sqrt(norm_window)
    return (peak_values / norm_scale[:, None]).T
```

```python
import functools
import math

import jax
import jax.numpy as jnp
import ml_dtypes
import numpy as np
from jax import lax
from jax.experimental import pallas as pl
from jax.experimental.pallas import tpu as pltpu
from jax.sharding import PartitionSpec as P

NFFT = 4096
BINS = 2048
HOP = 2048
LANES = 128
ROWS = HOP // LANES
FINE = 32
GROUP = 8
FLOOR = 1e-6

ROOT_SCALE = {128: 1.66575, 64: 1.66575, 32: 1.6245, 16: 1.6245, 8: 1.6245}


def root_order(index, period):
    return period // math.gcd(int(index), period)


def row_scale(count, period):
    return np.array([ROOT_SCALE.get(root_order(i, period), 1.0) for i in range(count)])


def as_bf16(table):
    return np.asarray(table, np.float32).astype(ml_dtypes.bfloat16)


def two_parts(table):
    high = as_bf16(table)
    low = as_bf16(np.asarray(table, np.float64) - high.astype(np.float64))
    return high, low


def turn(left, right, period):
    angle = 2.0 * np.pi * (np.outer(left, right) % period) / period
    return np.cos(angle), np.sin(angle)


@functools.lru_cache(maxsize=None)
def tables():
    eye = np.eye(GROUP)
    fine, wide, rows = np.arange(FINE), np.arange(LANES), np.arange(ROWS)
    window = 0.5 - 0.5 * np.cos(2.0 * np.pi * np.arange(NFFT) / NFFT)
    cos, sin = turn(fine, fine, FINE)
    first = np.concatenate([np.kron(eye, cos), np.kron(eye, -sin)], axis=0)
    first_high, first_low = two_parts(first)
    fwd_cos, fwd_sin = turn(fine, wide, NFFT)
    f_order = np.array([4 * d + g for g in range(4) for d in range(ROWS)])
    cos, sin = turn(wide, f_order, LANES)
    second = np.block([[cos, -sin], [sin, cos]])
    second_high, second_low = two_parts(second)
    scale_q = row_scale(FINE, FINE)
    scale_c = row_scale(LANES, LANES)
    cos, sin = turn(fine, rows, FINE)
    cos, sin = cos * scale_q[:, None], sin * scale_q[:, None]
    third = np.block([[np.kron(eye, cos), np.kron(eye, -sin)], [np.kron(eye, sin), np.kron(eye, cos)]])
    inv_cos, inv_sin = turn(fine, wide, NFFT)
    undo = 1.0 / (scale_q[:, None] * scale_c[None, :])
    cos, sin = turn(wide, wide, LANES)
    cos, sin = cos * scale_c[:, None], sin * scale_c[:, None]
    fourth = np.block([[cos, sin], [-sin, cos]])
    order = np.zeros((ROWS * 16, ROWS * 16))
    for m in range(16):
        for d in range(ROWS):
            order[m * ROWS + d, d * 16 + m] = 1.0
    f32 = lambda t: np.asarray(t, np.float32)
    return dict(
        window=f32(window.reshape(2 * ROWS, LANES)),
        first_high=first_high,
        first_low=first_low,
        fwd=f32(np.stack([fwd_cos, fwd_sin])),
        second_both=np.concatenate([second_high, second_low], axis=1),
        third=as_bf16(third),
        inv=f32(np.stack([inv_cos * undo, inv_sin * undo])),
        fourth=as_bf16(fourth),
        order=as_bf16(order),
    ), float((window * window).sum())


def dot(left, right):
    return jnp.dot(left, right, preferred_element_type=jnp.float32)


def split(value):
    high = value.astype(jnp.bfloat16)
    return high, (value - high.astype(jnp.float32)).astype(jnp.bfloat16)


def repeat(count, body, carry):
    if count <= 8:
        for step in range(count):
            carry = body(step, carry)
        return carry
    return lax.fori_loop(0, count, body, carry)


def filter_kernel(
    segs, own, energy, place, cutoff, strain, tmpl, window, first_high, first_low, fwd,
    second_both, third, inv, fourth, order, out, spec, bank,
):
    tmpl_count = tmpl.shape[2]
    w_low, w_high = window[:ROWS][None], window[ROWS:][None]
    fwd_cos, fwd_sin = fwd[0][None], fwd[1][None]

    def frames(start, last):
        here = strain[pl.ds(start, GROUP)]
        if last:
            after = jnp.concatenate([strain[pl.ds(start + 1, GROUP - 1)], strain[pl.ds(0, 1)]], axis=0)
        else:
            after = strain[pl.ds(start + 1, GROUP)]
        both = jnp.concatenate([here * w_low, after * w_high], axis=1)
        return both.reshape(GROUP * FINE, LANES)

    def forward(start, power, last):
        pair = jnp.concatenate([frames(start, False), frames(start + GROUP, last)], axis=1)
        high, low = split(pair)
        step = dot(first_high[...], high) + dot(first_high[...], low) + dot(first_low[...], high)
        half = GROUP * FINE
        for h in range(2):
            re = step[:half, h * LANES:(h + 1) * LANES].reshape(GROUP, FINE, LANES)
            im = step[half:, h * LANES:(h + 1) * LANES].reshape(GROUP, FINE, LANES)
            turned = jnp.concatenate([re * fwd_cos + im * fwd_sin, im * fwd_cos - re * fwd_sin], axis=2)
            high, low = split(turned.reshape(half, 2 * LANES))
            wide = dot(high, second_both[...])
            value = wide[:, :LANES] + wide[:, LANES:] + dot(low, second_both[:, :LANES])
            at = (start + h * GROUP) * FINE
            spec[pl.ds(at, half)] = value
            power = power + jnp.sum((value * value).reshape(GROUP, FINE, LANES), axis=0)
        return power

    power = jnp.zeros((FINE, LANES), jnp.float32)
    pairs = segs // (2 * GROUP)
    power = repeat(pairs - 1, lambda i, p: forward(i * 2 * GROUP, p, False), power)
    power = forward((pairs - 1) * 2 * GROUP, power, True)
    power = power + pltpu.roll(power, LANES // 2, 1)
    density = power / (segs * energy) + FLOOR

    lane = lax.broadcasted_iota(jnp.int32, (ROWS, LANES), 1)
    row = lax.broadcasted_iota(jnp.int32, (ROWS, LANES), 0)
    bins = row * LANES + lane
    part = lane // FINE

    def gather_lanes(flipped, at, source):
        result = None
        for g in range(4):
            piece = flipped[at + g * ROWS:at + (g + 1) * ROWS]
            if source is not None and g != source:
                piece = pltpu.roll(piece, ((g - source) % 4) * FINE, 1)
            result = piece if g == 0 else jnp.where(part == g, piece, result)
        return result

    inverse_density = gather_lanes((1.0 / jnp.concatenate([density] * 4, axis=0)).T, 0, None)

    pieces = [
        jnp.concatenate(
            [tmpl[j, part_at, :, at:at + LANES] for j in range(tmpl.shape[0]) for at in range(0, tmpl.shape[3], LANES)],
            axis=0,
        )
        for part_at in range(2)
    ]
    bank[...] = dot(order[...], jnp.concatenate(pieces, axis=1))

    inv_cos, inv_sin = inv[0][None], inv[1][None]
    column = lax.broadcasted_iota(jnp.int32, (GROUP, LANES), 1)

    def block(number, _):
        at = pl.multiple_of((place[0] * own + number * GROUP) * FINE, GROUP * FINE)
        white = spec[pl.ds(at, GROUP * FINE)].reshape(GROUP, FINE, LANES) / density[None]
        white = white.astype(jnp.bfloat16).astype(jnp.float32).reshape(2, 4 * FINE, LANES)
        re_parts, im_parts = [], []
        for half in range(2):
            flipped = white[half].T
            for s in range(4):
                re_parts.append(gather_lanes(flipped, 0, s))
                im_parts.append(gather_lanes(flipped, LANES // 2, s))
        white_re = jnp.stack(re_parts)
        white_im = jnp.stack(im_parts)

        def pair_of(step, result):
            sides, norms = [], []
            for side in range(2):
                m = 2 * step + side
                rows = pl.ds(m * ROWS, ROWS)
                keep = bins < cutoff[m]
                h_re = jnp.where(keep, bank[rows, :LANES], 0.0)
                h_im = jnp.where(keep, bank[rows, LANES:], 0.0)
                norms.append(jnp.sum((h_re * h_re + h_im * h_im) * inverse_density, keepdims=True))
                c_re = h_re[None] * white_re + h_im[None] * white_im
                c_im = h_re[None] * white_im - h_im[None] * white_re
                both = jnp.concatenate([c_re, c_im], axis=0).reshape(2 * GROUP * ROWS, LANES)
                sides.append(both.astype(jnp.bfloat16))
            section = dot(third[...], jnp.concatenate(sides, axis=1))
            half = GROUP * FINE
            for side in range(2):
                re = section[:half, side * LANES:(side + 1) * LANES].reshape(GROUP, FINE, LANES)
                im = section[half:, side * LANES:(side + 1) * LANES].reshape(GROUP, FINE, LANES)
                turned = jnp.concatenate([re * inv_cos - im * inv_sin, re * inv_sin + im * inv_cos], axis=2)
                wave = dot(turned.reshape(half, 2 * LANES).astype(jnp.bfloat16), fourth[...])
                square = wave[:, :LANES] * wave[:, :LANES] + wave[:, LANES:] * wave[:, LANES:]
                top = jnp.max(jnp.max(square.reshape(GROUP, FINE, LANES), axis=1), axis=1, keepdims=True)
                value = jnp.sqrt(top) / (jnp.sqrt(norms[side]) * math.sqrt(energy))
                result = jnp.where(column == 2 * step + side, value, result)
            return result

        result = repeat(tmpl_count // 2, pair_of, jnp.zeros((GROUP, LANES), jnp.float32))
        out[pl.ds(number * GROUP, GROUP)] = result[:, :tmpl_count]
        return _

    repeat(own // GROUP, block, 0)


def on_device(strain, templates, cutoff):
    tm, devices = lax.axis_size("tm"), lax.axis_size("tm") * lax.axis_size("tmpl")
    segs = devices * (strain.shape[0] // HOP)
    own = segs // tm
    chunk = strain.reshape(1, ROWS, LANES)
    record = lax.all_to_all(
        jnp.broadcast_to(chunk, (devices, ROWS, LANES)), ("tm", "tmpl"), split_axis=0, concat_axis=0, tiled=True
    )
    bank = lax.all_to_all(
        jnp.broadcast_to(templates[None], (tm,) + templates.shape), "tm", split_axis=0, concat_axis=0, tiled=True
    )
    place = lax.axis_index("tm").astype(jnp.int32).reshape(1)
    held, energy = tables()
    smem = pl.BlockSpec(memory_space=pltpu.SMEM)
    vmem = pl.BlockSpec(memory_space=pltpu.VMEM)
    return pl.pallas_call(
        functools.partial(filter_kernel, segs, own, energy),
        out_shape=jax.ShapeDtypeStruct((own, templates.shape[1]), jnp.float32),
        in_specs=[smem, smem] + [vmem] * (2 + len(held)),
        out_specs=vmem,
        scratch_shapes=[
            pltpu.VMEM((segs * FINE, LANES), jnp.float32),
            pltpu.VMEM((templates.shape[1] * ROWS, 2 * LANES), jnp.float32),
        ],
        compiler_params=pltpu.CompilerParams(vmem_limit_bytes=48 * 1024 * 1024),
        name="matched_filter",
    )(place, cutoff, record, bank, *[jnp.asarray(t) for t in held.values()])


def solution(mesh):
    in_specs = (P(("tm", "tmpl")), P(None, "tmpl", "tm"), P("tmpl"))
    out_specs = P("tm", "tmpl")
    return jax.shard_map(
        on_device, mesh=mesh, in_specs=in_specs, out_specs=out_specs, check_vma=False
    )
```

```python
import functools
import math

import jax
import jax.numpy as jnp
import ml_dtypes
import numpy as np
from jax import lax
from jax.experimental import pallas as pl
from jax.experimental.pallas import tpu as pltpu
from jax.sharding import PartitionSpec as P

NFFT = 4096
BINS = 2048
HOP = 2048
LANES = 128
ROWS = HOP // LANES
FINE = 32
GROUP = 8
FLOOR = 1e-6

ROOT_SCALE = {128: 1.66575, 64: 1.66575, 32: 1.6245, 16: 1.6245, 8: 1.6245}


def root_order(index, period):
    return period // math.gcd(int(index), period)


def row_scale(count, period):
    return np.array([ROOT_SCALE.get(root_order(i, period), 1.0) for i in range(count)])


def as_bf16(table):
    return np.asarray(table, np.float32).astype(ml_dtypes.bfloat16)


def two_parts(table):
    high = as_bf16(table)
    low = as_bf16(np.asarray(table, np.float64) - high.astype(np.float64))
    return high, low


def turn(left, right, period):
    angle = 2.0 * np.pi * (np.outer(left, right) % period) / period
    return np.cos(angle), np.sin(angle)


@functools.lru_cache(maxsize=None)
def tables():
    eye = np.eye(GROUP)
    fine, wide, rows = np.arange(FINE), np.arange(LANES), np.arange(ROWS)
    window = 0.5 - 0.5 * np.cos(2.0 * np.pi * np.arange(NFFT) / NFFT)
    cos, sin = turn(fine, fine, FINE)
    halves = np.zeros((GROUP + 1, GROUP, FINE))
    for s in range(GROUP):
        halves[s, s] = 1.0
    halves[GROUP - 1, GROUP - 1, ROWS:] = 0.0
    halves[GROUP, GROUP - 1, ROWS:] = 1.0
    spread = lambda t: (halves[:, None] * t[None, :, None, :]).reshape((GROUP + 1) * FINE, GROUP * FINE)
    first = np.concatenate([spread(cos), spread(-sin)], axis=0)
    first_high, first_low = two_parts(first)
    fwd_cos, fwd_sin = turn(fine, wide, NFFT)
    f_order = np.array([4 * d + g for g in range(4) for d in range(ROWS)])
    cos, sin = turn(wide, f_order, LANES)
    second = np.block([[cos, -sin], [sin, cos]])
    second_high, second_low = two_parts(second)
    scale_q = row_scale(FINE, FINE)
    scale_c = row_scale(LANES, LANES)
    cos, sin = turn(fine, rows, FINE)
    cos, sin = cos * scale_q[:, None], sin * scale_q[:, None]
    third = np.block([[np.kron(eye, cos), np.kron(eye, -sin)], [np.kron(eye, sin), np.kron(eye, cos)]])
    inv_cos, inv_sin = turn(fine, wide, NFFT)
    undo = 1.0 / (scale_q[:, None] * scale_c[None, :])
    cos, sin = turn(wide, wide, LANES)
    cos, sin = cos * scale_c[:, None], sin * scale_c[:, None]
    fourth = np.block([[cos, sin], [-sin, cos]])
    order = np.zeros((ROWS * 16, ROWS * 16))
    for m in range(16):
        for d in range(ROWS):
            order[m * ROWS + d, d * 16 + m] = 1.0
    f32 = lambda t: np.asarray(t, np.float32)
    return dict(
        window=f32(window.reshape(2 * ROWS, LANES)),
        first_high=first_high,
        first_low=first_low,
        fwd=f32(np.stack([fwd_cos, fwd_sin])),
        second_both=np.concatenate([second_high, second_low], axis=1),
        third=as_bf16(third),
        inv=f32(np.stack([inv_cos * undo, inv_sin * undo])),
        fourth=as_bf16(fourth),
        order=as_bf16(order),
    ), float((window * window).sum())


def dot(left, right):
    return jnp.dot(left, right, preferred_element_type=jnp.float32)


def split(value):
    high = value.astype(jnp.bfloat16)
    return high, (value - high.astype(jnp.float32)).astype(jnp.bfloat16)


def repeat(count, body, carry):
    if count <= 8:
        for step in range(count):
            carry = body(step, carry)
        return carry
    return lax.fori_loop(0, count, body, carry)


def natural(flipped, at, source):
    part = lax.broadcasted_iota(jnp.int32, (ROWS, LANES), 1) // FINE
    result = None
    for g in range(4):
        piece = flipped[at + g * ROWS:at + (g + 1) * ROWS]
        if g != source:
            piece = pltpu.roll(piece, ((g - source) % 4) * FINE, 1)
        result = piece if g == 0 else jnp.where(part == g, piece, result)
    return result


def forward_kernel(devices, *refs):
    chunks = refs[:devices]
    window, first_high, first_low, fwd, second_both, spec, sent, record = refs[devices:]
    rank = lax.axis_index("tmpl")
    size = chunks[0].shape[0]
    for shift, chunk in enumerate(chunks):
        record[pl.ds(lax.rem(rank + shift, devices) * size, size)] = chunk[...]
    own = record.shape[0]
    w_low, w_high = window[:ROWS][None], window[ROWS:][None]
    fwd_cos, fwd_sin = fwd[0][None], fwd[1][None]
    parts = GROUP + 1

    def group(start, power, last):
        here = record[pl.ds(start, GROUP)]
        if last:
            after = jnp.concatenate([record[pl.ds(start + 1, GROUP - 1)], record[pl.ds(0, 1)]], axis=0)
        else:
            after = record[pl.ds(start + 1, GROUP)]
        both = jnp.concatenate([here * w_low, after * w_high], axis=1)
        high, low = split(both.reshape(GROUP * FINE, LANES))
        step = dot(first_high[...], high) + dot(first_high[...], low) + dot(first_low[...], high)
        re = step[:parts * FINE].reshape(parts, FINE, LANES)
        im = step[parts * FINE:].reshape(parts, FINE, LANES)
        turned = jnp.concatenate([re * fwd_cos + im * fwd_sin, im * fwd_cos - re * fwd_sin], axis=2)
        high, low = split(turned.reshape(parts * FINE, 2 * LANES))
        wide = dot(high, second_both[...])
        value = wide[:, :LANES] + wide[:, LANES:] + dot(low, second_both[:, :LANES])
        value = jnp.concatenate([value, jnp.zeros((3 * FINE, LANES), jnp.float32)], axis=0)
        flipped = [value[i * LANES:(i + 1) * LANES].T for i in range(3)]
        pairs = [
            (natural(flipped[s // 4], 0, s % 4), natural(flipped[s // 4], LANES // 2, s % 4)) for s in range(parts)
        ]
        if last:
            sent[1], sent[2] = pairs[GROUP - 1]
            sent[3], sent[4] = pairs[GROUP]
        else:
            pairs[GROUP - 1] = tuple(a + b for a, b in zip(pairs[GROUP - 1], pairs[GROUP]))
        for s in range(GROUP):
            spec[0, pl.ds(start + s, 1)] = pairs[s][0][None]
            spec[1, pl.ds(start + s, 1)] = pairs[s][1][None]
            if s < GROUP - 1 or not last:
                power = power + pairs[s][0] * pairs[s][0] + pairs[s][1] * pairs[s][1]
        return power

    power = jnp.zeros((ROWS, LANES), jnp.float32)
    power = repeat(own // GROUP - 1, lambda i, p: group(i * GROUP, p, False), power)
    sent[0] = group(own - GROUP, power, True)


def bank_kernel(devices, *refs):
    blocks = refs[:devices]
    cutoff, order, bank, gathered = refs[devices:]
    rank = lax.axis_index("tm")
    width = blocks[0].shape[2]
    for shift, block in enumerate(blocks):
        first = lax.rem(rank + shift, devices) * (width // LANES)
        for at in range(width // LANES):
            lanes = slice(at * LANES, (at + 1) * LANES)
            gathered[first + at] = jnp.concatenate([block[0, :, lanes], block[1, :, lanes]], axis=1)
    count = blocks[0].shape[1]
    lane = lax.broadcasted_iota(jnp.int32, (ROWS, LANES), 1)
    row = lax.broadcasted_iota(jnp.int32, (ROWS, LANES), 0)
    bins = row * LANES + lane
    value = dot(order[...], gathered[...].reshape(ROWS * count, 2 * LANES))
    for m in range(count):
        keep = bins < cutoff[m]
        rows = slice(m * ROWS, (m + 1) * ROWS)
        bank[0, m] = jnp.where(keep, value[rows, :LANES], 0.0)
        bank[1, m] = jnp.where(keep, value[rows, LANES:], 0.0)


def filter_kernel(devices, segs, energy, *refs):
    shares = refs[:devices]
    spec, bank, third, inv, fourth, out = refs[devices:]
    own, count = out.shape
    power = shares[0][0]
    for share in shares[1:]:
        power = power + share[0]
    for i in range(devices):
        after = shares[(i + 1) % devices]
        re, im = shares[i][1] + after[3], shares[i][2] + after[4]
        power = power + re * re + im * im
        if i == 0:
            last_re, last_im = re, im
    density = power / (segs * energy) + FLOOR
    inverse_density = 1.0 / density
    inv_cos, inv_sin = inv[0][None], inv[1][None]
    column = lax.broadcasted_iota(jnp.int32, (GROUP, LANES), 1)

    def whiten(value):
        return (value / density[None]).astype(jnp.bfloat16).astype(jnp.float32)

    def block(start, last):
        x_re, x_im = spec[0, pl.ds(start, GROUP)], spec[1, pl.ds(start, GROUP)]
        if last:
            x_re = jnp.concatenate([x_re[:GROUP - 1], last_re[None]], axis=0)
            x_im = jnp.concatenate([x_im[:GROUP - 1], last_im[None]], axis=0)
        white_re, white_im = whiten(x_re), whiten(x_im)

        def pair_of(step, result):
            sides, norms = [], []
            for side in range(2):
                m = 2 * step + side
                h_re, h_im = bank[0, m], bank[1, m]
                norms.append(jnp.sum((h_re * h_re + h_im * h_im) * inverse_density, keepdims=True))
                c_re = h_re[None] * white_re + h_im[None] * white_im
                c_im = h_re[None] * white_im - h_im[None] * white_re
                both = jnp.concatenate([c_re, c_im], axis=0).reshape(2 * GROUP * ROWS, LANES)
                sides.append(both.astype(jnp.bfloat16))
            section = dot(third[...], jnp.concatenate(sides, axis=1))
            half = GROUP * FINE
            for side in range(2):
                re = section[:half, side * LANES:(side + 1) * LANES].reshape(GROUP, FINE, LANES)
                im = section[half:, side * LANES:(side + 1) * LANES].reshape(GROUP, FINE, LANES)
                turned = jnp.concatenate([re * inv_cos - im * inv_sin, re * inv_sin + im * inv_cos], axis=2)
                wave = dot(turned.reshape(half, 2 * LANES).astype(jnp.bfloat16), fourth[...])
                square = wave[:, :LANES] * wave[:, :LANES] + wave[:, LANES:] * wave[:, LANES:]
                top = jnp.max(jnp.max(square.reshape(GROUP, FINE, LANES), axis=1), axis=1, keepdims=True)
                value = jnp.sqrt(top) / (jnp.sqrt(norms[side]) * math.sqrt(energy))
                result = jnp.where(column == 2 * step + side, value, result)
            return result

        result = repeat(count // 2, pair_of, jnp.zeros((GROUP, LANES), jnp.float32))
        out[pl.ds(start, GROUP)] = result[:, :count]

    def earlier(number, carry):
        block(pl.multiple_of(number * GROUP, GROUP), False)
        return carry

    repeat(own // GROUP - 1, earlier, 0)
    block(own - GROUP, True)


def around(array, axis):
    devices = lax.axis_size(axis)
    return [array] + [
        lax.ppermute(array, axis, [((i + shift) % devices, i) for i in range(devices)]) for shift in range(1, devices)
    ]


def on_device(strain, templates, cutoff):
    tm, tmpl = lax.axis_size("tm"), lax.axis_size("tmpl")
    size = strain.shape[0] // HOP
    own = size * tmpl
    count = templates.shape[1]
    held, energy = tables()
    held = {name: jnp.asarray(table) for name, table in held.items()}
    smem = pl.BlockSpec(memory_space=pltpu.SMEM)
    vmem = pl.BlockSpec(memory_space=pltpu.VMEM)
    params = pltpu.CompilerParams(vmem_limit_bytes=48 * 1024 * 1024)
    f32 = jnp.float32
    chunks = around(strain.reshape(size, ROWS, LANES), "tmpl")
    blocks = around(templates, "tm")
    spec, sent = pl.pallas_call(
        functools.partial(forward_kernel, tmpl),
        out_shape=(
            jax.ShapeDtypeStruct((2, own, ROWS, LANES), f32),
            jax.ShapeDtypeStruct((5, ROWS, LANES), f32),
        ),
        in_specs=[vmem] * (tmpl + 5),
        out_specs=(vmem, vmem),
        scratch_shapes=[pltpu.VMEM((own, ROWS, LANES), f32)],
        compiler_params=params,
        name="forward",
    )(*chunks, held["window"], held["first_high"], held["first_low"], held["fwd"], held["second_both"])
    shares = around(sent, "tm")
    bank = pl.pallas_call(
        functools.partial(bank_kernel, tm),
        out_shape=jax.ShapeDtypeStruct((2, count, ROWS, LANES), f32),
        in_specs=[vmem] * tm + [smem, vmem],
        out_specs=vmem,
        scratch_shapes=[pltpu.VMEM((ROWS, count, 2 * LANES), jnp.bfloat16)],
        compiler_params=params,
        name="bank",
    )(*blocks, cutoff, held["order"])
    return pl.pallas_call(
        functools.partial(filter_kernel, tm, own * tm, energy),
        out_shape=jax.ShapeDtypeStruct((own, count), f32),
        in_specs=[vmem] * (tm + 5),
        out_specs=vmem,
        compiler_params=params,
        name="matched_filter",
    )(*shares, spec, bank, held["third"], held["inv"], held["fourth"])


def solution(mesh):
    in_specs = (P(("tm", "tmpl")), P(None, "tmpl", "tm"), P("tmpl"))
    out_specs = P("tm", "tmpl")
    return jax.shard_map(
        on_device, mesh=mesh, in_specs=in_specs, out_specs=out_specs, check_vma=False
    )
```

```python
import functools
import math

import jax
import jax.numpy as jnp
import ml_dtypes
import numpy as np
from jax import lax
from jax.experimental import pallas as pl
from jax.experimental.pallas import tpu as pltpu
from jax.sharding import PartitionSpec as P

NFFT = 4096
BINS = 2048
HOP = 2048
LANES = 128
ROWS = HOP // LANES
FINE = 32
GROUP = 8
FLOOR = 1e-6

ROOT_SCALE = {128: 1.66575, 64: 1.66575, 32: 1.6245, 16: 1.6245, 8: 1.6245}


def root_order(index, period):
    return period // math.gcd(int(index), period)


def row_scale(count, period):
    return np.array([ROOT_SCALE.get(root_order(i, period), 1.0) for i in range(count)])


def as_bf16(table):
    return np.asarray(table, np.float32).astype(ml_dtypes.bfloat16)


def two_parts(table):
    high = as_bf16(table)
    low = as_bf16(np.asarray(table, np.float64) - high.astype(np.float64))
    return high, low


def turn(left, right, period):
    angle = 2.0 * np.pi * (np.outer(left, right) % period) / period
    return np.cos(angle), np.sin(angle)


@functools.lru_cache(maxsize=None)
def tables():
    eye = np.eye(GROUP)
    fine, wide, rows = np.arange(FINE), np.arange(LANES), np.arange(ROWS)
    window = 0.5 - 0.5 * np.cos(2.0 * np.pi * np.arange(NFFT) / NFFT)
    cos, sin = turn(fine, fine, FINE)
    halves = np.zeros((GROUP + 1, GROUP, FINE))
    for s in range(GROUP):
        halves[s, s] = 1.0
    halves[GROUP - 1, GROUP - 1, ROWS:] = 0.0
    halves[GROUP, GROUP - 1, ROWS:] = 1.0
    spread = lambda t: (halves[:, None] * t[None, :, None, :]).reshape((GROUP + 1) * FINE, GROUP * FINE)
    first = np.concatenate([spread(cos), spread(-sin)], axis=0)
    first_high, first_low = two_parts(first)
    fwd_cos, fwd_sin = turn(fine, wide, NFFT)
    f_order = np.array([4 * d + g for g in range(4) for d in range(ROWS)])
    cos, sin = turn(wide, f_order, LANES)
    second = np.block([[cos, -sin], [sin, cos]])
    second_high, second_low = two_parts(second)
    scale_q = row_scale(FINE, FINE)
    scale_c = row_scale(LANES, LANES)
    cos, sin = turn(fine, rows, FINE)
    cos, sin = cos * scale_q[:, None], sin * scale_q[:, None]
    third = np.block([[np.kron(eye, cos), np.kron(eye, -sin)], [np.kron(eye, sin), np.kron(eye, cos)]])
    inv_cos, inv_sin = turn(fine, wide, NFFT)
    undo = 1.0 / (scale_q[:, None] * scale_c[None, :])
    cos, sin = turn(wide, wide, LANES)
    cos, sin = cos * scale_c[:, None], sin * scale_c[:, None]
    fourth = np.block([[cos, sin], [-sin, cos]])
    order = np.zeros((ROWS * 16, ROWS * 16))
    for m in range(16):
        for d in range(ROWS):
            order[m * ROWS + d, d * 16 + m] = 1.0
    f32 = lambda t: np.asarray(t, np.float32)
    return dict(
        window=f32(window.reshape(2 * ROWS, LANES)),
        first_high=first_high,
        first_low=first_low,
        fwd=f32(np.stack([fwd_cos, fwd_sin])),
        second_both=np.concatenate([second_high, second_low], axis=1),
        third=as_bf16(third),
        inv=f32(np.stack([inv_cos * undo, inv_sin * undo])),
        fourth=as_bf16(fourth),
        order=as_bf16(order),
    ), float((window * window).sum())


def dot(left, right):
    return jnp.dot(left, right, preferred_element_type=jnp.float32)


def split(value):
    high = value.astype(jnp.bfloat16)
    return high, (value - high.astype(jnp.float32)).astype(jnp.bfloat16)


def repeat(count, body, carry):
    if count <= 8:
        for step in range(count):
            carry = body(step, carry)
        return carry
    return lax.fori_loop(0, count, body, carry)


def natural(flipped, at, source):
    part = lax.broadcasted_iota(jnp.int32, (ROWS, LANES), 1) // FINE
    result = None
    for g in range(4):
        piece = flipped[at + g * ROWS:at + (g + 1) * ROWS]
        if g != source:
            piece = pltpu.roll(piece, ((g - source) % 4) * FINE, 1)
        result = piece if g == 0 else jnp.where(part == g, piece, result)
    return result


def forward_kernel(size, chunks, window, first_high, first_low, fwd, second_both, spec, sent, record):
    rank = lax.axis_index("tmpl")
    for other in range(chunks.shape[0] // size):
        record[pl.ds((rank ^ other) * size, size)] = chunks[other * size:(other + 1) * size]
    own = record.shape[0]
    w_low, w_high = window[:ROWS][None], window[ROWS:][None]
    fwd_cos, fwd_sin = fwd[0][None], fwd[1][None]
    parts = GROUP + 1

    def group(start, power, last):
        here = record[pl.ds(start, GROUP)]
        if last:
            after = jnp.concatenate([record[pl.ds(start + 1, GROUP - 1)], record[pl.ds(0, 1)]], axis=0)
        else:
            after = record[pl.ds(start + 1, GROUP)]
        both = jnp.concatenate([here * w_low, after * w_high], axis=1)
        high, low = split(both.reshape(GROUP * FINE, LANES))
        step = dot(first_high[...], high) + dot(first_high[...], low) + dot(first_low[...], high)
        re = step[:parts * FINE].reshape(parts, FINE, LANES)
        im = step[parts * FINE:].reshape(parts, FINE, LANES)
        turned = jnp.concatenate([re * fwd_cos + im * fwd_sin, im * fwd_cos - re * fwd_sin], axis=2)
        high, low = split(turned.reshape(parts * FINE, 2 * LANES))
        wide = dot(high, second_both[...])
        value = wide[:, :LANES] + wide[:, LANES:] + dot(low, second_both[:, :LANES])
        value = jnp.concatenate([value, jnp.zeros((3 * FINE, LANES), jnp.float32)], axis=0)
        flipped = [value[i * LANES:(i + 1) * LANES].T for i in range(3)]
        pairs = [
            (natural(flipped[s // 4], 0, s % 4), natural(flipped[s // 4], LANES // 2, s % 4)) for s in range(parts)
        ]
        if last:
            sent[1], sent[2] = pairs[GROUP - 1]
            sent[3], sent[4] = pairs[GROUP]
        else:
            pairs[GROUP - 1] = tuple(a + b for a, b in zip(pairs[GROUP - 1], pairs[GROUP]))
        for s in range(GROUP):
            spec[0, pl.ds(start + s, 1)] = pairs[s][0][None]
            spec[1, pl.ds(start + s, 1)] = pairs[s][1][None]
            if s < GROUP - 1 or not last:
                power = power + pairs[s][0] * pairs[s][0] + pairs[s][1] * pairs[s][1]
        return power

    power = jnp.zeros((ROWS, LANES), jnp.float32)
    power = repeat(own // GROUP - 1, lambda i, p: group(i * GROUP, p, False), power)
    sent[0] = group(own - GROUP, power, True)


def bank_kernel(devices, *refs):
    blocks = refs[:devices]
    cutoff, order, bank, gathered = refs[devices:]
    rank = lax.axis_index("tm")
    width = blocks[0].shape[2]
    for other, block in enumerate(blocks):
        first = (rank ^ other) * (width // LANES)
        for at in range(width // LANES):
            lanes = slice(at * LANES, (at + 1) * LANES)
            gathered[first + at] = jnp.concatenate([block[0, :, lanes], block[1, :, lanes]], axis=1)
    count = blocks[0].shape[1]
    lane = lax.broadcasted_iota(jnp.int32, (ROWS, LANES), 1)
    row = lax.broadcasted_iota(jnp.int32, (ROWS, LANES), 0)
    bins = row * LANES + lane
    value = dot(order[...], gathered[...].reshape(ROWS * count, 2 * LANES))
    for m in range(count):
        keep = bins < cutoff[m]
        rows = slice(m * ROWS, (m + 1) * ROWS)
        bank[0, m] = jnp.where(keep, value[rows, :LANES], 0.0)
        bank[1, m] = jnp.where(keep, value[rows, LANES:], 0.0)


def filter_kernel(devices, segs, energy, *refs):
    shares = refs[:devices]
    spec, bank, third, inv, fourth, out, held = refs[devices:]
    own, count = out.shape
    rank = lax.axis_index("tm")
    power = shares[0][0]
    for share in shares[1:]:
        power = power + share[0]
    for other, share in enumerate(shares):
        held[rank ^ other] = share[3:5]
    for other, share in enumerate(shares):
        after = held[lax.rem((rank ^ other) + 1, devices)]
        re, im = share[1] + after[0], share[2] + after[1]
        power = power + re * re + im * im
        if other == 0:
            last_re, last_im = re, im
    density = power / (segs * energy) + FLOOR
    inverse_density = 1.0 / density
    inv_cos, inv_sin = inv[0][None], inv[1][None]
    column = lax.broadcasted_iota(jnp.int32, (GROUP, LANES), 1)

    def whiten(value):
        return (value / density[None]).astype(jnp.bfloat16).astype(jnp.float32)

    def block(start, last):
        x_re, x_im = spec[0, pl.ds(start, GROUP)], spec[1, pl.ds(start, GROUP)]
        if last:
            x_re = jnp.concatenate([x_re[:GROUP - 1], last_re[None]], axis=0)
            x_im = jnp.concatenate([x_im[:GROUP - 1], last_im[None]], axis=0)
        white_re, white_im = whiten(x_re), whiten(x_im)

        def pair_of(step, result):
            sides, norms = [], []
            for side in range(2):
                m = 2 * step + side
                h_re, h_im = bank[0, m], bank[1, m]
                norms.append(jnp.sum((h_re * h_re + h_im * h_im) * inverse_density, keepdims=True))
                c_re = h_re[None] * white_re + h_im[None] * white_im
                c_im = h_re[None] * white_im - h_im[None] * white_re
                both = jnp.concatenate([c_re, c_im], axis=0).reshape(2 * GROUP * ROWS, LANES)
                sides.append(both.astype(jnp.bfloat16))
            section = dot(third[...], jnp.concatenate(sides, axis=1))
            half = GROUP * FINE
            for side in range(2):
                re = section[:half, side * LANES:(side + 1) * LANES].reshape(GROUP, FINE, LANES)
                im = section[half:, side * LANES:(side + 1) * LANES].reshape(GROUP, FINE, LANES)
                turned = jnp.concatenate([re * inv_cos - im * inv_sin, re * inv_sin + im * inv_cos], axis=2)
                wave = dot(turned.reshape(half, 2 * LANES).astype(jnp.bfloat16), fourth[...])
                square = wave[:, :LANES] * wave[:, :LANES] + wave[:, LANES:] * wave[:, LANES:]
                top = jnp.max(jnp.max(square.reshape(GROUP, FINE, LANES), axis=1), axis=1, keepdims=True)
                value = jnp.sqrt(top) / (jnp.sqrt(norms[side]) * math.sqrt(energy))
                result = jnp.where(column == 2 * step + side, value, result)
            return result

        result = repeat(count // 2, pair_of, jnp.zeros((GROUP, LANES), jnp.float32))
        out[pl.ds(start, GROUP)] = result[:, :count]

    def earlier(number, carry):
        block(pl.multiple_of(number * GROUP, GROUP), False)
        return carry

    repeat(own // GROUP - 1, earlier, 0)
    block(own - GROUP, True)


def swap(array, axis, bits):
    return lax.ppermute(array, axis, [(i, i ^ bits) for i in range(lax.axis_size(axis))])


def load_kernel(count, *refs):
    sources, targets, sems = refs[1:1 + count], refs[1 + count:1 + 2 * count], refs[-1]
    copies = [pltpu.make_async_copy(s, t, sems.at[i]) for i, (s, t) in enumerate(zip(sources, targets))]
    for copy in copies:
        copy.start()
    for copy in copies:
        copy.wait()


def on_device(strain, templates, cutoff):
    tm, tmpl = lax.axis_size("tm"), lax.axis_size("tmpl")
    size = strain.shape[0] // HOP
    own = size * tmpl
    count = templates.shape[1]
    smem = pl.BlockSpec(memory_space=pltpu.SMEM)
    vmem = pl.BlockSpec(memory_space=pltpu.VMEM)
    anywhere = pl.BlockSpec(memory_space=pltpu.HBM)
    params = pltpu.CompilerParams(vmem_limit_bytes=48 * 1024 * 1024)
    f32 = jnp.float32

    chunks = strain.reshape(size, ROWS, LANES)
    after = chunks
    bits = 1
    while bits < tmpl:
        arrived = swap(chunks, "tmpl", bits)
        if 2 * bits < tmpl:
            after = arrived
        chunks = jnp.concatenate([chunks, arrived], axis=0)
        bits *= 2
    blocks = [templates] + [swap(templates, "tm", other) for other in range(1, tm)]

    held, energy = tables()
    names = list(held)
    loaded = pl.pallas_call(
        functools.partial(load_kernel, len(names)),
        out_shape=[jax.ShapeDtypeStruct(held[n].shape, held[n].dtype) for n in names],
        in_specs=[pl.BlockSpec(memory_space=pl.ANY)] + [anywhere] * len(names),
        out_specs=[vmem] * len(names),
        scratch_shapes=[pltpu.SemaphoreType.DMA((len(names),))],
        compiler_params=params,
        cost_estimate=pl.CostEstimate(flops=0, bytes_accessed=3000000, transcendentals=0),
        name="load",
    )(after, *[jnp.asarray(held[n]) for n in names])
    held = dict(zip(names, loaded))

    spec, sent = pl.pallas_call(
        functools.partial(forward_kernel, size),
        out_shape=(
            jax.ShapeDtypeStruct((2, own, ROWS, LANES), f32),
            jax.ShapeDtypeStruct((5, ROWS, LANES), f32),
        ),
        in_specs=[vmem] * 6,
        out_specs=(vmem, vmem),
        scratch_shapes=[pltpu.VMEM((own, ROWS, LANES), f32)],
        compiler_params=params,
        name="forward",
    )(chunks, held["window"], held["first_high"], held["first_low"], held["fwd"], held["second_both"])
    shares = [sent] + [swap(sent, "tm", other) for other in range(1, tm)]
    bank = pl.pallas_call(
        functools.partial(bank_kernel, tm),
        out_shape=jax.ShapeDtypeStruct((2, count, ROWS, LANES), f32),
        in_specs=[vmem] * tm + [smem, vmem],
        out_specs=vmem,
        scratch_shapes=[pltpu.VMEM((ROWS, count, 2 * LANES), jnp.bfloat16)],
        compiler_params=params,
        cost_estimate=pl.CostEstimate(flops=0, bytes_accessed=2500000, transcendentals=0),
        name="bank",
    )(*blocks, cutoff, held["order"])
    return pl.pallas_call(
        functools.partial(filter_kernel, tm, own * tm, energy),
        out_shape=jax.ShapeDtypeStruct((own, count), f32),
        in_specs=[vmem] * (tm + 5),
        out_specs=vmem,
        scratch_shapes=[pltpu.VMEM((tm, 2, ROWS, LANES), f32)],
        compiler_params=params,
        name="matched_filter",
    )(*shares, spec, bank, held["third"], held["inv"], held["fourth"])


def solution(mesh):
    in_specs = (P(("tm", "tmpl")), P(None, "tmpl", "tm"), P("tmpl"))
    out_specs = P("tm", "tmpl")
    return jax.shard_map(
        on_device, mesh=mesh, in_specs=in_specs, out_specs=out_specs, check_vma=False
    )
```

```python
import functools
import math

import jax
import jax.numpy as jnp
import ml_dtypes
import numpy as np
from jax import lax
from jax.experimental import pallas as pl
from jax.experimental.pallas import tpu as pltpu
from jax.sharding import PartitionSpec as P

NFFT = 4096
BINS = 2048
HOP = 2048
LANES = 128
ROWS = HOP // LANES
FINE = 32
GROUP = 8
FLOOR = 1e-6

ROOT_SCALE = {128: 1.66575, 64: 1.66575, 32: 1.6245, 16: 1.6245, 8: 1.6245}


def root_order(index, period):
    return period // math.gcd(int(index), period)


def row_scale(count, period):
    return np.array([ROOT_SCALE.get(root_order(i, period), 1.0) for i in range(count)])


def as_bf16(table):
    return np.asarray(table, np.float32).astype(ml_dtypes.bfloat16)


def two_parts(table):
    high = as_bf16(table)
    low = as_bf16(np.asarray(table, np.float64) - high.astype(np.float64))
    return high, low


def turn(left, right, period):
    angle = 2.0 * np.pi * (np.outer(left, right) % period) / period
    return np.cos(angle), np.sin(angle)


@functools.lru_cache(maxsize=None)
def tables():
    fine, wide, rows = np.arange(FINE), np.arange(LANES), np.arange(ROWS)
    window = 0.5 - 0.5 * np.cos(2.0 * np.pi * np.arange(NFFT) / NFFT)
    cos, sin = turn(fine, fine, FINE)
    first_high, first_low = two_parts(np.tile(np.concatenate([cos, -sin]), (1, GROUP)))
    fwd_cos, fwd_sin = turn(fine, wide, NFFT)
    f_order = np.array([4 * d + g for g in range(4) for d in range(ROWS)])
    cos, sin = turn(wide, f_order, LANES)
    second_high, second_low = two_parts(np.block([[cos, -sin], [sin, cos]]))
    scale_q, scale_c = row_scale(FINE, FINE), row_scale(LANES, LANES)
    cos, sin = turn(fine, rows, FINE)
    cos, sin = np.tile(cos * scale_q[:, None], (1, GROUP)), np.tile(sin * scale_q[:, None], (1, GROUP))
    third = np.block([[cos, -sin], [sin, cos]])
    inv_cos, inv_sin = turn(fine, wide, NFFT)
    undo = 1.0 / (scale_q[:, None] * scale_c[None, :])
    cos, sin = turn(wide, wide, LANES)
    cos, sin = cos * scale_c[:, None], sin * scale_c[:, None]
    fourth = np.block([[cos, sin], [-sin, cos]])
    narrow = np.concatenate(
        [first_high, first_low, as_bf16(third), np.concatenate([second_high, second_low], axis=1), as_bf16(fourth)]
    )
    broad = np.concatenate([window.reshape(FINE, LANES), fwd_cos, fwd_sin, inv_cos * undo, inv_sin * undo])
    return narrow, np.asarray(broad, np.float32), float((window * window).sum())


def dot(left, right):
    return jnp.dot(left, right, preferred_element_type=jnp.float32)


def split(value):
    high = value.astype(jnp.bfloat16)
    return high, (value - high.astype(jnp.float32)).astype(jnp.bfloat16)


def repeat(count, body, carry):
    if count <= 8:
        for step in range(count):
            carry = body(step, carry)
        return carry
    return lax.fori_loop(0, count, body, carry)


def block_diagonal(rows, width):
    lane = lax.broadcasted_iota(jnp.int32, rows.shape, 1)
    owner = lax.rem(lane // width, GROUP)
    return jnp.concatenate(
        [jnp.where(owner == s, rows, jnp.zeros_like(rows)) for s in range(GROUP)], axis=0
    )


def natural(flipped, at, source):
    part = lax.broadcasted_iota(jnp.int32, (ROWS, LANES), 1) // FINE
    result = None
    for g in range(4):
        piece = flipped[at + g * ROWS:at + (g + 1) * ROWS]
        if source is not None and g != source:
            piece = pltpu.roll(piece, ((g - source) % 4) * FINE, 1)
        result = piece if g == 0 else jnp.where(part == g, piece, result)
    return result


def pack_kernel(strain, templates, copies, held):
    held[...] = templates[...]
    copies[...] = jnp.broadcast_to(strain[...][None], copies.shape)


def bank_kernel(devices, *refs):
    blocks = refs[:devices]
    cutoff, bank, gathered = refs[devices:]
    rank = lax.axis_index("tm")
    width = blocks[0].shape[2]
    for other, block in enumerate(blocks):
        first = (rank ^ other) * (width // LANES)
        for at in range(width // LANES):
            lanes = slice(at * LANES, (at + 1) * LANES)
            gathered[first + at] = jnp.concatenate([block[0, :, lanes], block[1, :, lanes]], axis=1)
    count = blocks[0].shape[1]
    lane = lax.broadcasted_iota(jnp.int32, (ROWS, LANES), 1)
    row = lax.broadcasted_iota(jnp.int32, (ROWS, LANES), 0)
    bins = row * LANES + lane
    shape = (count * ROWS, count * ROWS)
    to, source = lax.broadcasted_iota(jnp.int32, shape, 0), lax.broadcasted_iota(jnp.int32, shape, 1)
    order = (source == (to % ROWS) * count + to // ROWS).astype(jnp.float32).astype(jnp.bfloat16)
    value = dot(order, gathered[...].reshape(ROWS * count, 2 * LANES))
    for m in range(count):
        keep = bins < cutoff[m]
        rows = slice(m * ROWS, (m + 1) * ROWS)
        bank[0, m] = jnp.where(keep, value[rows, :LANES], 0.0)
        bank[1, m] = jnp.where(keep, value[rows, LANES:], 0.0)


def filter_kernel(energy, record, bank, narrow, broad, out, spec):
    segs = record.shape[0]
    own, count = out.shape
    half = GROUP * FINE
    w_low, w_high = broad[:ROWS][None], broad[ROWS:FINE][None]
    fwd_cos, fwd_sin = broad[FINE:2 * FINE][None], broad[2 * FINE:3 * FINE][None]
    inv_cos, inv_sin = broad[3 * FINE:4 * FINE][None], broad[4 * FINE:5 * FINE][None]
    high, low = narrow[:2 * FINE], narrow[2 * FINE:4 * FINE]
    spread = lambda part: jnp.concatenate(
        [block_diagonal(part[:FINE], part.shape[1] // GROUP), block_diagonal(part[FINE:], part.shape[1] // GROUP)]
    )
    first_high, first_low = spread(high), spread(low)
    third_rows = narrow[4 * FINE:6 * FINE]
    third = jnp.concatenate([block_diagonal(third_rows[:FINE], ROWS), block_diagonal(third_rows[FINE:], ROWS)])
    second = slice(6 * FINE, 6 * FINE + 2 * LANES)
    fourth = slice(6 * FINE + 2 * LANES, 6 * FINE + 4 * LANES)

    def frames(start, last):
        here = record[pl.ds(start, GROUP)]
        if last:
            after = jnp.concatenate([record[pl.ds(start + 1, GROUP - 1)], record[pl.ds(0, 1)]], axis=0)
        else:
            after = record[pl.ds(start + 1, GROUP)]
        both = jnp.concatenate([here * w_low, after * w_high], axis=1)
        return both.reshape(half, LANES)

    def forward(start, power, last):
        pair = jnp.concatenate([frames(start, False), frames(start + GROUP, last)], axis=1)
        high, low = split(pair)
        step = dot(first_high, high) + dot(first_high, low) + dot(first_low, high)
        for h in range(2):
            re = step[:half, h * LANES:(h + 1) * LANES].reshape(GROUP, FINE, LANES)
            im = step[half:, h * LANES:(h + 1) * LANES].reshape(GROUP, FINE, LANES)
            turned = jnp.concatenate([re * fwd_cos + im * fwd_sin, im * fwd_cos - re * fwd_sin], axis=2)
            high, low = split(turned.reshape(half, 2 * LANES))
            wide = dot(high, narrow[second])
            value = wide[:, :LANES] + wide[:, LANES:] + dot(low, narrow[second, :LANES])
            spec[pl.ds((start + h * GROUP) * FINE, half)] = value
            power = power + jnp.sum((value * value).reshape(GROUP, FINE, LANES), axis=0)
        return power

    power = jnp.zeros((FINE, LANES), jnp.float32)
    pairs = segs // (2 * GROUP)
    power = repeat(pairs - 1, lambda i, p: forward(i * 2 * GROUP, p, False), power)
    power = forward((pairs - 1) * 2 * GROUP, power, True)
    power = power + pltpu.roll(power, LANES // 2, 1)
    density = power / (segs * energy) + FLOOR
    inverse_density = natural((1.0 / jnp.concatenate([density] * 4, axis=0)).T, 0, None)

    place = lax.axis_index("tm") * own
    column = lax.broadcasted_iota(jnp.int32, (GROUP, LANES), 1)

    def block(number, carry):
        at = pl.multiple_of((place + number * GROUP) * FINE, half)
        white = spec[pl.ds(at, half)].reshape(GROUP, FINE, LANES) / density[None]
        white = white.astype(jnp.bfloat16).astype(jnp.float32).reshape(2, 4 * FINE, LANES)
        re_parts, im_parts = [], []
        for side in range(2):
            flipped = white[side].T
            for s in range(4):
                re_parts.append(natural(flipped, 0, s))
                im_parts.append(natural(flipped, LANES // 2, s))
        white_re, white_im = jnp.stack(re_parts), jnp.stack(im_parts)

        def pair_of(step, result):
            sides, norms = [], []
            for side in range(2):
                m = 2 * step + side
                h_re, h_im = bank[0, m], bank[1, m]
                norms.append(jnp.sum((h_re * h_re + h_im * h_im) * inverse_density, keepdims=True))
                c_re = h_re[None] * white_re + h_im[None] * white_im
                c_im = h_re[None] * white_im - h_im[None] * white_re
                both = jnp.concatenate([c_re, c_im], axis=0).reshape(2 * GROUP * ROWS, LANES)
                sides.append(both.astype(jnp.bfloat16))
            section = dot(third, jnp.concatenate(sides, axis=1))
            for side in range(2):
                re = section[:half, side * LANES:(side + 1) * LANES].reshape(GROUP, FINE, LANES)
                im = section[half:, side * LANES:(side + 1) * LANES].reshape(GROUP, FINE, LANES)
                turned = jnp.concatenate([re * inv_cos - im * inv_sin, re * inv_sin + im * inv_cos], axis=2)
                wave = dot(turned.reshape(half, 2 * LANES).astype(jnp.bfloat16), narrow[fourth])
                square = wave[:, :LANES] * wave[:, :LANES] + wave[:, LANES:] * wave[:, LANES:]
                top = jnp.max(jnp.max(square.reshape(GROUP, FINE, LANES), axis=1), axis=1, keepdims=True)
                value = jnp.sqrt(top) / (jnp.sqrt(norms[side]) * math.sqrt(energy))
                result = jnp.where(column == 2 * step + side, value, result)
            return result

        result = repeat(count // 2, pair_of, jnp.zeros((GROUP, LANES), jnp.float32))
        out[pl.ds(number * GROUP, GROUP)] = result[:, :count]
        return carry

    repeat(own // GROUP, block, 0)


def swap(array, axis, bits):
    return lax.ppermute(array, axis, [(i, i ^ bits) for i in range(lax.axis_size(axis))])


def on_device(strain, templates, cutoff):
    tm, devices = lax.axis_size("tm"), lax.axis_size("tm") * lax.axis_size("tmpl")
    size = strain.shape[0] // HOP
    segs = devices * size
    own = segs // tm
    count = templates.shape[1]
    smem = pl.BlockSpec(memory_space=pltpu.SMEM)
    vmem = pl.BlockSpec(memory_space=pltpu.VMEM)
    params = pltpu.CompilerParams(vmem_limit_bytes=40 * 1024 * 1024)
    f32 = jnp.float32

    copies, held = pl.pallas_call(
        pack_kernel,
        out_shape=(
            jax.ShapeDtypeStruct((devices, size * ROWS, LANES), f32),
            jax.ShapeDtypeStruct(templates.shape, templates.dtype),
        ),
        in_specs=[vmem, vmem],
        out_specs=(vmem, vmem),
        compiler_params=params,
        name="pack",
    )(strain.reshape(size * ROWS, LANES), templates)
    record = lax.all_to_all(copies, ("tm", "tmpl"), split_axis=0, concat_axis=0, tiled=True)
    record = record.reshape(segs, ROWS, LANES)
    blocks = [held] + [swap(held, "tm", other) for other in range(1, tm)]
    bank = pl.pallas_call(
        functools.partial(bank_kernel, tm),
        out_shape=jax.ShapeDtypeStruct((2, count, ROWS, LANES), f32),
        in_specs=[vmem] * tm + [smem],
        out_specs=vmem,
        scratch_shapes=[pltpu.VMEM((ROWS, count, 2 * LANES), jnp.bfloat16)],
        compiler_params=params,
        cost_estimate=pl.CostEstimate(flops=0, bytes_accessed=2500000, transcendentals=0),
        name="bank",
    )(*blocks, cutoff)
    narrow, broad, energy = tables()
    return pl.pallas_call(
        functools.partial(filter_kernel, energy),
        out_shape=jax.ShapeDtypeStruct((own, count), f32),
        in_specs=[vmem] * 4,
        out_specs=vmem,
        scratch_shapes=[pltpu.VMEM((segs * FINE, LANES), f32)],
        compiler_params=params,
        name="matched_filter",
    )(record, bank, jnp.asarray(narrow), jnp.asarray(broad))


def solution(mesh):
    in_specs = (P(("tm", "tmpl")), P(None, "tmpl", "tm"), P("tmpl"))
    out_specs = P("tm", "tmpl")
    return jax.shard_map(
        on_device, mesh=mesh, in_specs=in_specs, out_specs=out_specs, check_vma=False
    )
```

```python
import functools
import math

import jax
import jax.numpy as jnp
import ml_dtypes
import numpy as np
from jax import lax
from jax.experimental import pallas as pl
from jax.experimental.pallas import tpu as pltpu
from jax.sharding import Mesh, PartitionSpec as P

NFFT = 4096
BINS = 2048
HOP = 2048
LANES = 128
ROWS = HOP // LANES
FINE = 32
GROUP = 8
FLOOR = 1e-6

ROOT_SCALE = {128: 1.66575, 64: 1.66575, 32: 1.6245, 16: 1.6245, 8: 1.6245}


def root_order(index, period):
    return period // math.gcd(int(index), period)


def row_scale(count, period):
    return np.array([ROOT_SCALE.get(root_order(i, period), 1.0) for i in range(count)])


def as_bf16(table):
    return np.asarray(table, np.float32).astype(ml_dtypes.bfloat16)


def two_parts(table):
    high = as_bf16(table)
    low = as_bf16(np.asarray(table, np.float64) - high.astype(np.float64))
    return high, low


def turn(left, right, period):
    angle = 2.0 * np.pi * (np.outer(left, right) % period) / period
    return np.cos(angle), np.sin(angle)


@functools.lru_cache(maxsize=None)
def tables():
    fine, wide, rows = np.arange(FINE), np.arange(LANES), np.arange(ROWS)
    window = 0.5 - 0.5 * np.cos(2.0 * np.pi * np.arange(NFFT) / NFFT)
    cos, sin = turn(fine, fine, FINE)
    first_high, first_low = two_parts(np.tile(np.concatenate([cos, -sin]), (1, GROUP)))
    fwd_cos, fwd_sin = turn(fine, wide, NFFT)
    f_order = np.array([4 * d + g for g in range(4) for d in range(ROWS)])
    cos, sin = turn(wide, f_order, LANES)
    second_high, second_low = two_parts(np.block([[cos, -sin], [sin, cos]]))
    scale_q, scale_c = row_scale(FINE, FINE), row_scale(LANES, LANES)
    cos, sin = turn(fine, rows, FINE)
    cos, sin = np.tile(cos * scale_q[:, None], (1, GROUP)), np.tile(sin * scale_q[:, None], (1, GROUP))
    third = np.block([[cos, -sin], [sin, cos]])
    inv_cos, inv_sin = turn(fine, wide, NFFT)
    undo = 1.0 / (scale_q[:, None] * scale_c[None, :])
    cos, sin = turn(wide, wide, LANES)
    cos, sin = cos * scale_c[:, None], sin * scale_c[:, None]
    fourth = np.block([[cos, sin], [-sin, cos]])
    narrow = np.concatenate(
        [first_high, first_low, as_bf16(third), np.concatenate([second_high, second_low], axis=1), as_bf16(fourth)]
    )
    broad = np.concatenate([window.reshape(FINE, LANES), fwd_cos, fwd_sin, inv_cos * undo, inv_sin * undo])
    return narrow, np.asarray(broad, np.float32), float((window * window).sum())


def dot(left, right):
    return jnp.dot(left, right, preferred_element_type=jnp.float32)


def split(value):
    high = value.astype(jnp.bfloat16)
    return high, (value - high.astype(jnp.float32)).astype(jnp.bfloat16)


def repeat(count, body, carry):
    if count <= 8:
        for step in range(count):
            carry = body(step, carry)
        return carry
    return lax.fori_loop(0, count, body, carry)


def block_diagonal(rows, width):
    lane = lax.broadcasted_iota(jnp.int32, rows.shape, 1)
    owner = lax.rem(lane // width, GROUP)
    return jnp.concatenate(
        [jnp.where(owner == s, rows, jnp.zeros_like(rows)) for s in range(GROUP)], axis=0
    )


def natural(flipped, at, source):
    part = lax.broadcasted_iota(jnp.int32, (ROWS, LANES), 1) // FINE
    result = None
    for g in range(4):
        piece = flipped[at + g * ROWS:at + (g + 1) * ROWS]
        if source is not None and g != source:
            piece = pltpu.roll(piece, ((g - source) % 4) * FINE, 1)
        result = piece if g == 0 else jnp.where(part == g, piece, result)
    return result


def pack_kernel(strain, copies, sems):
    moves = [pltpu.make_async_copy(strain, copies.at[i], sems.at[i]) for i in range(copies.shape[0])]
    for move in moves:
        move.start()
    for move in moves:
        move.wait()


def bank_kernel(devices, *refs):
    blocks = refs[:devices]
    cutoff, bank, gathered = refs[devices:]
    rank = lax.axis_index("tm")
    width = blocks[0].shape[2]
    for other, block in enumerate(blocks):
        first = (rank ^ other) * (width // LANES)
        for at in range(width // LANES):
            lanes = slice(at * LANES, (at + 1) * LANES)
            gathered[first + at] = jnp.concatenate([block[0, :, lanes], block[1, :, lanes]], axis=1)
    count = blocks[0].shape[1]
    lane = lax.broadcasted_iota(jnp.int32, (ROWS, LANES), 1)
    row = lax.broadcasted_iota(jnp.int32, (ROWS, LANES), 0)
    bins = row * LANES + lane
    shape = (count * ROWS, count * ROWS)
    to, source = lax.broadcasted_iota(jnp.int32, shape, 0), lax.broadcasted_iota(jnp.int32, shape, 1)
    order = (source == (to % ROWS) * count + to // ROWS).astype(jnp.float32).astype(jnp.bfloat16)
    value = dot(order, gathered[...].reshape(ROWS * count, 2 * LANES))
    for m in range(count):
        keep = bins < cutoff[m]
        rows = slice(m * ROWS, (m + 1) * ROWS)
        bank[0, m] = jnp.where(keep, value[rows, :LANES], 0.0)
        bank[1, m] = jnp.where(keep, value[rows, LANES:], 0.0)


def filter_kernel(energy, mine, others, bank, narrow, broad, out, spec, pairs):
    core = lax.axis_index("core")
    size = mine.shape[1]
    segs = 2 * mine.shape[0] * (size // ROWS)
    pairs[:, core] = mine[...]
    pairs[:, 1 - core] = others[...]
    record = pairs.reshape(segs, ROWS, LANES)
    own, count = out.shape
    half = GROUP * FINE
    w_low, w_high = broad[:ROWS][None], broad[ROWS:FINE][None]
    fwd_cos, fwd_sin = broad[FINE:2 * FINE][None], broad[2 * FINE:3 * FINE][None]
    inv_cos, inv_sin = broad[3 * FINE:4 * FINE][None], broad[4 * FINE:5 * FINE][None]
    high, low = narrow[:2 * FINE], narrow[2 * FINE:4 * FINE]
    spread = lambda part: jnp.concatenate(
        [block_diagonal(part[:FINE], part.shape[1] // GROUP), block_diagonal(part[FINE:], part.shape[1] // GROUP)]
    )
    first_high, first_low = spread(high), spread(low)
    third_rows = narrow[4 * FINE:6 * FINE]
    third = jnp.concatenate([block_diagonal(third_rows[:FINE], ROWS), block_diagonal(third_rows[FINE:], ROWS)])
    second = slice(6 * FINE, 6 * FINE + 2 * LANES)
    fourth = slice(6 * FINE + 2 * LANES, 6 * FINE + 4 * LANES)

    def frames(start, last):
        here = record[pl.ds(start, GROUP)]
        if last:
            after = jnp.concatenate([record[pl.ds(start + 1, GROUP - 1)], record[pl.ds(0, 1)]], axis=0)
        else:
            after = record[pl.ds(start + 1, GROUP)]
        both = jnp.concatenate([here * w_low, after * w_high], axis=1)
        return both.reshape(half, LANES)

    def forward(start, power, last):
        pair = jnp.concatenate([frames(start, False), frames(start + GROUP, last)], axis=1)
        high, low = split(pair)
        step = dot(first_high, high) + dot(first_high, low) + dot(first_low, high)
        for h in range(2):
            re = step[:half, h * LANES:(h + 1) * LANES].reshape(GROUP, FINE, LANES)
            im = step[half:, h * LANES:(h + 1) * LANES].reshape(GROUP, FINE, LANES)
            turned = jnp.concatenate([re * fwd_cos + im * fwd_sin, im * fwd_cos - re * fwd_sin], axis=2)
            high, low = split(turned.reshape(half, 2 * LANES))
            wide = dot(high, narrow[second])
            value = wide[:, :LANES] + wide[:, LANES:] + dot(low, narrow[second, :LANES])
            spec[pl.ds((start + h * GROUP) * FINE, half)] = value
            power = power + jnp.sum((value * value).reshape(GROUP, FINE, LANES), axis=0)
        return power

    power = jnp.zeros((FINE, LANES), jnp.float32)
    pairs = segs // (2 * GROUP)
    power = repeat(pairs - 1, lambda i, p: forward(i * 2 * GROUP, p, False), power)
    power = forward((pairs - 1) * 2 * GROUP, power, True)
    power = power + pltpu.roll(power, LANES // 2, 1)
    density = power / (segs * energy) + FLOOR
    inverse_density = natural((1.0 / jnp.concatenate([density] * 4, axis=0)).T, 0, None)

    place = lax.axis_index("tm") * own
    column = lax.broadcasted_iota(jnp.int32, (GROUP, LANES), 1)

    def block(number, carry):
        at = pl.multiple_of((place + number * GROUP) * FINE, half)
        white = spec[pl.ds(at, half)].reshape(GROUP, FINE, LANES) / density[None]
        white = white.astype(jnp.bfloat16).astype(jnp.float32).reshape(2, 4 * FINE, LANES)
        re_parts, im_parts = [], []
        for side in range(2):
            flipped = white[side].T
            for s in range(4):
                re_parts.append(natural(flipped, 0, s))
                im_parts.append(natural(flipped, LANES // 2, s))
        white_re, white_im = jnp.stack(re_parts), jnp.stack(im_parts)

        def pair_of(step, result):
            sides, norms = [], []
            for side in range(2):
                m = 2 * step + side
                h_re, h_im = bank[0, m], bank[1, m]
                norms.append(jnp.sum((h_re * h_re + h_im * h_im) * inverse_density, keepdims=True))
                c_re = h_re[None] * white_re + h_im[None] * white_im
                c_im = h_re[None] * white_im - h_im[None] * white_re
                both = jnp.concatenate([c_re, c_im], axis=0).reshape(2 * GROUP * ROWS, LANES)
                sides.append(both.astype(jnp.bfloat16))
            section = dot(third, jnp.concatenate(sides, axis=1))
            for side in range(2):
                re = section[:half, side * LANES:(side + 1) * LANES].reshape(GROUP, FINE, LANES)
                im = section[half:, side * LANES:(side + 1) * LANES].reshape(GROUP, FINE, LANES)
                turned = jnp.concatenate([re * inv_cos - im * inv_sin, re * inv_sin + im * inv_cos], axis=2)
                wave = dot(turned.reshape(half, 2 * LANES).astype(jnp.bfloat16), narrow[fourth])
                square = wave[:, :LANES] * wave[:, :LANES] + wave[:, LANES:] * wave[:, LANES:]
                top = jnp.max(jnp.max(square.reshape(GROUP, FINE, LANES), axis=1), axis=1, keepdims=True)
                value = jnp.sqrt(top) / (jnp.sqrt(norms[side]) * math.sqrt(energy))
                result = jnp.where(column == 2 * step + side, value, result)
            return result

        result = repeat(count // 2, pair_of, jnp.zeros((GROUP, LANES), jnp.float32))
        out[pl.ds(number * GROUP, GROUP)] = result[:, :count]
        return carry

    repeat(own // GROUP, block, 0)


def swap(array, axis, bits):
    return lax.ppermute(array, axis, [(i, i ^ bits) for i in range(lax.axis_size(axis))])


def on_device(strain, templates, cutoff):
    tm, chips = lax.axis_size("tm"), lax.axis_size("tm") * lax.axis_size("chip")
    size = strain.shape[0] // HOP
    segs = 2 * chips * size
    own = segs // tm
    count = templates.shape[1]
    smem = pl.BlockSpec(memory_space=pltpu.SMEM)
    vmem = pl.BlockSpec(memory_space=pltpu.VMEM)
    anywhere = pl.BlockSpec(memory_space=pl.ANY)
    params = pltpu.CompilerParams(vmem_limit_bytes=40 * 1024 * 1024)
    f32 = jnp.float32

    copies = pl.pallas_call(
        pack_kernel,
        out_shape=jax.ShapeDtypeStruct((chips, size * ROWS, LANES), f32),
        in_specs=[anywhere],
        out_specs=anywhere,
        scratch_shapes=[pltpu.SemaphoreType.DMA((chips,))],
        name="pack",
    )(strain.reshape(size * ROWS, LANES))
    copies, templates = lax.optimization_barrier((copies, templates))
    mine = lax.all_to_all(copies, ("tm", "chip"), split_axis=0, concat_axis=0, tiled=True)
    blocks = [swap(templates, "tm", other) for other in range(1, tm)]
    mine, *blocks = lax.optimization_barrier((mine, *blocks))
    others = swap(mine, "core", 1)
    blocks = [templates] + blocks
    bank = pl.pallas_call(
        functools.partial(bank_kernel, tm),
        out_shape=jax.ShapeDtypeStruct((2, count, ROWS, LANES), f32),
        in_specs=[vmem] * tm + [smem],
        out_specs=vmem,
        scratch_shapes=[pltpu.VMEM((ROWS, count, 2 * LANES), jnp.bfloat16)],
        compiler_params=params,
        cost_estimate=pl.CostEstimate(flops=0, bytes_accessed=2500000, transcendentals=0),
        name="bank",
    )(*blocks, cutoff)
    narrow, broad, energy = tables()
    return pl.pallas_call(
        functools.partial(filter_kernel, energy),
        out_shape=jax.ShapeDtypeStruct((own, count), f32),
        in_specs=[vmem] * 5,
        out_specs=vmem,
        scratch_shapes=[
            pltpu.VMEM((segs * FINE, LANES), f32),
            pltpu.VMEM((chips, 2, size * ROWS, LANES), f32),
        ],
        compiler_params=params,
        name="matched_filter",
    )(mine, others, bank, jnp.asarray(narrow), jnp.asarray(broad))


def solution(mesh):
    tm, tmpl = mesh.devices.shape
    split_mesh = Mesh(mesh.devices.reshape(tm, tmpl // 2, 2), ("tm", "chip", "core"))
    bank = ("chip", "core")
    in_specs = (P(("tm",) + bank), P(None, bank, "tm"), P(bank))
    out_specs = P("tm", bank)
    return jax.shard_map(
        on_device, mesh=split_mesh, in_specs=in_specs, out_specs=out_specs, check_vma=False
    )
```

```python
import functools
import math

import jax
import jax.numpy as jnp
import ml_dtypes
import numpy as np
from jax import lax
from jax.experimental import pallas as pl
from jax.experimental.pallas import tpu as pltpu
from jax.sharding import PartitionSpec as P

NFFT = 4096
BINS = 2048
HOP = 2048
LANES = 128
ROWS = HOP // LANES
FINE = 32
GROUP = 8
FLOOR = 1e-6

ROOT_SCALE = {128: 1.66575, 64: 1.66575, 32: 1.6245, 16: 1.6245, 8: 1.6245}


def root_order(index, period):
    return period // math.gcd(int(index), period)


def row_scale(count, period):
    return np.array([ROOT_SCALE.get(root_order(i, period), 1.0) for i in range(count)])


def as_bf16(table):
    return np.asarray(table, np.float32).astype(ml_dtypes.bfloat16)


def two_parts(table):
    high = as_bf16(table)
    low = as_bf16(np.asarray(table, np.float64) - high.astype(np.float64))
    return high, low


def turn(left, right, period):
    angle = 2.0 * np.pi * (np.outer(left, right) % period) / period
    return np.cos(angle), np.sin(angle)


@functools.lru_cache(maxsize=None)
def tables():
    fine, wide, rows = np.arange(FINE), np.arange(LANES), np.arange(ROWS)
    window = 0.5 - 0.5 * np.cos(2.0 * np.pi * np.arange(NFFT) / NFFT)
    cos, sin = turn(fine, fine, FINE)
    first_high, first_low = two_parts(np.tile(np.concatenate([cos, -sin]), (1, GROUP)))
    fwd_cos, fwd_sin = turn(fine, wide, NFFT)
    f_order = np.array([4 * d + g for g in range(4) for d in range(ROWS)])
    cos, sin = turn(wide, f_order, LANES)
    second_high, second_low = two_parts(np.block([[cos, -sin], [sin, cos]]))
    scale_q, scale_c = row_scale(FINE, FINE), row_scale(LANES, LANES)
    cos, sin = turn(fine, rows, FINE)
    cos, sin = np.tile(cos * scale_q[:, None], (1, GROUP)), np.tile(sin * scale_q[:, None], (1, GROUP))
    third = np.block([[cos, -sin], [sin, cos]])
    inv_cos, inv_sin = turn(fine, wide, NFFT)
    undo = 1.0 / (scale_q[:, None] * scale_c[None, :])
    cos, sin = turn(wide, wide, LANES)
    cos, sin = cos * scale_c[:, None], sin * scale_c[:, None]
    fourth = np.block([[cos, sin], [-sin, cos]])
    narrow = np.concatenate(
        [first_high, first_low, as_bf16(third), np.concatenate([second_high, second_low], axis=1), as_bf16(fourth)]
    )
    broad = np.concatenate([window.reshape(FINE, LANES), fwd_cos, fwd_sin, inv_cos * undo, inv_sin * undo])
    return narrow, np.asarray(broad, np.float32), float((window * window).sum())


def dot(left, right):
    return jnp.dot(left, right, preferred_element_type=jnp.float32)


def split(value):
    high = value.astype(jnp.bfloat16)
    return high, (value - high.astype(jnp.float32)).astype(jnp.bfloat16)


def repeat(count, body, carry):
    if count <= 8:
        for step in range(count):
            carry = body(step, carry)
        return carry
    return lax.fori_loop(0, count, body, carry)


def block_diagonal(rows, width):
    lane = lax.broadcasted_iota(jnp.int32, rows.shape, 1)
    owner = lax.rem(lane // width, GROUP)
    return jnp.concatenate(
        [jnp.where(owner == s, rows, jnp.zeros_like(rows)) for s in range(GROUP)], axis=0
    )


def natural(flipped, at, source):
    part = lax.broadcasted_iota(jnp.int32, (ROWS, LANES), 1) // FINE
    result = None
    for g in range(4):
        piece = flipped[at + g * ROWS:at + (g + 1) * ROWS]
        if source is not None and g != source:
            piece = pltpu.roll(piece, ((g - source) % 4) * FINE, 1)
        result = piece if g == 0 else jnp.where(part == g, piece, result)
    return result


def spread(part, width):
    return jnp.concatenate([block_diagonal(part[:FINE], width), block_diagonal(part[FINE:], width)])


def halved(part):
    lane = lax.broadcasted_iota(jnp.int32, (FINE, part.shape[1]), 1)
    rows = []
    for at in (0, FINE):
        table = part[at:at + FINE]
        zero = jnp.zeros_like(table)
        for s in range(GROUP + 1):
            low = min(s, GROUP - 1) * FINE + (ROWS if s == GROUP else 0)
            high = min(s, GROUP - 1) * FINE + (ROWS if s == GROUP - 1 else FINE)
            rows.append(jnp.where((lane >= low) & (lane < high), table, zero))
    return jnp.concatenate(rows)


def prepare_kernel(strain, templates, narrow, chunk, block, first, third):
    chunk[...] = strain[...]
    block[...] = templates[...]
    first[0] = halved(narrow[:2 * FINE])
    first[1] = halved(narrow[2 * FINE:4 * FINE])
    third[...] = spread(narrow[4 * FINE:6 * FINE], ROWS)


def bank_kernel(blocks, cutoff, bank, gathered):
    rank = lax.axis_index("tm")
    devices, _, count, width = blocks.shape
    for other in range(devices):
        first = (rank ^ other) * (width // LANES)
        for at in range(width // LANES):
            lanes = slice(at * LANES, (at + 1) * LANES)
            gathered[first + at] = jnp.concatenate([blocks[other, 0, :, lanes], blocks[other, 1, :, lanes]], axis=1)
    lane = lax.broadcasted_iota(jnp.int32, (ROWS, LANES), 1)
    row = lax.broadcasted_iota(jnp.int32, (ROWS, LANES), 0)
    bins = row * LANES + lane
    shape = (count * ROWS, count * ROWS)
    to, source = lax.broadcasted_iota(jnp.int32, shape, 0), lax.broadcasted_iota(jnp.int32, shape, 1)
    order = (source == (to % ROWS) * count + to // ROWS).astype(jnp.float32).astype(jnp.bfloat16)
    value = dot(order, gathered[...].reshape(ROWS * count, 2 * LANES))
    for m in range(count):
        keep = bins < cutoff[m]
        rows = slice(m * ROWS, (m + 1) * ROWS)
        bank[0, m] = jnp.where(keep, value[rows, :LANES], 0.0)
        bank[1, m] = jnp.where(keep, value[rows, LANES:], 0.0)


def forward_kernel(offsets, chunks, first, narrow, broad, spec, sent, record):
    rank = lax.axis_index("tmpl")
    size = chunks.shape[0] // len(offsets)
    for at, offset in enumerate(offsets):
        record[pl.ds((rank ^ offset) * size, size)] = chunks[at * size:(at + 1) * size]
    own = record.shape[0]
    w_low, w_high = broad[:ROWS][None], broad[ROWS:FINE][None]
    fwd_cos, fwd_sin = broad[FINE:2 * FINE][None], broad[2 * FINE:3 * FINE][None]
    second = slice(6 * FINE, 6 * FINE + 2 * LANES)
    parts = GROUP + 1

    def group(start, power, last):
        here = record[pl.ds(start, GROUP)]
        if last:
            after = jnp.concatenate([record[pl.ds(start + 1, GROUP - 1)], record[pl.ds(0, 1)]], axis=0)
        else:
            after = record[pl.ds(start + 1, GROUP)]
        both = jnp.concatenate([here * w_low, after * w_high], axis=1)
        high, low = split(both.reshape(GROUP * FINE, LANES))
        step = dot(first[0], high) + dot(first[0], low) + dot(first[1], high)
        re = step[:parts * FINE].reshape(parts, FINE, LANES)
        im = step[parts * FINE:].reshape(parts, FINE, LANES)
        turned = jnp.concatenate([re * fwd_cos + im * fwd_sin, im * fwd_cos - re * fwd_sin], axis=2)
        high, low = split(turned.reshape(parts * FINE, 2 * LANES))
        wide = dot(high, narrow[second])
        value = wide[:, :LANES] + wide[:, LANES:] + dot(low, narrow[second, :LANES])
        value = jnp.concatenate([value, jnp.zeros((3 * FINE, LANES), jnp.float32)], axis=0)
        flipped = [value[i * LANES:(i + 1) * LANES].T for i in range(3)]
        pairs = [
            (natural(flipped[s // 4], 0, s % 4), natural(flipped[s // 4], LANES // 2, s % 4)) for s in range(parts)
        ]
        if last:
            sent[1], sent[2] = pairs[GROUP - 1]
            sent[3], sent[4] = pairs[GROUP]
        else:
            pairs[GROUP - 1] = tuple(a + b for a, b in zip(pairs[GROUP - 1], pairs[GROUP]))
        for s in range(GROUP):
            spec[0, pl.ds(start + s, 1)] = pairs[s][0][None]
            spec[1, pl.ds(start + s, 1)] = pairs[s][1][None]
            if s < GROUP - 1 or not last:
                power = power + pairs[s][0] * pairs[s][0] + pairs[s][1] * pairs[s][1]
        return power

    power = jnp.zeros((ROWS, LANES), jnp.float32)
    power = repeat(own // GROUP - 1, lambda i, p: group(i * GROUP, p, False), power)
    sent[0] = group(own - GROUP, power, True)


def filter_kernel(devices, segs, energy, *refs):
    shares = refs[:devices]
    spec, bank, third, narrow, broad, out, held = refs[devices:]
    own, count = out.shape
    half = GROUP * FINE
    inv_cos, inv_sin = broad[3 * FINE:4 * FINE][None], broad[4 * FINE:5 * FINE][None]
    fourth = slice(6 * FINE + 2 * LANES, 6 * FINE + 4 * LANES)
    rank = lax.axis_index("tm")
    power = shares[0][0]
    for share in shares[1:]:
        power = power + share[0]
    for other, share in enumerate(shares):
        held[rank ^ other] = share[3:5]
    for other, share in enumerate(shares):
        after = held[lax.rem((rank ^ other) + 1, devices)]
        re, im = share[1] + after[0], share[2] + after[1]
        power = power + re * re + im * im
        if other == 0:
            last_re, last_im = re, im
    density = power / (segs * energy) + FLOOR
    inverse_density = 1.0 / density
    column = lax.broadcasted_iota(jnp.int32, (GROUP, LANES), 1)

    def whiten(value):
        return (value / density[None]).astype(jnp.bfloat16).astype(jnp.float32)

    def block(start, last):
        x_re, x_im = spec[0, pl.ds(start, GROUP)], spec[1, pl.ds(start, GROUP)]
        if last:
            x_re = jnp.concatenate([x_re[:GROUP - 1], last_re[None]], axis=0)
            x_im = jnp.concatenate([x_im[:GROUP - 1], last_im[None]], axis=0)
        white_re, white_im = whiten(x_re), whiten(x_im)

        def pair_of(step, result):
            sides, norms = [], []
            for side in range(2):
                m = 2 * step + side
                h_re, h_im = bank[0, m], bank[1, m]
                norms.append(jnp.sum((h_re * h_re + h_im * h_im) * inverse_density, keepdims=True))
                c_re = h_re[None] * white_re + h_im[None] * white_im
                c_im = h_re[None] * white_im - h_im[None] * white_re
                both = jnp.concatenate([c_re, c_im], axis=0).reshape(2 * GROUP * ROWS, LANES)
                sides.append(both.astype(jnp.bfloat16))
            section = dot(third[...], jnp.concatenate(sides, axis=1))
            for side in range(2):
                re = section[:half, side * LANES:(side + 1) * LANES].reshape(GROUP, FINE, LANES)
                im = section[half:, side * LANES:(side + 1) * LANES].reshape(GROUP, FINE, LANES)
                turned = jnp.concatenate([re * inv_cos - im * inv_sin, re * inv_sin + im * inv_cos], axis=2)
                wave = dot(turned.reshape(half, 2 * LANES).astype(jnp.bfloat16), narrow[fourth])
                square = wave[:, :LANES] * wave[:, :LANES] + wave[:, LANES:] * wave[:, LANES:]
                top = jnp.max(jnp.max(square.reshape(GROUP, FINE, LANES), axis=1), axis=1, keepdims=True)
                value = jnp.sqrt(top) / (jnp.sqrt(norms[side]) * math.sqrt(energy))
                result = jnp.where(column == 2 * step + side, value, result)
            return result

        result = repeat(count // 2, pair_of, jnp.zeros((GROUP, LANES), jnp.float32))
        out[pl.ds(start, GROUP)] = result[:, :count]

    def earlier(number, carry):
        block(pl.multiple_of(number * GROUP, GROUP), False)
        return carry

    repeat(own // GROUP - 1, earlier, 0)
    block(own - GROUP, True)


def swap(array, axis, bits):
    return lax.ppermute(array, axis, [(i, i ^ bits) for i in range(lax.axis_size(axis))])


def on_device(strain, templates, cutoff):
    tm, tmpl = lax.axis_size("tm"), lax.axis_size("tmpl")
    size = strain.shape[0] // HOP
    own = size * tmpl
    count = templates.shape[1]
    smem = pl.BlockSpec(memory_space=pltpu.SMEM)
    vmem = pl.BlockSpec(memory_space=pltpu.VMEM)
    params = pltpu.CompilerParams(vmem_limit_bytes=40 * 1024 * 1024)
    f32, bf16 = jnp.float32, jnp.bfloat16
    narrow, broad, energy = tables()
    narrow, broad = jnp.asarray(narrow), jnp.asarray(broad)

    chunk = strain.reshape(size, ROWS, LANES)
    block = templates[None]
    bits = tmpl // 2
    arrived = swap(chunk, "tmpl", bits)
    chunk, block, first, third = pl.pallas_call(
        prepare_kernel,
        out_shape=(
            jax.ShapeDtypeStruct(chunk.shape, f32),
            jax.ShapeDtypeStruct(block.shape, bf16),
            jax.ShapeDtypeStruct((2, 2 * (GROUP + 1) * FINE, GROUP * FINE), bf16),
            jax.ShapeDtypeStruct((2 * GROUP * FINE, 2 * GROUP * ROWS), bf16),
        ),
        in_specs=[vmem] * 3,
        out_specs=(vmem,) * 4,
        compiler_params=params,
        cost_estimate=pl.CostEstimate(flops=0, bytes_accessed=3000000, transcendentals=0),
        name="prepare",
    )(chunk, block, narrow)
    chunks, offsets = jnp.concatenate([chunk, arrived], axis=0), [0, bits]
    while bits > 1:
        bits //= 2
        chunks = jnp.concatenate([chunks, swap(chunks, "tmpl", bits)], axis=0)
        offsets = offsets + [o ^ bits for o in offsets]
    bits = 1
    while bits < tm:
        block = jnp.concatenate([block, swap(block, "tm", bits)], axis=0)
        bits *= 2

    spec, sent = pl.pallas_call(
        functools.partial(forward_kernel, tuple(offsets)),
        out_shape=(
            jax.ShapeDtypeStruct((2, own, ROWS, LANES), f32),
            jax.ShapeDtypeStruct((5, ROWS, LANES), f32),
        ),
        in_specs=[vmem] * 4,
        out_specs=(vmem, vmem),
        scratch_shapes=[pltpu.VMEM((own, ROWS, LANES), f32)],
        compiler_params=params,
        name="forward",
    )(chunks, first, narrow, broad)
    shares = [sent] + [swap(sent, "tm", other) for other in range(1, tm)]
    bank = pl.pallas_call(
        bank_kernel,
        out_shape=jax.ShapeDtypeStruct((2, count, ROWS, LANES), f32),
        in_specs=[vmem, smem],
        out_specs=vmem,
        scratch_shapes=[pltpu.VMEM((ROWS, count, 2 * LANES), bf16)],
        compiler_params=params,
        cost_estimate=pl.CostEstimate(flops=0, bytes_accessed=2500000, transcendentals=0),
        name="bank",
    )(block, cutoff)
    return pl.pallas_call(
        functools.partial(filter_kernel, tm, own * tm, energy),
        out_shape=jax.ShapeDtypeStruct((own, count), f32),
        in_specs=[vmem] * (tm + 5),
        out_specs=vmem,
        scratch_shapes=[pltpu.VMEM((tm, 2, ROWS, LANES), f32)],
        compiler_params=params,
        name="matched_filter",
    )(*shares, spec, bank, third, narrow, broad)


def solution(mesh):
    in_specs = (P(("tm", "tmpl")), P(None, "tmpl", "tm"), P("tmpl"))
    out_specs = P("tm", "tmpl")
    return jax.shard_map(
        on_device, mesh=mesh, in_specs=in_specs, out_specs=out_specs, check_vma=False
    )
```

```python
import functools
import math

import jax
import jax.numpy as jnp
import ml_dtypes
import numpy as np
from jax import lax
from jax.experimental import pallas as pl
from jax.experimental.pallas import tpu as pltpu
from jax.sharding import PartitionSpec as P

NFFT = 4096
BINS = 2048
HOP = 2048
LANES = 128
ROWS = HOP // LANES
FINE = 32
GROUP = 8
FLOOR = 1e-6

ROOT_SCALE = {128: 1.66575, 64: 1.66575, 32: 1.6245, 16: 1.6245, 8: 1.6245}


def root_order(index, period):
    return period // math.gcd(int(index), period)


def row_scale(count, period):
    return np.array([ROOT_SCALE.get(root_order(i, period), 1.0) for i in range(count)])


def as_bf16(table):
    return np.asarray(table, np.float32).astype(ml_dtypes.bfloat16)


def two_parts(table):
    high = as_bf16(table)
    low = as_bf16(np.asarray(table, np.float64) - high.astype(np.float64))
    return high, low


def turn(left, right, period):
    angle = 2.0 * np.pi * (np.outer(left, right) % period) / period
    return np.cos(angle), np.sin(angle)


@functools.lru_cache(maxsize=None)
def tables():
    fine, wide, rows = np.arange(FINE), np.arange(LANES), np.arange(ROWS)
    window = 0.5 - 0.5 * np.cos(2.0 * np.pi * np.arange(NFFT) / NFFT)
    cos, sin = turn(fine, fine, FINE)
    first_high, first_low = two_parts(np.tile(np.concatenate([cos, -sin]), (1, GROUP)))
    fwd_cos, fwd_sin = turn(fine, wide, NFFT)
    f_order = np.array([4 * d + g for g in range(4) for d in range(ROWS)])
    cos, sin = turn(wide, f_order, LANES)
    second_high, second_low = two_parts(np.block([[cos, -sin], [sin, cos]]))
    scale_q, scale_c = row_scale(FINE, FINE), row_scale(LANES, LANES)
    cos, sin = turn(fine, rows, FINE)
    cos, sin = np.tile(cos * scale_q[:, None], (1, GROUP)), np.tile(sin * scale_q[:, None], (1, GROUP))
    third = np.block([[cos, -sin], [sin, cos]])
    inv_cos, inv_sin = turn(fine, wide, NFFT)
    undo = 1.0 / (scale_q[:, None] * scale_c[None, :])
    cos, sin = turn(wide, wide, LANES)
    cos, sin = cos * scale_c[:, None], sin * scale_c[:, None]
    fourth = np.block([[cos, sin], [-sin, cos]])
    narrow = np.concatenate(
        [first_high, first_low, as_bf16(third), np.concatenate([second_high, second_low], axis=1), as_bf16(fourth)]
    )
    broad = np.concatenate([window.reshape(FINE, LANES), fwd_cos, fwd_sin, inv_cos * undo, inv_sin * undo])
    return narrow, np.asarray(broad, np.float32), float((window * window).sum())


def dot(left, right):
    return jnp.dot(left, right, preferred_element_type=jnp.float32)


def split(value):
    high = value.astype(jnp.bfloat16)
    return high, (value - high.astype(jnp.float32)).astype(jnp.bfloat16)


def repeat(count, body, carry):
    if count <= 8:
        for step in range(count):
            carry = body(step, carry)
        return carry
    return lax.fori_loop(0, count, body, carry)


def block_diagonal(rows, width):
    lane = lax.broadcasted_iota(jnp.int32, rows.shape, 1)
    owner = lax.rem(lane // width, GROUP)
    return jnp.concatenate(
        [jnp.where(owner == s, rows, jnp.zeros_like(rows)) for s in range(GROUP)], axis=0
    )


def natural(flipped, at, source):
    part = lax.broadcasted_iota(jnp.int32, (ROWS, LANES), 1) // FINE
    result = None
    for g in range(4):
        piece = flipped[at + g * ROWS:at + (g + 1) * ROWS]
        if source is not None and g != source:
            piece = pltpu.roll(piece, ((g - source) % 4) * FINE, 1)
        result = piece if g == 0 else jnp.where(part == g, piece, result)
    return result


def pack_kernel(strain, copies):
    copies[...] = jnp.broadcast_to(strain[...][None], copies.shape)


def bank_kernel(devices, *refs):
    blocks = refs[:devices]
    cutoff, bank, gathered = refs[devices:]
    rank = lax.axis_index("tm")
    _, count, width = blocks[0].shape
    shape = (count, count)
    same = lax.broadcasted_iota(jnp.int32, shape, 0) == lax.broadcasted_iota(jnp.int32, shape, 1)
    column = jnp.sum(jnp.where(same, cutoff[...], 0), axis=1, keepdims=True)
    lane = lax.broadcasted_iota(jnp.int32, (count, LANES), 1)
    for other, block in enumerate(blocks):
        first = (rank ^ other) * (width // LANES)
        for at in range(width // LANES):
            lanes = slice(at * LANES, (at + 1) * LANES)
            keep = lane + (first + at) * LANES < column
            both = [jnp.where(keep, block[i, :, lanes].astype(jnp.float32), 0.0) for i in range(2)]
            gathered[first + at] = jnp.concatenate(both, axis=1).astype(jnp.bfloat16)
    shape = (count * ROWS, count * ROWS)
    to, source = lax.broadcasted_iota(jnp.int32, shape, 0), lax.broadcasted_iota(jnp.int32, shape, 1)
    order = (source == (to % ROWS) * count + to // ROWS).astype(jnp.float32).astype(jnp.bfloat16)
    value = dot(order, gathered[...].reshape(ROWS * count, 2 * LANES))
    bank[0] = value[:, :LANES].reshape(count, ROWS, LANES)
    bank[1] = value[:, LANES:].reshape(count, ROWS, LANES)


def filter_kernel(energy, record, bank, narrow, broad, out, spec):
    segs = record.shape[0]
    own, count = out.shape
    half = GROUP * FINE
    w_low, w_high = broad[:ROWS][None], broad[ROWS:FINE][None]
    fwd_cos, fwd_sin = broad[FINE:2 * FINE][None], broad[2 * FINE:3 * FINE][None]
    inv_cos, inv_sin = broad[3 * FINE:4 * FINE][None], broad[4 * FINE:5 * FINE][None]
    high, low = narrow[:2 * FINE], narrow[2 * FINE:4 * FINE]
    spread = lambda part: jnp.concatenate(
        [block_diagonal(part[:FINE], part.shape[1] // GROUP), block_diagonal(part[FINE:], part.shape[1] // GROUP)]
    )
    first_high, first_low = spread(high), spread(low)
    third_rows = narrow[4 * FINE:6 * FINE]
    third = jnp.concatenate([block_diagonal(third_rows[:FINE], ROWS), block_diagonal(third_rows[FINE:], ROWS)])
    second = slice(6 * FINE, 6 * FINE + 2 * LANES)
    fourth = slice(6 * FINE + 2 * LANES, 6 * FINE + 4 * LANES)

    def frames(start, last):
        here = record[pl.ds(start, GROUP)]
        if last:
            after = jnp.concatenate([record[pl.ds(start + 1, GROUP - 1)], record[pl.ds(0, 1)]], axis=0)
        else:
            after = record[pl.ds(start + 1, GROUP)]
        both = jnp.concatenate([here * w_low, after * w_high], axis=1)
        return both.reshape(half, LANES)

    def forward(start, power, last):
        pair = jnp.concatenate([frames(start, False), frames(start + GROUP, last)], axis=1)
        high, low = split(pair)
        step = dot(first_high, high) + dot(first_high, low) + dot(first_low, high)
        for h in range(2):
            re = step[:half, h * LANES:(h + 1) * LANES].reshape(GROUP, FINE, LANES)
            im = step[half:, h * LANES:(h + 1) * LANES].reshape(GROUP, FINE, LANES)
            turned = jnp.concatenate([re * fwd_cos + im * fwd_sin, im * fwd_cos - re * fwd_sin], axis=2)
            high, low = split(turned.reshape(half, 2 * LANES))
            wide = dot(high, narrow[second])
            value = wide[:, :LANES] + wide[:, LANES:] + dot(low, narrow[second, :LANES])
            spec[pl.ds((start + h * GROUP) * FINE, half)] = value
            power = power + jnp.sum((value * value).reshape(GROUP, FINE, LANES), axis=0)
        return power

    power = jnp.zeros((FINE, LANES), jnp.float32)
    pairs = segs // (2 * GROUP)
    power = repeat(pairs - 1, lambda i, p: forward(i * 2 * GROUP, p, False), power)
    power = forward((pairs - 1) * 2 * GROUP, power, True)
    power = power + pltpu.roll(power, LANES // 2, 1)
    density = power / (segs * energy) + FLOOR
    inverse_density = natural((1.0 / jnp.concatenate([density] * 4, axis=0)).T, 0, None)

    place = lax.axis_index("tm") * own
    column = lax.broadcasted_iota(jnp.int32, (GROUP, LANES), 1)

    def block(number, carry):
        at = pl.multiple_of((place + number * GROUP) * FINE, half)
        white = spec[pl.ds(at, half)].reshape(GROUP, FINE, LANES) / density[None]
        white = white.astype(jnp.bfloat16).astype(jnp.float32).reshape(2, 4 * FINE, LANES)
        re_parts, im_parts = [], []
        for side in range(2):
            flipped = white[side].T
            for s in range(4):
                re_parts.append(natural(flipped, 0, s))
                im_parts.append(natural(flipped, LANES // 2, s))
        white_re, white_im = jnp.stack(re_parts), jnp.stack(im_parts)

        def pair_of(step, result):
            sides, norms = [], []
            for side in range(2):
                m = 2 * step + side
                h_re, h_im = bank[0, m], bank[1, m]
                norms.append(jnp.sum((h_re * h_re + h_im * h_im) * inverse_density, keepdims=True))
                c_re = h_re[None] * white_re + h_im[None] * white_im
                c_im = h_re[None] * white_im - h_im[None] * white_re
                both = jnp.concatenate([c_re, c_im], axis=0).reshape(2 * GROUP * ROWS, LANES)
                sides.append(both.astype(jnp.bfloat16))
            section = dot(third, jnp.concatenate(sides, axis=1))
            for side in range(2):
                re = section[:half, side * LANES:(side + 1) * LANES].reshape(GROUP, FINE, LANES)
                im = section[half:, side * LANES:(side + 1) * LANES].reshape(GROUP, FINE, LANES)
                turned = jnp.concatenate([re * inv_cos - im * inv_sin, re * inv_sin + im * inv_cos], axis=2)
                wave = dot(turned.reshape(half, 2 * LANES).astype(jnp.bfloat16), narrow[fourth])
                square = wave[:, :LANES] * wave[:, :LANES] + wave[:, LANES:] * wave[:, LANES:]
                top = jnp.max(jnp.max(square.reshape(GROUP, FINE, LANES), axis=1), axis=1, keepdims=True)
                value = jnp.sqrt(top) / (jnp.sqrt(norms[side]) * math.sqrt(energy))
                result = jnp.where(column == 2 * step + side, value, result)
            return result

        result = repeat(count // 2, pair_of, jnp.zeros((GROUP, LANES), jnp.float32))
        out[pl.ds(number * GROUP, GROUP)] = result[:, :count]
        return carry

    repeat(own // GROUP, block, 0)


def swap(array, axis, bits):
    return lax.ppermute(array, axis, [(i, i ^ bits) for i in range(lax.axis_size(axis))])


def on_device(strain, templates, cutoff):
    tm, devices = lax.axis_size("tm"), lax.axis_size("tm") * lax.axis_size("tmpl")
    size = strain.shape[0] // HOP
    segs = devices * size
    own = segs // tm
    count = templates.shape[1]
    vmem = pl.BlockSpec(memory_space=pltpu.VMEM)
    params = pltpu.CompilerParams(vmem_limit_bytes=40 * 1024 * 1024)
    f32 = jnp.float32

    copies = pl.pallas_call(
        pack_kernel,
        out_shape=jax.ShapeDtypeStruct((devices, size * ROWS, LANES), f32),
        in_specs=[vmem],
        out_specs=vmem,
        compiler_params=params,
        name="pack",
    )(strain.reshape(size * ROWS, LANES))
    copies, held = lax.optimization_barrier((copies, templates))
    record = lax.all_to_all(copies, ("tm", "tmpl"), split_axis=0, concat_axis=0, tiled=True)
    record = record.reshape(segs, ROWS, LANES)
    blocks = [held] + [swap(held, "tm", other) for other in range(1, tm)]
    bank = pl.pallas_call(
        functools.partial(bank_kernel, tm),
        out_shape=jax.ShapeDtypeStruct((2, count, ROWS, LANES), f32),
        in_specs=[vmem] * (tm + 1),
        out_specs=vmem,
        scratch_shapes=[pltpu.VMEM((ROWS, count, 2 * LANES), jnp.bfloat16)],
        compiler_params=params,
        cost_estimate=pl.CostEstimate(flops=0, bytes_accessed=2500000, transcendentals=0),
        name="bank",
    )(*blocks, cutoff.reshape(1, count))
    narrow, broad, energy = tables()
    return pl.pallas_call(
        functools.partial(filter_kernel, energy),
        out_shape=jax.ShapeDtypeStruct((own, count), f32),
        in_specs=[vmem] * 4,
        out_specs=vmem,
        scratch_shapes=[pltpu.VMEM((segs * FINE, LANES), f32)],
        compiler_params=params,
        name="matched_filter",
    )(record, bank, jnp.asarray(narrow), jnp.asarray(broad))


def solution(mesh):
    in_specs = (P(("tm", "tmpl")), P(None, "tmpl", "tm"), P("tmpl"))
    out_specs = P("tm", "tmpl")
    return jax.shard_map(
        on_device, mesh=mesh, in_specs=in_specs, out_specs=out_specs, check_vma=False
    )
```

```python
import functools
import math

import jax
import jax.numpy as jnp
import ml_dtypes
import numpy as np
from jax import lax
from jax.experimental import pallas as pl
from jax.experimental.pallas import tpu as pltpu
from jax.sharding import PartitionSpec as P

NFFT = 4096
BINS = 2048
HOP = 2048
LANES = 128
ROWS = HOP // LANES
FINE = 32
GROUP = 8
FLOOR = 1e-6

ROOT_SCALE = {128: 1.66575, 64: 1.66575, 32: 1.6245, 16: 1.6245, 8: 1.6245}


def root_order(index, period):
    return period // math.gcd(int(index), period)


def row_scale(count, period):
    return np.array([ROOT_SCALE.get(root_order(i, period), 1.0) for i in range(count)])


def as_bf16(table):
    return np.asarray(table, np.float32).astype(ml_dtypes.bfloat16)


def two_parts(table):
    high = as_bf16(table)
    low = as_bf16(np.asarray(table, np.float64) - high.astype(np.float64))
    return high, low


def turn(left, right, period):
    angle = 2.0 * np.pi * (np.outer(left, right) % period) / period
    return np.cos(angle), np.sin(angle)


@functools.lru_cache(maxsize=None)
def tables():
    eye = np.eye(GROUP)
    fine, wide, rows = np.arange(FINE), np.arange(LANES), np.arange(ROWS)
    window = 0.5 - 0.5 * np.cos(2.0 * np.pi * np.arange(NFFT) / NFFT)
    cos, sin = turn(fine, fine, FINE)
    first_high, first_low = two_parts(np.concatenate([np.kron(eye, cos), np.kron(eye, -sin)]))
    fwd_cos, fwd_sin = turn(fine, wide, NFFT)
    f_order = np.array([4 * d + g for g in range(4) for d in range(ROWS)])
    cos, sin = turn(wide, f_order, LANES)
    second_high, second_low = two_parts(np.block([[cos, -sin], [sin, cos]]))
    scale_q = row_scale(FINE, FINE)
    cos, sin = turn(fine, rows, FINE)
    per_row = lambda t: np.einsum("qd,st->qstd", t * scale_q[:, None], eye).reshape(GROUP * FINE, GROUP * ROWS)
    third = np.block([[per_row(cos), per_row(-sin)], [per_row(sin), per_row(cos)]])
    fourth = []
    for q in range(FINE):
        cos, sin = turn(wide, q + FINE * wide, NFFT)
        fourth.append(np.block([[cos, sin], [-sin, cos]]) / scale_q[q])
    narrow = np.concatenate(
        [first_high, first_low, np.concatenate([second_high, second_low], axis=1), as_bf16(third)]
        + [as_bf16(table) for table in fourth]
    )
    broad = np.concatenate([window.reshape(FINE, LANES), fwd_cos, fwd_sin])
    return narrow, np.asarray(broad, np.float32), float((window * window).sum())


def dot(left, right):
    return jnp.dot(left, right, preferred_element_type=jnp.float32)


def split(value):
    high = value.astype(jnp.bfloat16)
    return high, (value - high.astype(jnp.float32)).astype(jnp.bfloat16)


def repeat(count, body, carry):
    if count <= 8:
        for step in range(count):
            carry = body(step, carry)
        return carry
    return lax.fori_loop(0, count, body, carry)


def natural(flipped, at, source):
    part = lax.broadcasted_iota(jnp.int32, (ROWS, LANES), 1) // FINE
    result = None
    for g in range(4):
        piece = flipped[at + g * ROWS:at + (g + 1) * ROWS]
        if source is not None and g != source:
            piece = pltpu.roll(piece, ((g - source) % 4) * FINE, 1)
        result = piece if g == 0 else jnp.where(part == g, piece, result)
    return result


def pack_kernel(strain, copies, held, filled, sems):
    fetch = pltpu.make_async_copy(strain, held, sems.at[0])
    fetch.start()
    fetch.wait()
    filled[...] = jnp.broadcast_to(held[...][None], filled.shape)
    give = pltpu.make_async_copy(filled, copies, sems.at[1])
    give.start()
    give.wait()


def bank_kernel(devices, *refs):
    blocks = refs[:devices]
    cutoff, bank, gathered = refs[devices:]
    rank = lax.axis_index("tm")
    _, count, width = blocks[0].shape
    shape = (count, count)
    same = lax.broadcasted_iota(jnp.int32, shape, 0) == lax.broadcasted_iota(jnp.int32, shape, 1)
    column = jnp.sum(jnp.where(same, cutoff[...], 0), axis=1, keepdims=True)
    lane = lax.broadcasted_iota(jnp.int32, (count, LANES), 1)
    for other, block in enumerate(blocks):
        first = (rank ^ other) * (width // LANES)
        for at in range(width // LANES):
            lanes = slice(at * LANES, (at + 1) * LANES)
            keep = lane + (first + at) * LANES < column
            both = [jnp.where(keep, block[i, :, lanes].astype(jnp.float32), 0.0) for i in range(2)]
            gathered[first + at] = jnp.concatenate(both, axis=1).astype(jnp.bfloat16)
    shape = (count * ROWS, count * ROWS)
    to, source = lax.broadcasted_iota(jnp.int32, shape, 0), lax.broadcasted_iota(jnp.int32, shape, 1)
    order = (source == (to % ROWS) * count + to // ROWS).astype(jnp.float32).astype(jnp.bfloat16)
    value = dot(order, gathered[...].reshape(ROWS * count, 2 * LANES))
    bank[0] = value[:, :LANES].reshape(count, ROWS, LANES)
    bank[1] = value[:, LANES:].reshape(count, ROWS, LANES)


def filter_kernel(energy, record, bank, narrow, broad, out, spec, sections):
    segs = record.shape[0]
    own, count = out.shape
    half = GROUP * FINE
    w_low, w_high = broad[:ROWS][None], broad[ROWS:FINE][None]
    fwd_cos, fwd_sin = broad[FINE:2 * FINE][None], broad[2 * FINE:3 * FINE][None]
    first = jnp.concatenate([narrow[:2 * half], narrow[:2 * half], narrow[2 * half:4 * half]], axis=1)
    second = narrow[4 * half:5 * half]
    second = jnp.concatenate([second, second], axis=0)

    def frames(start, last):
        here = record[pl.ds(start, GROUP)]
        if last:
            after = jnp.concatenate([record[pl.ds(start + 1, GROUP - 1)], record[pl.ds(0, 1)]], axis=0)
        else:
            after = record[pl.ds(start + 1, GROUP)]
        both = jnp.concatenate([here * w_low, after * w_high], axis=1)
        return both.reshape(half, LANES)

    def forward(start, power, last):
        pair = jnp.concatenate([frames(start, False), frames(start + GROUP, last)], axis=1)
        high, low = split(pair)
        step = dot(first, jnp.concatenate([high, low, high], axis=0))
        for h in range(2):
            re = step[:half, h * LANES:(h + 1) * LANES].reshape(GROUP, FINE, LANES)
            im = step[half:, h * LANES:(h + 1) * LANES].reshape(GROUP, FINE, LANES)
            turned = jnp.concatenate([re * fwd_cos + im * fwd_sin, im * fwd_cos - re * fwd_sin], axis=2)
            high, low = split(turned.reshape(half, 2 * LANES))
            both = dot(jnp.concatenate([high, low], axis=1), second)
            value = both[:, :LANES] + both[:, LANES:]
            spec[pl.ds((start + h * GROUP) * FINE, half)] = value
            power = power + jnp.sum((value * value).reshape(GROUP, FINE, LANES), axis=0)
        return power

    power = jnp.zeros((FINE, LANES), jnp.float32)
    pairs = segs // (2 * GROUP)
    power = repeat(pairs - 1, lambda i, p: forward(i * 2 * GROUP, p, False), power)
    power = forward((pairs - 1) * 2 * GROUP, power, True)
    power = power + pltpu.roll(power, LANES // 2, 1)
    density = power / (segs * energy) + FLOOR
    inverse_density = natural((1.0 / jnp.concatenate([density] * 4, axis=0)).T, 0, None)

    place = lax.axis_index("tm") * own
    column = lax.broadcasted_iota(jnp.int32, (GROUP, LANES), 1)

    def block(number, carry):
        at = pl.multiple_of((place + number * GROUP) * FINE, half)
        white = spec[pl.ds(at, half)].reshape(GROUP, FINE, LANES) / density[None]
        white = white.astype(jnp.bfloat16).astype(jnp.float32).reshape(2, 4 * FINE, LANES)
        re_parts, im_parts = [], []
        for side in range(2):
            flipped = white[side].T
            for s in range(4):
                re_parts.append(natural(flipped, 0, s))
                im_parts.append(natural(flipped, LANES // 2, s))
        white_re, white_im = jnp.stack(re_parts), jnp.stack(im_parts)

        norms = []
        for step in range(count // 2):
            sides = []
            for m in (2 * step, 2 * step + 1):
                h_re, h_im = bank[0, m], bank[1, m]
                norms.append(jnp.sum((h_re * h_re + h_im * h_im) * inverse_density, keepdims=True))
                c_re = h_re[None] * white_re + h_im[None] * white_im
                c_im = h_re[None] * white_im - h_im[None] * white_re
                both = jnp.concatenate([c_re, c_im], axis=0).reshape(2 * GROUP * ROWS, LANES)
                sides.append(both.astype(jnp.bfloat16))
            section = dot(narrow[5 * half:7 * half], jnp.concatenate(sides, axis=1))
            for part in range(2):
                rows = section[part * half:(part + 1) * half].reshape(FINE, GROUP, 2 * LANES)
                rows = jnp.concatenate([rows[:, :, :LANES], rows[:, :, LANES:]], axis=1)
                lanes = slice(part * LANES, (part + 1) * LANES)
                sections[:, 2 * step * GROUP:2 * (step + 1) * GROUP, lanes] = rows.astype(jnp.bfloat16)
        best = jnp.zeros((count * GROUP, LANES), jnp.float32)
        for q in range(FINE):
            wave = dot(sections[q], narrow[(7 + q) * half:(8 + q) * half])
            best = jnp.maximum(best, wave[:, :LANES] * wave[:, :LANES] + wave[:, LANES:] * wave[:, LANES:])
        result = jnp.zeros((GROUP, LANES), jnp.float32)
        for m in range(count):
            top = jnp.max(best[m * GROUP:(m + 1) * GROUP], axis=1, keepdims=True)
            value = jnp.sqrt(top) / (jnp.sqrt(norms[m]) * math.sqrt(energy))
            result = jnp.where(column == m, value, result)
        out[pl.ds(pl.multiple_of(number * GROUP, GROUP), GROUP)] = result[:, :count]
        return carry

    if own == GROUP:
        block(0, 0)
    else:
        lax.fori_loop(0, own // GROUP, block, 0)


def swap(array, axis, bits):
    return lax.ppermute(array, axis, [(i, i ^ bits) for i in range(lax.axis_size(axis))])


def on_device(strain, templates, cutoff):
    tm, devices = lax.axis_size("tm"), lax.axis_size("tm") * lax.axis_size("tmpl")
    size = strain.shape[0] // HOP
    segs = devices * size
    own = segs // tm
    count = templates.shape[1]
    vmem = pl.BlockSpec(memory_space=pltpu.VMEM)
    anywhere = pl.BlockSpec(memory_space=pl.ANY)
    params = pltpu.CompilerParams(vmem_limit_bytes=40 * 1024 * 1024)
    f32 = jnp.float32

    copies = pl.pallas_call(
        pack_kernel,
        out_shape=jax.ShapeDtypeStruct((devices, size * ROWS, LANES), f32),
        in_specs=[anywhere],
        out_specs=anywhere,
        scratch_shapes=[
            pltpu.VMEM((size * ROWS, LANES), f32),
            pltpu.VMEM((devices, size * ROWS, LANES), f32),
            pltpu.SemaphoreType.DMA((2,)),
        ],
        name="pack",
    )(strain.reshape(size * ROWS, LANES))
    copies, held = lax.optimization_barrier((copies, templates))
    record = lax.all_to_all(copies, ("tm", "tmpl"), split_axis=0, concat_axis=0, tiled=True)
    record = record.reshape(segs, ROWS, LANES)
    blocks = [held] + [swap(held, "tm", other) for other in range(1, tm)]
    bank = pl.pallas_call(
        functools.partial(bank_kernel, tm),
        out_shape=jax.ShapeDtypeStruct((2, count, ROWS, LANES), f32),
        in_specs=[vmem] * (tm + 1),
        out_specs=vmem,
        scratch_shapes=[pltpu.VMEM((ROWS, count, 2 * LANES), jnp.bfloat16)],
        compiler_params=params,
        cost_estimate=pl.CostEstimate(flops=0, bytes_accessed=2500000, transcendentals=0),
        name="bank",
    )(*blocks, cutoff.reshape(1, count))
    narrow, broad, energy = tables()
    return pl.pallas_call(
        functools.partial(filter_kernel, energy),
        out_shape=jax.ShapeDtypeStruct((own, count), f32),
        in_specs=[vmem] * 4,
        out_specs=vmem,
        scratch_shapes=[
            pltpu.VMEM((segs * FINE, LANES), f32),
            pltpu.VMEM((FINE, count * GROUP, 2 * LANES), jnp.bfloat16),
        ],
        compiler_params=params,
        name="matched_filter",
    )(record, bank, jnp.asarray(narrow), jnp.asarray(broad))


def solution(mesh):
    in_specs = (P(("tm", "tmpl")), P(None, "tmpl", "tm"), P("tmpl"))
    out_specs = P("tm", "tmpl")
    return jax.shard_map(
        on_device, mesh=mesh, in_specs=in_specs, out_specs=out_specs, check_vma=False
    )
```

```python
import functools
import math

import jax
import jax.numpy as jnp
import ml_dtypes
import numpy as np
from jax import lax
from jax.experimental import pallas as pl
from jax.experimental.pallas import tpu as pltpu
from jax.sharding import PartitionSpec as P

NFFT = 4096
BINS = 2048
HOP = 2048
LANES = 128
ROWS = HOP // LANES
FINE = 32
GROUP = 8
FLOOR = 1e-6

ROOT_SCALE = {128: 1.66575, 64: 1.66575, 32: 1.6245, 16: 1.6245, 8: 1.6245}


def root_order(index, period):
    return period // math.gcd(int(index), period)


def row_scale(count, period):
    return np.array([ROOT_SCALE.get(root_order(i, period), 1.0) for i in range(count)])


def as_bf16(table):
    return np.asarray(table, np.float32).astype(ml_dtypes.bfloat16)


def two_parts(table):
    high = as_bf16(table)
    low = as_bf16(np.asarray(table, np.float64) - high.astype(np.float64))
    return high, low


def turn(left, right, period):
    angle = 2.0 * np.pi * (np.outer(left, right) % period) / period
    return np.cos(angle), np.sin(angle)


@functools.lru_cache(maxsize=None)
def tables():
    fine, wide, rows = np.arange(FINE), np.arange(LANES), np.arange(ROWS)
    window = 0.5 - 0.5 * np.cos(2.0 * np.pi * np.arange(NFFT) / NFFT)
    cos, sin = turn(fine, fine, FINE)
    first_high, first_low = two_parts(np.tile(np.concatenate([cos, -sin]), (1, GROUP)))
    fwd_cos, fwd_sin = turn(fine, wide, NFFT)
    f_order = np.array([4 * d + g for g in range(4) for d in range(ROWS)])
    cos, sin = turn(wide, f_order, LANES)
    second_high, second_low = two_parts(np.block([[cos, -sin], [sin, cos]]))
    scale_q, scale_c = row_scale(FINE, FINE), row_scale(LANES, LANES)
    cos, sin = turn(fine, rows, FINE)
    cos, sin = np.tile(cos * scale_q[:, None], (1, GROUP)), np.tile(sin * scale_q[:, None], (1, GROUP))
    third = np.block([[cos, -sin], [sin, cos]])
    inv_cos, inv_sin = turn(fine, wide, NFFT)
    undo = 1.0 / (scale_q[:, None] * scale_c[None, :])
    cos, sin = turn(wide, wide, LANES)
    cos, sin = cos * scale_c[:, None], sin * scale_c[:, None]
    fourth = np.block([[cos, sin], [-sin, cos]])
    narrow = np.concatenate(
        [first_high, first_low, as_bf16(third), np.concatenate([second_high, second_low], axis=1), as_bf16(fourth)]
    )
    broad = np.concatenate([window.reshape(FINE, LANES), fwd_cos, fwd_sin, inv_cos * undo, inv_sin * undo])
    return narrow, np.asarray(broad, np.float32), float((window * window).sum())


def dot(left, right):
    return jnp.dot(left, right, preferred_element_type=jnp.float32)


def split(value):
    high = value.astype(jnp.bfloat16)
    return high, (value - high.astype(jnp.float32)).astype(jnp.bfloat16)


def repeat(count, body, carry):
    if count <= 8:
        for step in range(count):
            carry = body(step, carry)
        return carry
    return lax.fori_loop(0, count, body, carry)


def block_diagonal(rows, width):
    lane = lax.broadcasted_iota(jnp.int32, rows.shape, 1)
    owner = lax.rem(lane // width, GROUP)
    return jnp.concatenate(
        [jnp.where(owner == s, rows, jnp.zeros_like(rows)) for s in range(GROUP)], axis=0
    )


def natural(flipped, at, source):
    part = lax.broadcasted_iota(jnp.int32, (ROWS, LANES), 1) // FINE
    result = None
    for g in range(4):
        piece = flipped[at + g * ROWS:at + (g + 1) * ROWS]
        if source is not None and g != source:
            piece = pltpu.roll(piece, ((g - source) % 4) * FINE, 1)
        result = piece if g == 0 else jnp.where(part == g, piece, result)
    return result


def pack_kernel(strain, copies):
    copies[...] = jnp.broadcast_to(strain[...][None], copies.shape)


def bank_kernel(devices, *refs):
    blocks = refs[:devices]
    cutoff, bank, gathered = refs[devices:]
    rank = lax.axis_index("tm")
    _, count, width = blocks[0].shape
    shape = (count, count)
    same = lax.broadcasted_iota(jnp.int32, shape, 0) == lax.broadcasted_iota(jnp.int32, shape, 1)
    column = jnp.sum(jnp.where(same, cutoff[...], 0), axis=1, keepdims=True)
    lane = lax.broadcasted_iota(jnp.int32, (count, LANES), 1)
    for other, block in enumerate(blocks):
        first = (rank ^ other) * (width // LANES)
        for at in range(width // LANES):
            lanes = slice(at * LANES, (at + 1) * LANES)
            keep = lane + (first + at) * LANES < column
            both = [jnp.where(keep, block[i, :, lanes].astype(jnp.float32), 0.0) for i in range(2)]
            gathered[first + at] = jnp.concatenate(both, axis=1).astype(jnp.bfloat16)
    shape = (count * ROWS, count * ROWS)
    to, source = lax.broadcasted_iota(jnp.int32, shape, 0), lax.broadcasted_iota(jnp.int32, shape, 1)
    order = (source == (to % ROWS) * count + to // ROWS).astype(jnp.float32).astype(jnp.bfloat16)
    value = dot(order, gathered[...].reshape(ROWS * count, 2 * LANES))
    bank[0] = value[:, :LANES].reshape(count, ROWS, LANES)
    bank[1] = value[:, LANES:].reshape(count, ROWS, LANES)


def filter_kernel(energy, record, bank, narrow, broad, out, spec):
    segs = record.shape[0]
    own, count = out.shape
    half = GROUP * FINE
    w_low, w_high = broad[:ROWS][None], broad[ROWS:FINE][None]
    fwd_cos, fwd_sin = broad[FINE:2 * FINE][None], broad[2 * FINE:3 * FINE][None]
    inv_cos, inv_sin = broad[3 * FINE:4 * FINE][None], broad[4 * FINE:5 * FINE][None]
    high, low = narrow[:2 * FINE], narrow[2 * FINE:4 * FINE]
    spread = lambda part: jnp.concatenate(
        [block_diagonal(part[:FINE], part.shape[1] // GROUP), block_diagonal(part[FINE:], part.shape[1] // GROUP)]
    )
    first_high = spread(high)
    first = jnp.concatenate([first_high, first_high, spread(low)], axis=1)
    third_rows = narrow[4 * FINE:6 * FINE]
    third = jnp.concatenate([block_diagonal(third_rows[:FINE], ROWS), block_diagonal(third_rows[FINE:], ROWS)])
    second = slice(6 * FINE, 6 * FINE + 2 * LANES)
    fourth = slice(6 * FINE + 2 * LANES, 6 * FINE + 4 * LANES)

    def frames(start, last):
        here = record[pl.ds(start, GROUP)]
        if last:
            after = jnp.concatenate([record[pl.ds(start + 1, GROUP - 1)], record[pl.ds(0, 1)]], axis=0)
        else:
            after = record[pl.ds(start + 1, GROUP)]
        both = jnp.concatenate([here * w_low, after * w_high], axis=1)
        return both.reshape(half, LANES)

    def forward(start, power, last):
        pair = jnp.concatenate([frames(start, False), frames(start + GROUP, last)], axis=1)
        high, low = split(pair)
        step = dot(first, jnp.concatenate([high, low, high], axis=0))
        for h in range(2):
            re = step[:half, h * LANES:(h + 1) * LANES].reshape(GROUP, FINE, LANES)
            im = step[half:, h * LANES:(h + 1) * LANES].reshape(GROUP, FINE, LANES)
            turned = jnp.concatenate([re * fwd_cos + im * fwd_sin, im * fwd_cos - re * fwd_sin], axis=2)
            high, low = split(turned.reshape(half, 2 * LANES))
            both = dot(jnp.concatenate([high, low], axis=1), jnp.concatenate([narrow[second]] * 2, axis=0))
            value = both[:, :LANES] + both[:, LANES:]
            spec[pl.ds((start + h * GROUP) * FINE, half)] = value
            power = power + jnp.sum((value * value).reshape(GROUP, FINE, LANES), axis=0)
        return power

    power = jnp.zeros((FINE, LANES), jnp.float32)
    pairs = segs // (2 * GROUP)
    power = repeat(pairs - 1, lambda i, p: forward(i * 2 * GROUP, p, False), power)
    power = forward((pairs - 1) * 2 * GROUP, power, True)
    power = power + pltpu.roll(power, LANES // 2, 1)
    density = power / (segs * energy) + FLOOR
    inverse_density = natural((1.0 / jnp.concatenate([density] * 4, axis=0)).T, 0, None)

    place = lax.axis_index("tm") * own
    column = lax.broadcasted_iota(jnp.int32, (GROUP, LANES), 1)

    def block(number, carry):
        at = pl.multiple_of((place + number * GROUP) * FINE, half)
        white = spec[pl.ds(at, half)].reshape(GROUP, FINE, LANES) / density[None]
        white = white.astype(jnp.bfloat16).astype(jnp.float32).reshape(2, 4 * FINE, LANES)
        re_parts, im_parts = [], []
        for side in range(2):
            flipped = white[side].T
            for s in range(4):
                re_parts.append(natural(flipped, 0, s))
                im_parts.append(natural(flipped, LANES // 2, s))
        white_re, white_im = jnp.stack(re_parts), jnp.stack(im_parts)

        def pair_of(step, result):
            sides, norms = [], []
            for side in range(2):
                m = 2 * step + side
                h_re, h_im = bank[0, m], bank[1, m]
                norms.append(jnp.sum((h_re * h_re + h_im * h_im) * inverse_density, keepdims=True))
                c_re = h_re[None] * white_re + h_im[None] * white_im
                c_im = h_re[None] * white_im - h_im[None] * white_re
                both = jnp.concatenate([c_re, c_im], axis=0).reshape(2 * GROUP * ROWS, LANES)
                sides.append(both.astype(jnp.bfloat16))
            section = dot(third, jnp.concatenate(sides, axis=1))
            for side in range(2):
                re = section[:half, side * LANES:(side + 1) * LANES].reshape(GROUP, FINE, LANES)
                im = section[half:, side * LANES:(side + 1) * LANES].reshape(GROUP, FINE, LANES)
                turned = jnp.concatenate([re * inv_cos - im * inv_sin, re * inv_sin + im * inv_cos], axis=2)
                wave = dot(turned.reshape(half, 2 * LANES).astype(jnp.bfloat16), narrow[fourth])
                square = wave[:, :LANES] * wave[:, :LANES] + wave[:, LANES:] * wave[:, LANES:]
                top = jnp.max(jnp.max(square.reshape(GROUP, FINE, LANES), axis=1), axis=1, keepdims=True)
                value = jnp.sqrt(top) / (jnp.sqrt(norms[side]) * math.sqrt(energy))
                result = jnp.where(column == 2 * step + side, value, result)
            return result

        result = lax.fori_loop(
            0, count // 4, lambda i, r: pair_of(2 * i + 1, pair_of(2 * i, r)), jnp.zeros((GROUP, LANES), jnp.float32)
        )
        out[pl.ds(number * GROUP, GROUP)] = result[:, :count]
        return carry

    repeat(own // GROUP, block, 0)


def swap(array, axis, bits):
    return lax.ppermute(array, axis, [(i, i ^ bits) for i in range(lax.axis_size(axis))])


def on_device(strain, templates, cutoff):
    tm, devices = lax.axis_size("tm"), lax.axis_size("tm") * lax.axis_size("tmpl")
    size = strain.shape[0] // HOP
    segs = devices * size
    own = segs // tm
    count = templates.shape[1]
    vmem = pl.BlockSpec(memory_space=pltpu.VMEM)
    params = pltpu.CompilerParams(vmem_limit_bytes=40 * 1024 * 1024)
    f32 = jnp.float32

    copies = pl.pallas_call(
        pack_kernel,
        out_shape=jax.ShapeDtypeStruct((devices, size * ROWS, LANES), f32),
        in_specs=[vmem],
        out_specs=vmem,
        compiler_params=params,
        name="pack",
    )(strain.reshape(size * ROWS, LANES))
    copies, held = lax.optimization_barrier((copies, templates))
    record = lax.all_to_all(copies, ("tm", "tmpl"), split_axis=0, concat_axis=0, tiled=True)
    record = record.reshape(segs, ROWS, LANES)
    blocks = [held] + [swap(held, "tm", other) for other in range(1, tm)]
    bank = pl.pallas_call(
        functools.partial(bank_kernel, tm),
        out_shape=jax.ShapeDtypeStruct((2, count, ROWS, LANES), f32),
        in_specs=[vmem] * (tm + 1),
        out_specs=vmem,
        scratch_shapes=[pltpu.VMEM((ROWS, count, 2 * LANES), jnp.bfloat16)],
        compiler_params=params,
        cost_estimate=pl.CostEstimate(flops=0, bytes_accessed=2500000, transcendentals=0),
        name="bank",
    )(*blocks, cutoff.reshape(1, count))
    narrow, broad, energy = tables()
    return pl.pallas_call(
        functools.partial(filter_kernel, energy),
        out_shape=jax.ShapeDtypeStruct((own, count), f32),
        in_specs=[vmem] * 4,
        out_specs=vmem,
        scratch_shapes=[pltpu.VMEM((segs * FINE, LANES), f32)],
        compiler_params=params,
        name="matched_filter",
    )(record, bank, jnp.asarray(narrow), jnp.asarray(broad))


def solution(mesh):
    in_specs = (P(("tm", "tmpl")), P(None, "tmpl", "tm"), P("tmpl"))
    out_specs = P("tm", "tmpl")
    return jax.shard_map(
        on_device, mesh=mesh, in_specs=in_specs, out_specs=out_specs, check_vma=False
    )
```

```python
import functools
import math

import jax
import jax.numpy as jnp
import ml_dtypes
import numpy as np
from jax import lax
from jax.experimental import pallas as pl
from jax.experimental.pallas import tpu as pltpu
from jax.sharding import PartitionSpec as P

NFFT = 4096
BINS = 2048
HOP = 2048
LANES = 128
ROWS = HOP // LANES
FINE = 32
GROUP = 8
FLOOR = 1e-6

ROOT_SCALE = {128: 1.66575, 64: 1.66575, 32: 1.6245, 16: 1.6245, 8: 1.6245}


def root_order(index, period):
    return period // math.gcd(int(index), period)


def row_scale(count, period):
    return np.array([ROOT_SCALE.get(root_order(i, period), 1.0) for i in range(count)])


def as_bf16(table):
    return np.asarray(table, np.float32).astype(ml_dtypes.bfloat16)


def two_parts(table):
    high = as_bf16(table)
    low = as_bf16(np.asarray(table, np.float64) - high.astype(np.float64))
    return high, low


def turn(left, right, period):
    angle = 2.0 * np.pi * (np.outer(left, right) % period) / period
    return np.cos(angle), np.sin(angle)


@functools.lru_cache(maxsize=None)
def tables():
    fine, wide, rows = np.arange(FINE), np.arange(LANES), np.arange(ROWS)
    window = 0.5 - 0.5 * np.cos(2.0 * np.pi * np.arange(NFFT) / NFFT)
    cos, sin = turn(fine, fine, FINE)
    first_high, first_low = two_parts(np.tile(np.concatenate([cos, -sin]), (1, GROUP)))
    fwd_cos, fwd_sin = turn(fine, wide, NFFT)
    f_order = np.array([4 * d + g for g in range(4) for d in range(ROWS)])
    cos, sin = turn(wide, f_order, LANES)
    second_high, second_low = two_parts(np.block([[cos, -sin], [sin, cos]]))
    scale_q, scale_c = row_scale(FINE, FINE), row_scale(LANES, LANES)
    cos, sin = turn(fine, rows, FINE)
    cos, sin = np.tile(cos * scale_q[:, None], (1, GROUP)), np.tile(sin * scale_q[:, None], (1, GROUP))
    third = np.block([[cos, -sin], [sin, cos]])
    inv_cos, inv_sin = turn(fine, wide, NFFT)
    undo = 1.0 / (scale_q[:, None] * scale_c[None, :])
    cos, sin = turn(wide, wide, LANES)
    cos, sin = cos * scale_c[:, None], sin * scale_c[:, None]
    fourth = np.block([[cos, sin], [-sin, cos]])
    narrow = np.concatenate(
        [first_high, first_low, as_bf16(third), np.concatenate([second_high, second_low], axis=1), as_bf16(fourth)]
    )
    broad = np.concatenate([window.reshape(FINE, LANES), fwd_cos, fwd_sin, inv_cos * undo, inv_sin * undo])
    return narrow, np.asarray(broad, np.float32), float((window * window).sum())


def dot(left, right):
    return jnp.dot(left, right, preferred_element_type=jnp.float32)


def split(value):
    high = value.astype(jnp.bfloat16)
    return high, (value - high.astype(jnp.float32)).astype(jnp.bfloat16)


def repeat(count, body, carry):
    if count <= 8:
        for step in range(count):
            carry = body(step, carry)
        return carry
    return lax.fori_loop(0, count, body, carry)


def block_diagonal(rows, width):
    lane = lax.broadcasted_iota(jnp.int32, rows.shape, 1)
    owner = lax.rem(lane // width, GROUP)
    return jnp.concatenate(
        [jnp.where(owner == s, rows, jnp.zeros_like(rows)) for s in range(GROUP)], axis=0
    )


def natural(flipped, at, source):
    part = lax.broadcasted_iota(jnp.int32, (ROWS, LANES), 1) // FINE
    result = None
    for g in range(4):
        piece = flipped[at + g * ROWS:at + (g + 1) * ROWS]
        if source is not None and g != source:
            piece = pltpu.roll(piece, ((g - source) % 4) * FINE, 1)
        result = piece if g == 0 else jnp.where(part == g, piece, result)
    return result


def spread(part, width):
    return jnp.concatenate([block_diagonal(part[:FINE], width), block_diagonal(part[FINE:], width)])


def halved(part):
    lane = lax.broadcasted_iota(jnp.int32, (FINE, part.shape[1]), 1)
    rows = []
    for at in (0, FINE):
        table = part[at:at + FINE]
        zero = jnp.zeros_like(table)
        for s in range(GROUP + 1):
            low = min(s, GROUP - 1) * FINE + (ROWS if s == GROUP else 0)
            high = min(s, GROUP - 1) * FINE + (ROWS if s == GROUP - 1 else FINE)
            rows.append(jnp.where((lane >= low) & (lane < high), table, zero))
    return jnp.concatenate(rows)


def hold_kernel(strain, templates, chunk, block):
    chunk[...] = strain[...]
    block[...] = templates[...]


def bank_kernel(blocks, cutoff, bank, gathered):
    rank = lax.axis_index("tm")
    devices, _, count, width = blocks.shape
    shape = (count, count)
    same = lax.broadcasted_iota(jnp.int32, shape, 0) == lax.broadcasted_iota(jnp.int32, shape, 1)
    column = jnp.sum(jnp.where(same, cutoff[...], 0), axis=1, keepdims=True)
    lane = lax.broadcasted_iota(jnp.int32, (count, LANES), 1)
    for other in range(devices):
        first = (rank ^ other) * (width // LANES)
        for at in range(width // LANES):
            lanes = slice(at * LANES, (at + 1) * LANES)
            keep = lane + (first + at) * LANES < column
            both = [jnp.where(keep, blocks[other, i, :, lanes].astype(jnp.float32), 0.0) for i in range(2)]
            gathered[first + at] = jnp.concatenate(both, axis=1).astype(jnp.bfloat16)
    shape = (count * ROWS, count * ROWS)
    to, source = lax.broadcasted_iota(jnp.int32, shape, 0), lax.broadcasted_iota(jnp.int32, shape, 1)
    order = (source == (to % ROWS) * count + to // ROWS).astype(jnp.float32).astype(jnp.bfloat16)
    value = dot(order, gathered[...].reshape(ROWS * count, 2 * LANES))
    bank[0] = value[:, :LANES].reshape(count, ROWS, LANES)
    bank[1] = value[:, LANES:].reshape(count, ROWS, LANES)


def forward_kernel(offsets, mine, handed, narrow, broad, spec, sent, record):
    rank = lax.axis_index("tmpl")
    size = mine.shape[0] // len(offsets)
    odd = lax.rem(rank, 2) == 1
    for at, offset in enumerate(offsets):
        rows = slice(at * size, (at + 1) * size)
        record[pl.ds(((rank // 2) ^ offset) * size, size)] = jnp.where(odd, mine[rows], handed[rows])
    own = record.shape[0]
    w_low, w_high = broad[:ROWS][None], broad[ROWS:FINE][None]
    fwd_cos, fwd_sin = broad[FINE:2 * FINE][None], broad[2 * FINE:3 * FINE][None]
    second = slice(6 * FINE, 6 * FINE + 2 * LANES)
    parts = GROUP + 1
    first_high, first_low = halved(narrow[:2 * FINE]), halved(narrow[2 * FINE:4 * FINE])

    def group(start, power, last):
        here = record[pl.ds(start, GROUP)]
        if last:
            after = jnp.concatenate([record[pl.ds(start + 1, GROUP - 1)], record[pl.ds(0, 1)]], axis=0)
        else:
            after = record[pl.ds(start + 1, GROUP)]
        both = jnp.concatenate([here * w_low, after * w_high], axis=1)
        high, low = split(both.reshape(GROUP * FINE, LANES))
        step = dot(first_high, high) + dot(first_high, low) + dot(first_low, high)
        re = step[:parts * FINE].reshape(parts, FINE, LANES)
        im = step[parts * FINE:].reshape(parts, FINE, LANES)
        turned = jnp.concatenate([re * fwd_cos + im * fwd_sin, im * fwd_cos - re * fwd_sin], axis=2)
        high, low = split(turned.reshape(parts * FINE, 2 * LANES))
        wide = dot(high, narrow[second])
        value = wide[:, :LANES] + wide[:, LANES:] + dot(low, narrow[second, :LANES])
        value = jnp.concatenate([value, jnp.zeros((3 * FINE, LANES), jnp.float32)], axis=0)
        flipped = [value[i * LANES:(i + 1) * LANES].T for i in range(3)]
        pairs = [
            (natural(flipped[s // 4], 0, s % 4), natural(flipped[s // 4], LANES // 2, s % 4)) for s in range(parts)
        ]
        if last:
            sent[1], sent[2] = pairs[GROUP - 1]
            sent[3], sent[4] = pairs[GROUP]
        else:
            pairs[GROUP - 1] = tuple(a + b for a, b in zip(pairs[GROUP - 1], pairs[GROUP]))
        for s in range(GROUP):
            spec[0, pl.ds(start + s, 1)] = pairs[s][0][None]
            spec[1, pl.ds(start + s, 1)] = pairs[s][1][None]
            if s < GROUP - 1 or not last:
                power = power + pairs[s][0] * pairs[s][0] + pairs[s][1] * pairs[s][1]
        return power

    power = jnp.zeros((ROWS, LANES), jnp.float32)
    power = repeat(own // GROUP - 1, lambda i, p: group(i * GROUP, p, False), power)
    sent[0] = group(own - GROUP, power, True)


def filter_kernel(devices, segs, energy, *refs):
    sent, mine, handed, spec, bank, narrow, broad, out, held = refs
    odd = lax.rem(lax.axis_index("tmpl"), 2) == 1
    others = jnp.where(odd, mine[...], handed[...])
    shares = [sent[...]] + [others[5 * i:5 * (i + 1)] for i in range(devices - 1)]
    own, count = out.shape
    half = GROUP * FINE
    inv_cos, inv_sin = broad[3 * FINE:4 * FINE][None], broad[4 * FINE:5 * FINE][None]
    fourth = slice(6 * FINE + 2 * LANES, 6 * FINE + 4 * LANES)
    third = spread(narrow[4 * FINE:6 * FINE], ROWS)
    rank = lax.axis_index("tm")
    power = shares[0][0]
    for share in shares[1:]:
        power = power + share[0]
    for other, share in enumerate(shares):
        held[rank ^ other] = share[3:5]
    for other, share in enumerate(shares):
        after = held[lax.rem((rank ^ other) + 1, devices)]
        re, im = share[1] + after[0], share[2] + after[1]
        power = power + re * re + im * im
        if other == 0:
            last_re, last_im = re, im
    density = power / (segs * energy) + FLOOR
    inverse_density = 1.0 / density
    column = lax.broadcasted_iota(jnp.int32, (GROUP, LANES), 1)

    def whiten(value):
        return (value / density[None]).astype(jnp.bfloat16).astype(jnp.float32)

    def block(start, last):
        x_re, x_im = spec[0, pl.ds(start, GROUP)], spec[1, pl.ds(start, GROUP)]
        if last:
            x_re = jnp.concatenate([x_re[:GROUP - 1], last_re[None]], axis=0)
            x_im = jnp.concatenate([x_im[:GROUP - 1], last_im[None]], axis=0)
        white_re, white_im = whiten(x_re), whiten(x_im)

        def pair_of(step, result):
            sides, norms = [], []
            for side in range(2):
                m = 2 * step + side
                h_re, h_im = bank[0, m], bank[1, m]
                norms.append(jnp.sum((h_re * h_re + h_im * h_im) * inverse_density, keepdims=True))
                c_re = h_re[None] * white_re + h_im[None] * white_im
                c_im = h_re[None] * white_im - h_im[None] * white_re
                both = jnp.concatenate([c_re, c_im], axis=0).reshape(2 * GROUP * ROWS, LANES)
                sides.append(both.astype(jnp.bfloat16))
            section = dot(third, jnp.concatenate(sides, axis=1))
            for side in range(2):
                re = section[:half, side * LANES:(side + 1) * LANES].reshape(GROUP, FINE, LANES)
                im = section[half:, side * LANES:(side + 1) * LANES].reshape(GROUP, FINE, LANES)
                turned = jnp.concatenate([re * inv_cos - im * inv_sin, re * inv_sin + im * inv_cos], axis=2)
                wave = dot(turned.reshape(half, 2 * LANES).astype(jnp.bfloat16), narrow[fourth])
                square = wave[:, :LANES] * wave[:, :LANES] + wave[:, LANES:] * wave[:, LANES:]
                top = jnp.max(jnp.max(square.reshape(GROUP, FINE, LANES), axis=1), axis=1, keepdims=True)
                value = jnp.sqrt(top) / (jnp.sqrt(norms[side]) * math.sqrt(energy))
                result = jnp.where(column == 2 * step + side, value, result)
            return result

        result = repeat(count // 2, pair_of, jnp.zeros((GROUP, LANES), jnp.float32))
        out[pl.ds(start, GROUP)] = result[:, :count]

    def earlier(number, carry):
        block(pl.multiple_of(number * GROUP, GROUP), False)
        return carry

    repeat(own // GROUP - 1, earlier, 0)
    block(own - GROUP, True)


def swap(array, axis, bits):
    return lax.ppermute(array, axis, [(i, i ^ bits) for i in range(lax.axis_size(axis))])


def odd_swap(array, tm_bits, tmpl_bits):
    tm, tmpl = lax.axis_size("tm"), lax.axis_size("tmpl")
    pairs = [
        (i * tmpl + j, (i ^ tm_bits) * tmpl + (j ^ tmpl_bits)) for i in range(tm) for j in range(1, tmpl, 2)
    ]
    return lax.ppermute(array, ("tm", "tmpl"), pairs)


def hand(array, source):
    return lax.ppermute(array, "tmpl", [(j + source, j + 1 - source) for j in range(0, lax.axis_size("tmpl"), 2)])


def on_device(strain, templates, cutoff):
    tm, tmpl = lax.axis_size("tm"), lax.axis_size("tmpl")
    size = strain.shape[0] // HOP
    own = size * tmpl
    count = templates.shape[1]
    vmem = pl.BlockSpec(memory_space=pltpu.VMEM)
    params = pltpu.CompilerParams(vmem_limit_bytes=40 * 1024 * 1024)
    f32, bf16 = jnp.float32, jnp.bfloat16
    narrow, broad, energy = tables()
    narrow, broad = jnp.asarray(narrow), jnp.asarray(broad)

    chunk = strain.reshape(size, ROWS, LANES)
    block = templates[None]
    handed = hand(chunk, 0)
    chunk, block = pl.pallas_call(
        hold_kernel,
        out_shape=(jax.ShapeDtypeStruct(chunk.shape, f32), jax.ShapeDtypeStruct(block.shape, bf16)),
        in_specs=[vmem, vmem],
        out_specs=(vmem, vmem),
        compiler_params=params,
        cost_estimate=pl.CostEstimate(flops=0, bytes_accessed=3000000, transcendentals=0),
        name="hold",
    )(chunk, block)
    handed, block = lax.optimization_barrier((handed, block))
    chunks = jnp.concatenate([handed, chunk], axis=0)
    beside = swap(block, "tm", 1)
    offsets, bits = [0], tmpl // 2
    while bits > 1:
        arrived = odd_swap(chunks, 0, bits)
        if len(offsets) == 1:
            arrived, beside = lax.optimization_barrier((arrived, beside))
        chunks = jnp.concatenate([chunks, arrived], axis=0)
        offsets = offsets + [o ^ (bits // 2) for o in offsets]
        bits //= 2
    block = jnp.concatenate([block, beside], axis=0)
    bits = 2
    while bits < tm:
        block = jnp.concatenate([block, swap(block, "tm", bits)], axis=0)
        bits *= 2

    handed, block = lax.optimization_barrier((hand(chunks, 1), block))
    spec, sent = pl.pallas_call(
        functools.partial(forward_kernel, tuple(offsets)),
        out_shape=(
            jax.ShapeDtypeStruct((2, own, ROWS, LANES), f32),
            jax.ShapeDtypeStruct((5, ROWS, LANES), f32),
        ),
        in_specs=[vmem] * 4,
        out_specs=(vmem, vmem),
        scratch_shapes=[pltpu.VMEM((own, ROWS, LANES), f32)],
        compiler_params=params,
        name="forward",
    )(chunks, handed, narrow, broad)
    shares = jnp.concatenate([odd_swap(sent, other, 0) for other in range(1, tm)], axis=0)
    bank = pl.pallas_call(
        bank_kernel,
        out_shape=jax.ShapeDtypeStruct((2, count, ROWS, LANES), f32),
        in_specs=[vmem, vmem],
        out_specs=vmem,
        scratch_shapes=[pltpu.VMEM((ROWS, count, 2 * LANES), bf16)],
        compiler_params=params,
        cost_estimate=pl.CostEstimate(flops=0, bytes_accessed=2500000, transcendentals=0),
        name="bank",
    )(block, cutoff.reshape(1, count))
    return pl.pallas_call(
        functools.partial(filter_kernel, tm, own * tm, energy),
        out_shape=jax.ShapeDtypeStruct((own, count), f32),
        in_specs=[vmem] * 7,
        out_specs=vmem,
        scratch_shapes=[pltpu.VMEM((tm, 2, ROWS, LANES), f32)],
        compiler_params=params,
        name="matched_filter",
    )(sent, shares, hand(shares, 1), spec, bank, narrow, broad)


def solution(mesh):
    in_specs = (P(("tm", "tmpl")), P(None, "tmpl", "tm"), P("tmpl"))
    out_specs = P("tm", "tmpl")
    return jax.shard_map(
        on_device, mesh=mesh, in_specs=in_specs, out_specs=out_specs, check_vma=False
    )
```

```python
import functools
import math

import jax
import jax.numpy as jnp
import ml_dtypes
import numpy as np
from jax import lax
from jax.experimental import pallas as pl
from jax.experimental.pallas import tpu as pltpu
from jax.sharding import PartitionSpec as P

NFFT = 4096
BINS = 2048
HOP = 2048
LANES = 128
ROWS = HOP // LANES
FINE = 32
GROUP = 8
FLOOR = 1e-6

ROOT_SCALE = {128: 1.66575, 64: 1.66575, 32: 1.6245, 16: 1.6245, 8: 1.6245}


def root_order(index, period):
    return period // math.gcd(int(index), period)


def row_scale(count, period):
    return np.array([ROOT_SCALE.get(root_order(i, period), 1.0) for i in range(count)])


def as_bf16(table):
    return np.asarray(table, np.float32).astype(ml_dtypes.bfloat16)


def two_parts(table):
    high = as_bf16(table)
    low = as_bf16(np.asarray(table, np.float64) - high.astype(np.float64))
    return high, low


def turn(left, right, period):
    angle = 2.0 * np.pi * (np.outer(left, right) % period) / period
    return np.cos(angle), np.sin(angle)


@functools.lru_cache(maxsize=None)
def tables():
    fine, wide, rows = np.arange(FINE), np.arange(LANES), np.arange(ROWS)
    window = 0.5 - 0.5 * np.cos(2.0 * np.pi * np.arange(NFFT) / NFFT)
    cos, sin = turn(fine, fine, FINE)
    first_high, first_low = two_parts(np.tile(np.concatenate([cos, -sin]), (1, GROUP)))
    fwd_cos, fwd_sin = turn(fine, wide, NFFT)
    f_order = np.array([4 * d + g for g in range(4) for d in range(ROWS)])
    cos, sin = turn(wide, f_order, LANES)
    second_high, second_low = two_parts(np.block([[cos, -sin], [sin, cos]]))
    scale_q, scale_c = row_scale(FINE, FINE), row_scale(LANES, LANES)
    cos, sin = turn(fine, rows, FINE)
    cos, sin = np.tile(cos * scale_q[:, None], (1, GROUP)), np.tile(sin * scale_q[:, None], (1, GROUP))
    third = np.block([[cos, -sin], [sin, cos]])
    inv_cos, inv_sin = turn(fine, wide, NFFT)
    undo = 1.0 / (scale_q[:, None] * scale_c[None, :])
    cos, sin = turn(wide, wide, LANES)
    cos, sin = cos * scale_c[:, None], sin * scale_c[:, None]
    fourth = np.block([[cos, sin], [-sin, cos]])
    narrow = np.concatenate(
        [first_high, first_low, as_bf16(third), np.concatenate([second_high, second_low], axis=1), as_bf16(fourth)]
    )
    broad = np.concatenate([window.reshape(FINE, LANES), fwd_cos, fwd_sin, inv_cos * undo, inv_sin * undo])
    return narrow, np.asarray(broad, np.float32), float((window * window).sum())


def dot(left, right):
    return jnp.dot(left, right, preferred_element_type=jnp.float32)


def split(value):
    high = value.astype(jnp.bfloat16)
    return high, (value - high.astype(jnp.float32)).astype(jnp.bfloat16)


def repeat(count, body, carry):
    if count <= 8:
        for step in range(count):
            carry = body(step, carry)
        return carry
    return lax.fori_loop(0, count, body, carry)


def block_diagonal(rows, width):
    lane = lax.broadcasted_iota(jnp.int32, rows.shape, 1)
    owner = lax.rem(lane // width, GROUP)
    return jnp.concatenate(
        [jnp.where(owner == s, rows, jnp.zeros_like(rows)) for s in range(GROUP)], axis=0
    )


def natural(flipped, at, source):
    part = lax.broadcasted_iota(jnp.int32, (ROWS, LANES), 1) // FINE
    result = None
    for g in range(4):
        piece = flipped[at + g * ROWS:at + (g + 1) * ROWS]
        if source is not None and g != source:
            piece = pltpu.roll(piece, ((g - source) % 4) * FINE, 1)
        result = piece if g == 0 else jnp.where(part == g, piece, result)
    return result


def pack_kernel(strain, copies):
    copies[...] = jnp.broadcast_to(strain[...][None], copies.shape)


def bank_kernel(devices, *refs):
    blocks = refs[:devices]
    cutoff, bank, gathered = refs[devices:]
    rank = lax.axis_index("tm")
    _, count, width = blocks[0].shape
    shape = (count, count)
    same = lax.broadcasted_iota(jnp.int32, shape, 0) == lax.broadcasted_iota(jnp.int32, shape, 1)
    column = jnp.sum(jnp.where(same, cutoff[...], 0), axis=1, keepdims=True)
    lane = lax.broadcasted_iota(jnp.int32, (count, LANES), 1)
    for other, block in enumerate(blocks):
        first = (rank ^ other) * (width // LANES)
        for at in range(width // LANES):
            lanes = slice(at * LANES, (at + 1) * LANES)
            keep = lane + (first + at) * LANES < column
            both = [jnp.where(keep, block[i, :, lanes].astype(jnp.float32), 0.0) for i in range(2)]
            gathered[first + at] = jnp.concatenate(both, axis=1).astype(jnp.bfloat16)
    shape = (count * ROWS, count * ROWS)
    to, source = lax.broadcasted_iota(jnp.int32, shape, 0), lax.broadcasted_iota(jnp.int32, shape, 1)
    order = (source == (to % ROWS) * count + to // ROWS).astype(jnp.float32).astype(jnp.bfloat16)
    value = dot(order, gathered[...].reshape(ROWS * count, 2 * LANES))
    bank[0] = value[:, :LANES].reshape(count, ROWS, LANES)
    bank[1] = value[:, LANES:].reshape(count, ROWS, LANES)


def filter_kernel(energy, record, bank, narrow, broad, out, spec):
    segs = record.shape[0]
    own, count = out.shape
    half = GROUP * FINE
    w_low, w_high = broad[:ROWS][None], broad[ROWS:FINE][None]
    fwd_cos, fwd_sin = broad[FINE:2 * FINE][None], broad[2 * FINE:3 * FINE][None]
    inv_cos, inv_sin = broad[3 * FINE:4 * FINE][None], broad[4 * FINE:5 * FINE][None]
    high, low = narrow[:2 * FINE], narrow[2 * FINE:4 * FINE]
    spread = lambda part: jnp.concatenate(
        [block_diagonal(part[:FINE], part.shape[1] // GROUP), block_diagonal(part[FINE:], part.shape[1] // GROUP)]
    )
    first_high = spread(high)
    first = jnp.concatenate([first_high, first_high, spread(low)], axis=1)
    third_rows = narrow[4 * FINE:6 * FINE]
    third = jnp.concatenate([block_diagonal(third_rows[:FINE], ROWS), block_diagonal(third_rows[FINE:], ROWS)])
    second = slice(6 * FINE, 6 * FINE + 2 * LANES)
    fourth = slice(6 * FINE + 2 * LANES, 6 * FINE + 4 * LANES)

    def frames(start, last):
        here = record[pl.ds(start, GROUP)]
        if last:
            after = jnp.concatenate([record[pl.ds(start + 1, GROUP - 1)], record[pl.ds(0, 1)]], axis=0)
        else:
            after = record[pl.ds(start + 1, GROUP)]
        both = jnp.concatenate([here * w_low, after * w_high], axis=1)
        return both.reshape(half, LANES)

    def forward(start, power, last):
        pair = jnp.concatenate([frames(start, False), frames(start + GROUP, last)], axis=1)
        high, low = split(pair)
        step = dot(first, jnp.concatenate([high, low, high], axis=0))
        for h in range(2):
            re = step[:half, h * LANES:(h + 1) * LANES].reshape(GROUP, FINE, LANES)
            im = step[half:, h * LANES:(h + 1) * LANES].reshape(GROUP, FINE, LANES)
            turned = jnp.concatenate([re * fwd_cos + im * fwd_sin, im * fwd_cos - re * fwd_sin], axis=2)
            high, low = split(turned.reshape(half, 2 * LANES))
            both = dot(jnp.concatenate([high, low], axis=1), jnp.concatenate([narrow[second]] * 2, axis=0))
            value = both[:, :LANES] + both[:, LANES:]
            spec[pl.ds((start + h * GROUP) * FINE, half)] = value
            power = power + jnp.sum((value * value).reshape(GROUP, FINE, LANES), axis=0)
        return power

    power = jnp.zeros((FINE, LANES), jnp.float32)
    pairs = segs // (2 * GROUP)
    power = repeat(pairs - 1, lambda i, p: forward(i * 2 * GROUP, p, False), power)
    power = forward((pairs - 1) * 2 * GROUP, power, True)
    power = power + pltpu.roll(power, LANES // 2, 1)
    density = power / (segs * energy) + FLOOR
    inverse_density = natural((1.0 / jnp.concatenate([density] * 4, axis=0)).T, 0, None)

    place = lax.axis_index("tm") * own
    column = lax.broadcasted_iota(jnp.int32, (GROUP, LANES), 1)

    def block(number, carry):
        at = pl.multiple_of((place + number * GROUP) * FINE, half)
        white = spec[pl.ds(at, half)].reshape(GROUP, FINE, LANES) / density[None]
        white = white.astype(jnp.bfloat16).astype(jnp.float32).reshape(2, 4 * FINE, LANES)
        re_parts, im_parts = [], []
        for side in range(2):
            flipped = white[side].T
            for s in range(4):
                re_parts.append(natural(flipped, 0, s))
                im_parts.append(natural(flipped, LANES // 2, s))
        white_re, white_im = jnp.stack(re_parts), jnp.stack(im_parts)

        def pair_of(step, result):
            sides, norms = [], []
            for side in range(2):
                m = 2 * step + side
                h_re, h_im = bank[0, m], bank[1, m]
                norms.append(jnp.sum((h_re * h_re + h_im * h_im) * inverse_density, keepdims=True))
                c_re = h_re[None] * white_re + h_im[None] * white_im
                c_im = h_re[None] * white_im - h_im[None] * white_re
                both = jnp.concatenate([c_re, c_im], axis=0).reshape(2 * GROUP * ROWS, LANES)
                sides.append(both.astype(jnp.bfloat16))
            section = dot(third, jnp.concatenate(sides, axis=1))
            for side in range(2):
                re = section[:half, side * LANES:(side + 1) * LANES].reshape(GROUP, FINE, LANES)
                im = section[half:, side * LANES:(side + 1) * LANES].reshape(GROUP, FINE, LANES)
                turned = jnp.concatenate([re * inv_cos - im * inv_sin, re * inv_sin + im * inv_cos], axis=2)
                wave = dot(turned.reshape(half, 2 * LANES).astype(jnp.bfloat16), narrow[fourth])
                square = wave[:, :LANES] * wave[:, :LANES] + wave[:, LANES:] * wave[:, LANES:]
                top = jnp.max(jnp.max(square.reshape(GROUP, FINE, LANES), axis=1), axis=1, keepdims=True)
                value = jnp.sqrt(top) / (jnp.sqrt(norms[side]) * math.sqrt(energy))
                result = jnp.where(column == 2 * step + side, value, result)
            return result

        result = repeat(count // 2, pair_of, jnp.zeros((GROUP, LANES), jnp.float32))
        out[pl.ds(number * GROUP, GROUP)] = result[:, :count]
        return carry

    repeat(own // GROUP, block, 0)


def swap(array, axis, bits):
    return lax.ppermute(array, axis, [(i, i ^ bits) for i in range(lax.axis_size(axis))])


def on_device(strain, templates, cutoff):
    tm, devices = lax.axis_size("tm"), lax.axis_size("tm") * lax.axis_size("tmpl")
    size = strain.shape[0] // HOP
    segs = devices * size
    own = segs // tm
    count = templates.shape[1]
    vmem = pl.BlockSpec(memory_space=pltpu.VMEM)
    params = pltpu.CompilerParams(vmem_limit_bytes=40 * 1024 * 1024)
    f32 = jnp.float32

    copies = pl.pallas_call(
        pack_kernel,
        out_shape=pltpu.VMEM((devices, size * ROWS, LANES), f32),
        in_specs=[vmem],
        out_specs=vmem,
        compiler_params=params,
        name="pack",
    )(strain.reshape(size * ROWS, LANES))
    copies, held = lax.optimization_barrier((copies, templates))
    record = lax.all_to_all(copies, ("tm", "tmpl"), split_axis=0, concat_axis=0, tiled=True)
    record = record.reshape(segs, ROWS, LANES)
    blocks = [held] + [swap(held, "tm", other) for other in range(1, tm)]
    bank = pl.pallas_call(
        functools.partial(bank_kernel, tm),
        out_shape=jax.ShapeDtypeStruct((2, count, ROWS, LANES), f32),
        in_specs=[vmem] * (tm + 1),
        out_specs=vmem,
        scratch_shapes=[pltpu.VMEM((ROWS, count, 2 * LANES), jnp.bfloat16)],
        compiler_params=params,
        cost_estimate=pl.CostEstimate(flops=0, bytes_accessed=2500000, transcendentals=0),
        name="bank",
    )(*blocks, cutoff.reshape(1, count))
    narrow, broad, energy = tables()
    return pl.pallas_call(
        functools.partial(filter_kernel, energy),
        out_shape=jax.ShapeDtypeStruct((own, count), f32),
        in_specs=[vmem] * 4,
        out_specs=vmem,
        scratch_shapes=[pltpu.VMEM((segs * FINE, LANES), f32)],
        compiler_params=params,
        name="matched_filter",
    )(record, bank, jnp.asarray(narrow), jnp.asarray(broad))


def solution(mesh):
    in_specs = (P(("tm", "tmpl")), P(None, "tmpl", "tm"), P("tmpl"))
    out_specs = P("tm", "tmpl")
    return jax.shard_map(
        on_device, mesh=mesh, in_specs=in_specs, out_specs=out_specs, check_vma=False
    )
```

```python
import functools
import math

import jax
import jax.numpy as jnp
import ml_dtypes
import numpy as np
from jax import lax
from jax.experimental import pallas as pl
from jax.experimental.pallas import tpu as pltpu
from jax.sharding import PartitionSpec as P

NFFT = 4096
BINS = 2048
HOP = 2048
LANES = 128
ROWS = HOP // LANES
FINE = 32
GROUP = 8
FLOOR = 1e-6

ROOT_SCALE = {128: 1.66575, 64: 1.66575, 32: 1.6245, 16: 1.6245, 8: 1.6245}


def root_order(index, period):
    return period // math.gcd(int(index), period)


def row_scale(count, period):
    return np.array([ROOT_SCALE.get(root_order(i, period), 1.0) for i in range(count)])


def as_bf16(table):
    return np.asarray(table, np.float32).astype(ml_dtypes.bfloat16)


def two_parts(table):
    high = as_bf16(table)
    low = as_bf16(np.asarray(table, np.float64) - high.astype(np.float64))
    return high, low


def turn(left, right, period):
    angle = 2.0 * np.pi * (np.outer(left, right) % period) / period
    return np.cos(angle), np.sin(angle)


@functools.lru_cache(maxsize=None)
def tables():
    fine, wide, rows = np.arange(FINE), np.arange(LANES), np.arange(ROWS)
    window = 0.5 - 0.5 * np.cos(2.0 * np.pi * np.arange(NFFT) / NFFT)
    cos, sin = turn(fine, fine, FINE)
    first_high, first_low = two_parts(np.tile(np.concatenate([cos, -sin]), (1, GROUP)))
    fwd_cos, fwd_sin = turn(fine, wide, NFFT)
    f_order = np.array([4 * d + g for g in range(4) for d in range(ROWS)])
    cos, sin = turn(wide, f_order, LANES)
    second_high, second_low = two_parts(np.block([[cos, -sin], [sin, cos]]))
    scale_q, scale_c = row_scale(FINE, FINE), row_scale(LANES, LANES)
    cos, sin = turn(fine, rows, FINE)
    cos, sin = np.tile(cos * scale_q[:, None], (1, GROUP)), np.tile(sin * scale_q[:, None], (1, GROUP))
    third = np.block([[cos, -sin], [sin, cos]])
    inv_cos, inv_sin = turn(fine, wide, NFFT)
    undo = 1.0 / (scale_q[:, None] * scale_c[None, :])
    cos, sin = turn(wide, wide, LANES)
    cos, sin = cos * scale_c[:, None], sin * scale_c[:, None]
    fourth = np.block([[cos, sin], [-sin, cos]])
    narrow = np.concatenate(
        [first_high, first_low, as_bf16(third), np.concatenate([second_high, second_low], axis=1), as_bf16(fourth)]
    )
    broad = np.concatenate([window.reshape(FINE, LANES), fwd_cos, fwd_sin, inv_cos * undo, inv_sin * undo])
    return narrow, np.asarray(broad, np.float32), float((window * window).sum())


def dot(left, right):
    return jnp.dot(left, right, preferred_element_type=jnp.float32)


def split(value):
    high = value.astype(jnp.bfloat16)
    return high, (value - high.astype(jnp.float32)).astype(jnp.bfloat16)


def repeat(count, body, carry):
    if count <= 8:
        for step in range(count):
            carry = body(step, carry)
        return carry
    return lax.fori_loop(0, count, body, carry)


def block_diagonal(rows, width):
    lane = lax.broadcasted_iota(jnp.int32, rows.shape, 1)
    owner = lax.rem(lane // width, GROUP)
    return jnp.concatenate(
        [jnp.where(owner == s, rows, jnp.zeros_like(rows)) for s in range(GROUP)], axis=0
    )


def natural(flipped, at, source):
    part = lax.broadcasted_iota(jnp.int32, (ROWS, LANES), 1) // FINE
    result = None
    for g in range(4):
        piece = flipped[at + g * ROWS:at + (g + 1) * ROWS]
        if source is not None and g != source:
            piece = pltpu.roll(piece, ((g - source) % 4) * FINE, 1)
        result = piece if g == 0 else jnp.where(part == g, piece, result)
    return result


def pack_kernel(strain, copies):
    copies[...] = jnp.broadcast_to(strain[...][None], copies.shape)


def bank_kernel(devices, *refs):
    blocks = refs[:devices]
    cutoff, bank, gathered = refs[devices:]
    rank = lax.axis_index("tm")
    _, count, width = blocks[0].shape
    shape = (count, count)
    same = lax.broadcasted_iota(jnp.int32, shape, 0) == lax.broadcasted_iota(jnp.int32, shape, 1)
    column = jnp.sum(jnp.where(same, cutoff[...], 0), axis=1, keepdims=True)
    lane = lax.broadcasted_iota(jnp.int32, (count, LANES), 1)
    for other, block in enumerate(blocks):
        first = (rank ^ other) * (width // LANES)
        for at in range(width // LANES):
            lanes = slice(at * LANES, (at + 1) * LANES)
            keep = lane + (first + at) * LANES < column
            both = [jnp.where(keep, block[i, :, lanes].astype(jnp.float32), 0.0) for i in range(2)]
            gathered[first + at] = jnp.concatenate(both, axis=1).astype(jnp.bfloat16)
    shape = (count * ROWS, count * ROWS)
    to, source = lax.broadcasted_iota(jnp.int32, shape, 0), lax.broadcasted_iota(jnp.int32, shape, 1)
    order = (source == (to % ROWS) * count + to // ROWS).astype(jnp.float32).astype(jnp.bfloat16)
    value = dot(order, gathered[...].reshape(ROWS * count, 2 * LANES))
    bank[0] = value[:, :LANES].reshape(count, ROWS, LANES)
    bank[1] = value[:, LANES:].reshape(count, ROWS, LANES)


def filter_kernel(energy, mine, others, bank, narrow, broad, out, spec, halves):
    core = lax.rem(lax.axis_index("tmpl"), 2)
    halves[:, core] = mine[...]
    halves[:, 1 - core] = others[...]
    segs = 2 * mine.shape[0] * mine.shape[1] // ROWS
    record = halves.reshape(segs, ROWS, LANES)
    own, count = out.shape
    half = GROUP * FINE
    w_low, w_high = broad[:ROWS][None], broad[ROWS:FINE][None]
    fwd_cos, fwd_sin = broad[FINE:2 * FINE][None], broad[2 * FINE:3 * FINE][None]
    inv_cos, inv_sin = broad[3 * FINE:4 * FINE][None], broad[4 * FINE:5 * FINE][None]
    high, low = narrow[:2 * FINE], narrow[2 * FINE:4 * FINE]
    spread = lambda part: jnp.concatenate(
        [block_diagonal(part[:FINE], part.shape[1] // GROUP), block_diagonal(part[FINE:], part.shape[1] // GROUP)]
    )
    first_high = spread(high)
    first = jnp.concatenate([first_high, first_high, spread(low)], axis=1)
    third_rows = narrow[4 * FINE:6 * FINE]
    third = jnp.concatenate([block_diagonal(third_rows[:FINE], ROWS), block_diagonal(third_rows[FINE:], ROWS)])
    second = slice(6 * FINE, 6 * FINE + 2 * LANES)
    fourth = slice(6 * FINE + 2 * LANES, 6 * FINE + 4 * LANES)

    def frames(start, last):
        here = record[pl.ds(start, GROUP)]
        if last:
            after = jnp.concatenate([record[pl.ds(start + 1, GROUP - 1)], record[pl.ds(0, 1)]], axis=0)
        else:
            after = record[pl.ds(start + 1, GROUP)]
        both = jnp.concatenate([here * w_low, after * w_high], axis=1)
        return both.reshape(half, LANES)

    def forward(start, power, last):
        pair = jnp.concatenate([frames(start, False), frames(start + GROUP, last)], axis=1)
        high, low = split(pair)
        step = dot(first, jnp.concatenate([high, low, high], axis=0))
        for h in range(2):
            re = step[:half, h * LANES:(h + 1) * LANES].reshape(GROUP, FINE, LANES)
            im = step[half:, h * LANES:(h + 1) * LANES].reshape(GROUP, FINE, LANES)
            turned = jnp.concatenate([re * fwd_cos + im * fwd_sin, im * fwd_cos - re * fwd_sin], axis=2)
            high, low = split(turned.reshape(half, 2 * LANES))
            both = dot(jnp.concatenate([high, low], axis=1), jnp.concatenate([narrow[second]] * 2, axis=0))
            value = both[:, :LANES] + both[:, LANES:]
            spec[pl.ds((start + h * GROUP) * FINE, half)] = value
            power = power + jnp.sum((value * value).reshape(GROUP, FINE, LANES), axis=0)
        return power

    power = jnp.zeros((FINE, LANES), jnp.float32)
    pairs = segs // (2 * GROUP)
    power = repeat(pairs - 1, lambda i, p: forward(i * 2 * GROUP, p, False), power)
    power = forward((pairs - 1) * 2 * GROUP, power, True)
    power = power + pltpu.roll(power, LANES // 2, 1)
    density = power / (segs * energy) + FLOOR
    inverse_density = natural((1.0 / jnp.concatenate([density] * 4, axis=0)).T, 0, None)

    place = lax.axis_index("tm") * own
    column = lax.broadcasted_iota(jnp.int32, (GROUP, LANES), 1)

    def block(number, carry):
        at = pl.multiple_of((place + number * GROUP) * FINE, half)
        white = spec[pl.ds(at, half)].reshape(GROUP, FINE, LANES) / density[None]
        white = white.astype(jnp.bfloat16).astype(jnp.float32).reshape(2, 4 * FINE, LANES)
        re_parts, im_parts = [], []
        for side in range(2):
            flipped = white[side].T
            for s in range(4):
                re_parts.append(natural(flipped, 0, s))
                im_parts.append(natural(flipped, LANES // 2, s))
        white_re, white_im = jnp.stack(re_parts), jnp.stack(im_parts)

        def pair_of(step, result):
            sides, norms = [], []
            for side in range(2):
                m = 2 * step + side
                h_re, h_im = bank[0, m], bank[1, m]
                norms.append(jnp.sum((h_re * h_re + h_im * h_im) * inverse_density, keepdims=True))
                c_re = h_re[None] * white_re + h_im[None] * white_im
                c_im = h_re[None] * white_im - h_im[None] * white_re
                both = jnp.concatenate([c_re, c_im], axis=0).reshape(2 * GROUP * ROWS, LANES)
                sides.append(both.astype(jnp.bfloat16))
            section = dot(third, jnp.concatenate(sides, axis=1))
            for side in range(2):
                re = section[:half, side * LANES:(side + 1) * LANES].reshape(GROUP, FINE, LANES)
                im = section[half:, side * LANES:(side + 1) * LANES].reshape(GROUP, FINE, LANES)
                turned = jnp.concatenate([re * inv_cos - im * inv_sin, re * inv_sin + im * inv_cos], axis=2)
                wave = dot(turned.reshape(half, 2 * LANES).astype(jnp.bfloat16), narrow[fourth])
                square = wave[:, :LANES] * wave[:, :LANES] + wave[:, LANES:] * wave[:, LANES:]
                top = jnp.max(jnp.max(square.reshape(GROUP, FINE, LANES), axis=1), axis=1, keepdims=True)
                value = jnp.sqrt(top) / (jnp.sqrt(norms[side]) * math.sqrt(energy))
                result = jnp.where(column == 2 * step + side, value, result)
            return result

        result = repeat(count // 2, pair_of, jnp.zeros((GROUP, LANES), jnp.float32))
        out[pl.ds(number * GROUP, GROUP)] = result[:, :count]
        return carry

    repeat(own // GROUP, block, 0)


def swap(array, axis, bits):
    return lax.ppermute(array, axis, [(i, i ^ bits) for i in range(lax.axis_size(axis))])


def on_device(strain, templates, cutoff):
    tm, devices = lax.axis_size("tm"), lax.axis_size("tm") * lax.axis_size("tmpl")
    size = strain.shape[0] // HOP
    segs = devices * size
    own = segs // tm
    count = templates.shape[1]
    vmem = pl.BlockSpec(memory_space=pltpu.VMEM)
    params = pltpu.CompilerParams(vmem_limit_bytes=40 * 1024 * 1024)
    f32 = jnp.float32

    copies = pl.pallas_call(
        pack_kernel,
        out_shape=jax.ShapeDtypeStruct((devices // 2, size * ROWS, LANES), f32),
        in_specs=[vmem],
        out_specs=vmem,
        compiler_params=params,
        name="pack",
    )(strain.reshape(size * ROWS, LANES))
    copies, held = lax.optimization_barrier((copies, templates))
    copies = copies.reshape(devices, size * ROWS // 2, LANES)
    mine = lax.all_to_all(copies, ("tm", "tmpl"), split_axis=0, concat_axis=0, tiled=True)
    blocks = [swap(held, "tm", other) for other in range(1, tm)]
    mine, *blocks = lax.optimization_barrier((mine, *blocks))
    others = swap(mine, "tmpl", 1)
    blocks = [held] + blocks
    bank = pl.pallas_call(
        functools.partial(bank_kernel, tm),
        out_shape=jax.ShapeDtypeStruct((2, count, ROWS, LANES), f32),
        in_specs=[vmem] * (tm + 1),
        out_specs=vmem,
        scratch_shapes=[pltpu.VMEM((ROWS, count, 2 * LANES), jnp.bfloat16)],
        compiler_params=params,
        cost_estimate=pl.CostEstimate(flops=0, bytes_accessed=2500000, transcendentals=0),
        name="bank",
    )(*blocks, cutoff.reshape(1, count))
    narrow, broad, energy = tables()
    return pl.pallas_call(
        functools.partial(filter_kernel, energy),
        out_shape=jax.ShapeDtypeStruct((own, count), f32),
        in_specs=[vmem] * 5,
        out_specs=vmem,
        scratch_shapes=[
            pltpu.VMEM((segs * FINE, LANES), f32),
            pltpu.VMEM((devices, 2, size * ROWS // 2, LANES), f32),
        ],
        compiler_params=params,
        name="matched_filter",
    )(mine, others, bank, jnp.asarray(narrow), jnp.asarray(broad))


def solution(mesh):
    in_specs = (P(("tm", "tmpl")), P(None, "tmpl", "tm"), P("tmpl"))
    out_specs = P("tm", "tmpl")
    return jax.shard_map(
        on_device, mesh=mesh, in_specs=in_specs, out_specs=out_specs, check_vma=False
    )
```

```python
import functools
import math

import jax
import jax.numpy as jnp
import ml_dtypes
import numpy as np
from jax import lax
from jax.experimental import pallas as pl
from jax.experimental.pallas import tpu as pltpu
from jax.sharding import PartitionSpec as P

NFFT = 4096
BINS = 2048
HOP = 2048
LANES = 128
ROWS = HOP // LANES
FINE = 32
GROUP = 8
FLOOR = 1e-6

ROOT_SCALE = {128: 1.66575, 64: 1.66575, 32: 1.6245, 16: 1.6245, 8: 1.6245}


def root_order(index, period):
    return period // math.gcd(int(index), period)


def row_scale(count, period):
    return np.array([ROOT_SCALE.get(root_order(i, period), 1.0) for i in range(count)])


def as_bf16(table):
    return np.asarray(table, np.float32).astype(ml_dtypes.bfloat16)


def two_parts(table):
    high = as_bf16(table)
    low = as_bf16(np.asarray(table, np.float64) - high.astype(np.float64))
    return high, low


def turn(left, right, period):
    angle = 2.0 * np.pi * (np.outer(left, right) % period) / period
    return np.cos(angle), np.sin(angle)


@functools.lru_cache(maxsize=None)
def tables():
    fine, wide, rows = np.arange(FINE), np.arange(LANES), np.arange(ROWS)
    window = 0.5 - 0.5 * np.cos(2.0 * np.pi * np.arange(NFFT) / NFFT)
    cos, sin = turn(fine, fine, FINE)
    first_high, first_low = two_parts(np.tile(np.concatenate([cos, -sin]), (1, GROUP)))
    fwd_cos, fwd_sin = turn(fine, wide, NFFT)
    f_order = np.array([4 * d + g for g in range(4) for d in range(ROWS)])
    cos, sin = turn(wide, f_order, LANES)
    second_high, second_low = two_parts(np.block([[cos, -sin], [sin, cos]]))
    scale_q, scale_c = row_scale(FINE, FINE), row_scale(LANES, LANES)
    cos, sin = turn(fine, rows, FINE)
    cos, sin = np.tile(cos * scale_q[:, None], (1, GROUP)), np.tile(sin * scale_q[:, None], (1, GROUP))
    third = np.block([[cos, -sin], [sin, cos]])
    inv_cos, inv_sin = turn(fine, wide, NFFT)
    undo = 1.0 / (scale_q[:, None] * scale_c[None, :])
    cos, sin = turn(wide, wide, LANES)
    cos, sin = cos * scale_c[:, None], sin * scale_c[:, None]
    fourth = np.block([[cos, sin], [-sin, cos]])
    narrow = np.concatenate(
        [first_high, first_low, as_bf16(third), np.concatenate([second_high, second_low], axis=1), as_bf16(fourth)]
    )
    broad = np.concatenate([window.reshape(FINE, LANES), fwd_cos, fwd_sin, inv_cos * undo, inv_sin * undo])
    return narrow, np.asarray(broad, np.float32), float((window * window).sum())


def dot(left, right):
    return jnp.dot(left, right, preferred_element_type=jnp.float32)


def split(value):
    high = value.astype(jnp.bfloat16)
    return high, (value - high.astype(jnp.float32)).astype(jnp.bfloat16)


def repeat(count, body, carry):
    if count <= 8:
        for step in range(count):
            carry = body(step, carry)
        return carry
    return lax.fori_loop(0, count, body, carry)


def block_diagonal(rows, width):
    lane = lax.broadcasted_iota(jnp.int32, rows.shape, 1)
    owner = lax.rem(lane // width, GROUP)
    return jnp.concatenate(
        [jnp.where(owner == s, rows, jnp.zeros_like(rows)) for s in range(GROUP)], axis=0
    )


def natural(flipped, at, source):
    part = lax.broadcasted_iota(jnp.int32, (ROWS, LANES), 1) // FINE
    result = None
    for g in range(4):
        piece = flipped[at + g * ROWS:at + (g + 1) * ROWS]
        if source is not None and g != source:
            piece = pltpu.roll(piece, ((g - source) % 4) * FINE, 1)
        result = piece if g == 0 else jnp.where(part == g, piece, result)
    return result


def bank_kernel(devices, *refs):
    blocks = refs[:devices]
    cutoff, bank, gathered = refs[devices:]
    rank = lax.axis_index("tm")
    _, count, width = blocks[0].shape
    shape = (count, count)
    same = lax.broadcasted_iota(jnp.int32, shape, 0) == lax.broadcasted_iota(jnp.int32, shape, 1)
    column = jnp.sum(jnp.where(same, cutoff[...], 0), axis=1, keepdims=True)
    lane = lax.broadcasted_iota(jnp.int32, (count, LANES), 1)
    for other, block in enumerate(blocks):
        first = (rank ^ other) * (width // LANES)
        for at in range(width // LANES):
            lanes = slice(at * LANES, (at + 1) * LANES)
            keep = lane + (first + at) * LANES < column
            both = [jnp.where(keep, block[i, :, lanes].astype(jnp.float32), 0.0) for i in range(2)]
            gathered[first + at] = jnp.concatenate(both, axis=1).astype(jnp.bfloat16)
    shape = (count * ROWS, count * ROWS)
    to, source = lax.broadcasted_iota(jnp.int32, shape, 0), lax.broadcasted_iota(jnp.int32, shape, 1)
    order = (source == (to % ROWS) * count + to // ROWS).astype(jnp.float32).astype(jnp.bfloat16)
    value = dot(order, gathered[...].reshape(ROWS * count, 2 * LANES))
    bank[0] = value[:, :LANES].reshape(count, ROWS, LANES)
    bank[1] = value[:, LANES:].reshape(count, ROWS, LANES)


def filter_kernel(energy, mine, others, bank, narrow, broad, out, spec, halves):
    core = lax.rem(lax.axis_index("tmpl"), 2)
    halves[:, core] = mine[...]
    halves[:, 1 - core] = others[...]
    segs = 2 * mine.shape[0] * mine.shape[1] // ROWS
    record = halves.reshape(segs, ROWS, LANES)
    own, count = out.shape
    half = GROUP * FINE
    w_low, w_high = broad[:ROWS][None], broad[ROWS:FINE][None]
    fwd_cos, fwd_sin = broad[FINE:2 * FINE][None], broad[2 * FINE:3 * FINE][None]
    inv_cos, inv_sin = broad[3 * FINE:4 * FINE][None], broad[4 * FINE:5 * FINE][None]
    high, low = narrow[:2 * FINE], narrow[2 * FINE:4 * FINE]
    spread = lambda part: jnp.concatenate(
        [block_diagonal(part[:FINE], part.shape[1] // GROUP), block_diagonal(part[FINE:], part.shape[1] // GROUP)]
    )
    first_high = spread(high)
    first = jnp.concatenate([first_high, first_high, spread(low)], axis=1)
    third_rows = narrow[4 * FINE:6 * FINE]
    third = jnp.concatenate([block_diagonal(third_rows[:FINE], ROWS), block_diagonal(third_rows[FINE:], ROWS)])
    second = slice(6 * FINE, 6 * FINE + 2 * LANES)
    fourth = slice(6 * FINE + 2 * LANES, 6 * FINE + 4 * LANES)

    def frames(start, last):
        here = record[pl.ds(start, GROUP)]
        if last:
            after = jnp.concatenate([record[pl.ds(start + 1, GROUP - 1)], record[pl.ds(0, 1)]], axis=0)
        else:
            after = record[pl.ds(start + 1, GROUP)]
        both = jnp.concatenate([here * w_low, after * w_high], axis=1)
        return both.reshape(half, LANES)

    def first_product(start, last):
        pair = jnp.concatenate([frames(start, False), frames(start + GROUP, last)], axis=1)
        high, low = split(pair)
        return dot(first, jnp.concatenate([high, low, high], axis=0))

    def second_product(step, start, power):
        for h in range(2):
            re = step[:half, h * LANES:(h + 1) * LANES].reshape(GROUP, FINE, LANES)
            im = step[half:, h * LANES:(h + 1) * LANES].reshape(GROUP, FINE, LANES)
            turned = jnp.concatenate([re * fwd_cos + im * fwd_sin, im * fwd_cos - re * fwd_sin], axis=2)
            high, low = split(turned.reshape(half, 2 * LANES))
            both = dot(jnp.concatenate([high, low], axis=1), jnp.concatenate([narrow[second]] * 2, axis=0))
            value = both[:, :LANES] + both[:, LANES:]
            spec[pl.ds((start + h * GROUP) * FINE, half)] = value
            power = power + jnp.sum((value * value).reshape(GROUP, FINE, LANES), axis=0)
        return power

    power = jnp.zeros((FINE, LANES), jnp.float32)
    pairs = segs // (2 * GROUP)
    stride = 2 * GROUP
    if pairs <= 4:
        steps = [first_product(i * stride, i == pairs - 1) for i in range(pairs)]
        for i, step in enumerate(steps):
            power = second_product(step, i * stride, power)
    else:
        power = lax.fori_loop(
            0, pairs - 1, lambda i, p: second_product(first_product(i * stride, False), i * stride, p), power
        )
        start = (pairs - 1) * stride
        power = second_product(first_product(start, True), start, power)
    power = power + pltpu.roll(power, LANES // 2, 1)
    density = power / (segs * energy) + FLOOR
    inverse_density = natural((1.0 / jnp.concatenate([density] * 4, axis=0)).T, 0, None)

    place = lax.axis_index("tm") * own
    column = lax.broadcasted_iota(jnp.int32, (GROUP, LANES), 1)

    def block(number, carry):
        at = pl.multiple_of((place + number * GROUP) * FINE, half)
        white = spec[pl.ds(at, half)].reshape(GROUP, FINE, LANES) / density[None]
        white = white.astype(jnp.bfloat16).astype(jnp.float32).reshape(2, 4 * FINE, LANES)
        re_parts, im_parts = [], []
        for side in range(2):
            flipped = white[side].T
            for s in range(4):
                re_parts.append(natural(flipped, 0, s))
                im_parts.append(natural(flipped, LANES // 2, s))
        white_re, white_im = jnp.stack(re_parts), jnp.stack(im_parts)

        def section_of(step):
            sides, norms = [], []
            for m in (2 * step, 2 * step + 1):
                h_re, h_im = bank[0, m], bank[1, m]
                norms.append(jnp.sum((h_re * h_re + h_im * h_im) * inverse_density, keepdims=True))
                c_re = h_re[None] * white_re + h_im[None] * white_im
                c_im = h_re[None] * white_im - h_im[None] * white_re
                both = jnp.concatenate([c_re, c_im], axis=0).reshape(2 * GROUP * ROWS, LANES)
                sides.append(both.astype(jnp.bfloat16))
            return dot(third, jnp.concatenate(sides, axis=1)), norms

        def peaks_of(step, section, norms, result):
            for side in range(2):
                re = section[:half, side * LANES:(side + 1) * LANES].reshape(GROUP, FINE, LANES)
                im = section[half:, side * LANES:(side + 1) * LANES].reshape(GROUP, FINE, LANES)
                turned = jnp.concatenate([re * inv_cos - im * inv_sin, re * inv_sin + im * inv_cos], axis=2)
                wave = dot(turned.reshape(half, 2 * LANES).astype(jnp.bfloat16), narrow[fourth])
                square = wave[:, :LANES] * wave[:, :LANES] + wave[:, LANES:] * wave[:, LANES:]
                top = jnp.max(jnp.max(square.reshape(GROUP, FINE, LANES), axis=1), axis=1, keepdims=True)
                value = jnp.sqrt(top) / (jnp.sqrt(norms[side]) * math.sqrt(energy))
                result = jnp.where(column == 2 * step + side, value, result)
            return result

        result = jnp.zeros((GROUP, LANES), jnp.float32)
        ready = section_of(0)
        for step in range(count // 2):
            current = ready
            if step + 1 < count // 2:
                ready = section_of(step + 1)
            result = peaks_of(step, *current, result)
        out[pl.ds(number * GROUP, GROUP)] = result[:, :count]
        return carry

    repeat(own // GROUP, block, 0)


def swap(array, axis, bits):
    return lax.ppermute(array, axis, [(i, i ^ bits) for i in range(lax.axis_size(axis))])


def on_device(strain, templates, cutoff):
    tm, devices = lax.axis_size("tm"), lax.axis_size("tm") * lax.axis_size("tmpl")
    size = strain.shape[0] // HOP
    segs = devices * size
    own = segs // tm
    count = templates.shape[1]
    vmem = pl.BlockSpec(memory_space=pltpu.VMEM)
    params = pltpu.CompilerParams(vmem_limit_bytes=40 * 1024 * 1024)
    f32 = jnp.float32

    chunk = strain.reshape(1, size * ROWS, LANES)
    copies = jnp.broadcast_to(chunk, (devices // 2, size * ROWS, LANES))
    copies, held = lax.optimization_barrier((copies, templates))
    copies = copies.reshape(devices, size * ROWS // 2, LANES)
    mine = lax.all_to_all(copies, ("tm", "tmpl"), split_axis=0, concat_axis=0, tiled=True)
    blocks = [swap(held, "tm", other) for other in range(1, tm)]
    mine, *blocks = lax.optimization_barrier((mine, *blocks))
    others = swap(mine, "tmpl", 1)
    blocks = [held] + blocks
    bank = pl.pallas_call(
        functools.partial(bank_kernel, tm),
        out_shape=jax.ShapeDtypeStruct((2, count, ROWS, LANES), f32),
        in_specs=[vmem] * (tm + 1),
        out_specs=vmem,
        scratch_shapes=[pltpu.VMEM((ROWS, count, 2 * LANES), jnp.bfloat16)],
        compiler_params=params,
        cost_estimate=pl.CostEstimate(flops=0, bytes_accessed=2500000, transcendentals=0),
        name="bank",
    )(*blocks, cutoff.reshape(1, count))
    narrow, broad, energy = tables()
    return pl.pallas_call(
        functools.partial(filter_kernel, energy),
        out_shape=jax.ShapeDtypeStruct((own, count), f32),
        in_specs=[vmem] * 5,
        out_specs=vmem,
        scratch_shapes=[
            pltpu.VMEM((segs * FINE, LANES), f32),
            pltpu.VMEM((devices, 2, size * ROWS // 2, LANES), f32),
        ],
        compiler_params=params,
        name="matched_filter",
    )(mine, others, bank, jnp.asarray(narrow), jnp.asarray(broad))


def solution(mesh):
    in_specs = (P(("tm", "tmpl")), P(None, "tmpl", "tm"), P("tmpl"))
    out_specs = P("tm", "tmpl")
    return jax.shard_map(
        on_device, mesh=mesh, in_specs=in_specs, out_specs=out_specs, check_vma=False
    )
```

```python
import functools
import math

import jax
import jax.numpy as jnp
import ml_dtypes
import numpy as np
from jax import lax
from jax.experimental import pallas as pl
from jax.experimental.pallas import tpu as pltpu
from jax.sharding import PartitionSpec as P

NFFT = 4096
BINS = 2048
HOP = 2048
LANES = 128
ROWS = HOP // LANES
FINE = 32
GROUP = 8
FLOOR = 1e-6

ROOT_SCALE = {128: 1.66575, 64: 1.66575, 32: 1.6245, 16: 1.6245, 8: 1.6245}


def root_order(index, period):
    return period // math.gcd(int(index), period)


def row_scale(count, period):
    return np.array([ROOT_SCALE.get(root_order(i, period), 1.0) for i in range(count)])


def as_bf16(table):
    return np.asarray(table, np.float32).astype(ml_dtypes.bfloat16)


def two_parts(table):
    high = as_bf16(table)
    low = as_bf16(np.asarray(table, np.float64) - high.astype(np.float64))
    return high, low


def turn(left, right, period):
    angle = 2.0 * np.pi * (np.outer(left, right) % period) / period
    return np.cos(angle), np.sin(angle)


@functools.lru_cache(maxsize=None)
def tables():
    fine, wide, rows = np.arange(FINE), np.arange(LANES), np.arange(ROWS)
    window = 0.5 - 0.5 * np.cos(2.0 * np.pi * np.arange(NFFT) / NFFT)
    cos, sin = turn(fine, fine, FINE)
    first_high, first_low = two_parts(np.tile(np.concatenate([cos, -sin]), (1, GROUP)))
    fwd_cos, fwd_sin = turn(fine, wide, NFFT)
    f_order = np.array([4 * d + g for g in range(4) for d in range(ROWS)])
    cos, sin = turn(wide, f_order, LANES)
    second_high, second_low = two_parts(np.block([[cos, -sin], [sin, cos]]))
    scale_q, scale_c = row_scale(FINE, FINE), row_scale(LANES, LANES)
    cos, sin = turn(fine, rows, FINE)
    cos, sin = np.tile(cos * scale_q[:, None], (1, GROUP)), np.tile(sin * scale_q[:, None], (1, GROUP))
    third = np.block([[cos, -sin], [sin, cos]])
    inv_cos, inv_sin = turn(fine, wide, NFFT)
    undo = 1.0 / (scale_q[:, None] * scale_c[None, :])
    cos, sin = turn(wide, wide, LANES)
    cos, sin = cos * scale_c[:, None], sin * scale_c[:, None]
    fourth = np.block([[cos, sin], [-sin, cos]])
    narrow = np.concatenate(
        [first_high, first_low, as_bf16(third), np.concatenate([second_high, second_low], axis=1), as_bf16(fourth)]
    )
    broad = np.concatenate([window.reshape(FINE, LANES), fwd_cos, fwd_sin, inv_cos * undo, inv_sin * undo])
    return narrow, np.asarray(broad, np.float32), float((window * window).sum())


def dot(left, right):
    return jnp.dot(left, right, preferred_element_type=jnp.float32)


def split(value):
    high = value.astype(jnp.bfloat16)
    return high, (value - high.astype(jnp.float32)).astype(jnp.bfloat16)


def repeat(count, body, carry):
    if count <= 8:
        for step in range(count):
            carry = body(step, carry)
        return carry
    return lax.fori_loop(0, count, body, carry)


def block_diagonal(rows, width):
    lane = lax.broadcasted_iota(jnp.int32, rows.shape, 1)
    owner = lax.rem(lane // width, GROUP)
    return jnp.concatenate(
        [jnp.where(owner == s, rows, jnp.zeros_like(rows)) for s in range(GROUP)], axis=0
    )


def natural(flipped, at, source):
    part = lax.broadcasted_iota(jnp.int32, (ROWS, LANES), 1) // FINE
    result = None
    for g in range(4):
        piece = flipped[at + g * ROWS:at + (g + 1) * ROWS]
        if source is not None and g != source:
            piece = pltpu.roll(piece, ((g - source) % 4) * FINE, 1)
        result = piece if g == 0 else jnp.where(part == g, piece, result)
    return result


def bank_kernel(devices, *refs):
    blocks = refs[:devices]
    cutoff, bank, gathered = refs[devices:]
    rank = lax.axis_index("tm")
    _, count, width = blocks[0].shape
    shape = (count, count)
    same = lax.broadcasted_iota(jnp.int32, shape, 0) == lax.broadcasted_iota(jnp.int32, shape, 1)
    column = jnp.sum(jnp.where(same, cutoff[...], 0), axis=1, keepdims=True)
    lane = lax.broadcasted_iota(jnp.int32, (count, LANES), 1)
    for other, block in enumerate(blocks):
        first = (rank ^ other) * (width // LANES)
        for at in range(width // LANES):
            lanes = slice(at * LANES, (at + 1) * LANES)
            keep = lane + (first + at) * LANES < column
            both = [jnp.where(keep, block[i, :, lanes].astype(jnp.float32), 0.0) for i in range(2)]
            gathered[first + at] = jnp.concatenate(both, axis=1).astype(jnp.bfloat16)
    shape = (count * ROWS, count * ROWS)
    to, source = lax.broadcasted_iota(jnp.int32, shape, 0), lax.broadcasted_iota(jnp.int32, shape, 1)
    order = (source == (to % ROWS) * count + to // ROWS).astype(jnp.float32).astype(jnp.bfloat16)
    value = dot(order, gathered[...].reshape(ROWS * count, 2 * LANES))
    bank[0] = value[:, :LANES].reshape(count, ROWS, LANES)
    bank[1] = value[:, LANES:].reshape(count, ROWS, LANES)


def filter_kernel(energy, mine, others, bank, narrow, broad, out, spec, halves):
    core = lax.rem(lax.axis_index("tmpl"), 2)
    halves[:, core] = mine[...]
    halves[:, 1 - core] = others[...]
    segs = 2 * mine.shape[0] * mine.shape[1] // ROWS
    record = halves.reshape(segs, ROWS, LANES)
    own, count = out.shape
    half = GROUP * FINE
    w_low, w_high = broad[:ROWS][None], broad[ROWS:FINE][None]
    fwd_cos, fwd_sin = broad[FINE:2 * FINE][None], broad[2 * FINE:3 * FINE][None]
    inv_cos, inv_sin = broad[3 * FINE:4 * FINE][None], broad[4 * FINE:5 * FINE][None]
    high, low = narrow[:2 * FINE], narrow[2 * FINE:4 * FINE]
    spread = lambda part: jnp.concatenate(
        [block_diagonal(part[:FINE], part.shape[1] // GROUP), block_diagonal(part[FINE:], part.shape[1] // GROUP)]
    )
    first_high = spread(high)
    first = jnp.concatenate([first_high, first_high, spread(low)], axis=1)
    third_rows = narrow[4 * FINE:6 * FINE]
    third = jnp.concatenate([block_diagonal(third_rows[:FINE], ROWS), block_diagonal(third_rows[FINE:], ROWS)])
    second = slice(6 * FINE, 6 * FINE + 2 * LANES)
    fourth = slice(6 * FINE + 2 * LANES, 6 * FINE + 4 * LANES)

    def frames(start, last):
        here = record[pl.ds(start, GROUP)]
        if last:
            after = jnp.concatenate([record[pl.ds(start + 1, GROUP - 1)], record[pl.ds(0, 1)]], axis=0)
        else:
            after = record[pl.ds(start + 1, GROUP)]
        both = jnp.concatenate([here * w_low, after * w_high], axis=1)
        return both.reshape(half, LANES)

    def first_product(start, last):
        pair = jnp.concatenate([frames(start, False), frames(start + GROUP, last)], axis=1)
        high, low = split(pair)
        return dot(first, jnp.concatenate([high, low, high], axis=0))

    def second_product(step, h):
        re = step[:half, h * LANES:(h + 1) * LANES].reshape(GROUP, FINE, LANES)
        im = step[half:, h * LANES:(h + 1) * LANES].reshape(GROUP, FINE, LANES)
        turned = jnp.concatenate([re * fwd_cos + im * fwd_sin, im * fwd_cos - re * fwd_sin], axis=2)
        high, low = split(turned.reshape(half, 2 * LANES))
        return dot(jnp.concatenate([high, low], axis=1), jnp.concatenate([narrow[second]] * 2, axis=0))

    def add_power(both, at, power):
        value = both[:, :LANES] + both[:, LANES:]
        spec[pl.ds(at * FINE, half)] = value
        return power + jnp.sum((value * value).reshape(GROUP, FINE, LANES), axis=0)

    def whole(start, last, power):
        step = first_product(start, last)
        for h in range(2):
            power = add_power(second_product(step, h), start + h * GROUP, power)
        return power

    power = jnp.zeros((FINE, LANES), jnp.float32)
    pairs = segs // (2 * GROUP)
    stride = 2 * GROUP
    if pairs <= 4:
        steps = [first_product(i * stride, i == pairs - 1) for i in range(pairs)]
        waiting = None
        for i, step in enumerate(steps):
            for h in range(2):
                both = second_product(step, h)
                if waiting is not None:
                    power = add_power(*waiting, power)
                waiting = (both, i * stride + h * GROUP)
        power = add_power(*waiting, power)
    else:
        power = lax.fori_loop(0, pairs - 1, lambda i, p: whole(i * stride, False, p), power)
        power = whole((pairs - 1) * stride, True, power)
    power = power + pltpu.roll(power, LANES // 2, 1)
    density = power / (segs * energy) + FLOOR
    inverse_density = natural((1.0 / jnp.concatenate([density] * 4, axis=0)).T, 0, None)

    place = lax.axis_index("tm") * own
    column = lax.broadcasted_iota(jnp.int32, (GROUP, LANES), 1)

    def block(number, carry):
        at = pl.multiple_of((place + number * GROUP) * FINE, half)
        white = spec[pl.ds(at, half)].reshape(GROUP, FINE, LANES) / density[None]
        white = white.astype(jnp.bfloat16).astype(jnp.float32).reshape(2, 4 * FINE, LANES)
        re_parts, im_parts = [], []
        for side in range(2):
            flipped = white[side].T
            for s in range(4):
                re_parts.append(natural(flipped, 0, s))
                im_parts.append(natural(flipped, LANES // 2, s))
        white_re, white_im = jnp.stack(re_parts), jnp.stack(im_parts)

        def section_of(step):
            sides, norms = [], []
            for m in (2 * step, 2 * step + 1):
                h_re, h_im = bank[0, m], bank[1, m]
                norms.append(jnp.sum((h_re * h_re + h_im * h_im) * inverse_density, keepdims=True))
                c_re = h_re[None] * white_re + h_im[None] * white_im
                c_im = h_re[None] * white_im - h_im[None] * white_re
                both = jnp.concatenate([c_re, c_im], axis=0).reshape(2 * GROUP * ROWS, LANES)
                sides.append(both.astype(jnp.bfloat16))
            return dot(third, jnp.concatenate(sides, axis=1)), norms

        def wave_of(section, side):
            re = section[:half, side * LANES:(side + 1) * LANES].reshape(GROUP, FINE, LANES)
            im = section[half:, side * LANES:(side + 1) * LANES].reshape(GROUP, FINE, LANES)
            turned = jnp.concatenate([re * inv_cos - im * inv_sin, re * inv_sin + im * inv_cos], axis=2)
            return dot(turned.reshape(half, 2 * LANES).astype(jnp.bfloat16), narrow[fourth])

        def peak_of(m, wave, norm, result):
            square = wave[:, :LANES] * wave[:, :LANES] + wave[:, LANES:] * wave[:, LANES:]
            top = jnp.max(jnp.max(square.reshape(GROUP, FINE, LANES), axis=1), axis=1, keepdims=True)
            value = jnp.sqrt(top) / (jnp.sqrt(norm) * math.sqrt(energy))
            return jnp.where(column == m, value, result)

        result = jnp.zeros((GROUP, LANES), jnp.float32)
        ready, waiting = section_of(0), None
        for step in range(count // 2):
            section, norms = ready
            if step + 1 < count // 2:
                ready = section_of(step + 1)
            for side in range(2):
                wave = wave_of(section, side)
                if waiting is not None:
                    result = peak_of(*waiting, result)
                waiting = (2 * step + side, wave, norms[side])
        result = peak_of(*waiting, result)
        out[pl.ds(number * GROUP, GROUP)] = result[:, :count]
        return carry

    repeat(own // GROUP, block, 0)


def swap(array, axis, bits):
    return lax.ppermute(array, axis, [(i, i ^ bits) for i in range(lax.axis_size(axis))])


def on_device(strain, templates, cutoff):
    tm, devices = lax.axis_size("tm"), lax.axis_size("tm") * lax.axis_size("tmpl")
    size = strain.shape[0] // HOP
    segs = devices * size
    own = segs // tm
    count = templates.shape[1]
    vmem = pl.BlockSpec(memory_space=pltpu.VMEM)
    params = pltpu.CompilerParams(vmem_limit_bytes=40 * 1024 * 1024)
    f32 = jnp.float32

    chunk = strain.reshape(1, size * ROWS, LANES)
    copies = jnp.broadcast_to(chunk, (devices // 2, size * ROWS, LANES))
    copies, held = lax.optimization_barrier((copies, templates))
    copies = copies.reshape(devices, size * ROWS // 2, LANES)
    mine = lax.all_to_all(copies, ("tm", "tmpl"), split_axis=0, concat_axis=0, tiled=True)
    blocks = [swap(held, "tm", other) for other in range(1, tm)]
    mine, *blocks = lax.optimization_barrier((mine, *blocks))
    others = swap(mine, "tmpl", 1)
    blocks = [held] + blocks
    bank = pl.pallas_call(
        functools.partial(bank_kernel, tm),
        out_shape=jax.ShapeDtypeStruct((2, count, ROWS, LANES), f32),
        in_specs=[vmem] * (tm + 1),
        out_specs=vmem,
        scratch_shapes=[pltpu.VMEM((ROWS, count, 2 * LANES), jnp.bfloat16)],
        compiler_params=params,
        cost_estimate=pl.CostEstimate(flops=0, bytes_accessed=2500000, transcendentals=0),
        name="bank",
    )(*blocks, cutoff.reshape(1, count))
    narrow, broad, energy = tables()
    return pl.pallas_call(
        functools.partial(filter_kernel, energy),
        out_shape=jax.ShapeDtypeStruct((own, count), f32),
        in_specs=[vmem] * 5,
        out_specs=vmem,
        scratch_shapes=[
            pltpu.VMEM((segs * FINE, LANES), f32),
            pltpu.VMEM((devices, 2, size * ROWS // 2, LANES), f32),
        ],
        compiler_params=params,
        name="matched_filter",
    )(mine, others, bank, jnp.asarray(narrow), jnp.asarray(broad))


def solution(mesh):
    in_specs = (P(("tm", "tmpl")), P(None, "tmpl", "tm"), P("tmpl"))
    out_specs = P("tm", "tmpl")
    return jax.shard_map(
        on_device, mesh=mesh, in_specs=in_specs, out_specs=out_specs, check_vma=False
    )
```

```python
import functools
import math

import jax
import jax.numpy as jnp
import ml_dtypes
import numpy as np
from jax import lax
from jax.experimental import pallas as pl
from jax.experimental.pallas import tpu as pltpu
from jax.sharding import PartitionSpec as P

NFFT = 4096
BINS = 2048
HOP = 2048
LANES = 128
ROWS = HOP // LANES
FINE = 32
GROUP = 8
FLOOR = 1e-6

ROOT_SCALE = {128: 1.66575, 64: 1.66575, 32: 1.6245, 16: 1.6245, 8: 1.6245}


def root_order(index, period):
    return period // math.gcd(int(index), period)


def row_scale(count, period):
    return np.array([ROOT_SCALE.get(root_order(i, period), 1.0) for i in range(count)])


def as_bf16(table):
    return np.asarray(table, np.float32).astype(ml_dtypes.bfloat16)


def two_parts(table):
    high = as_bf16(table)
    low = as_bf16(np.asarray(table, np.float64) - high.astype(np.float64))
    return high, low


def turn(left, right, period):
    angle = 2.0 * np.pi * (np.outer(left, right) % period) / period
    return np.cos(angle), np.sin(angle)


@functools.lru_cache(maxsize=None)
def tables():
    fine, wide, rows = np.arange(FINE), np.arange(LANES), np.arange(ROWS)
    window = 0.5 - 0.5 * np.cos(2.0 * np.pi * np.arange(NFFT) / NFFT)
    cos, sin = turn(fine, fine, FINE)
    first_high, first_low = two_parts(np.tile(np.concatenate([cos, -sin]), (1, GROUP)))
    fwd_cos, fwd_sin = turn(fine, wide, NFFT)
    f_order = np.array([4 * d + g for g in range(4) for d in range(ROWS)])
    cos, sin = turn(wide, f_order, LANES)
    second_high, second_low = two_parts(np.block([[cos, -sin], [sin, cos]]))
    scale_q, scale_c = row_scale(FINE, FINE), row_scale(LANES, LANES)
    cos, sin = turn(fine, rows, FINE)
    cos, sin = np.tile(cos * scale_q[:, None], (1, GROUP)), np.tile(sin * scale_q[:, None], (1, GROUP))
    third = np.block([[cos, -sin], [sin, cos]])
    inv_cos, inv_sin = turn(fine, wide, NFFT)
    undo = 1.0 / (scale_q[:, None] * scale_c[None, :])
    cos, sin = turn(wide, wide, LANES)
    cos, sin = cos * scale_c[:, None], sin * scale_c[:, None]
    fourth = np.block([[cos, sin], [-sin, cos]])
    narrow = np.concatenate(
        [first_high, first_low, as_bf16(third), np.concatenate([second_high, second_low], axis=1), as_bf16(fourth)]
    )
    broad = np.concatenate([window.reshape(FINE, LANES), fwd_cos, fwd_sin, inv_cos * undo, inv_sin * undo])
    return narrow, np.asarray(broad, np.float32), float((window * window).sum())


def dot(left, right):
    return jnp.dot(left, right, preferred_element_type=jnp.float32)


def split(value):
    high = value.astype(jnp.bfloat16)
    return high, (value - high.astype(jnp.float32)).astype(jnp.bfloat16)


def repeat(count, body, carry):
    if count <= 8:
        for step in range(count):
            carry = body(step, carry)
        return carry
    return lax.fori_loop(0, count, body, carry)


def block_diagonal(rows, width):
    lane = lax.broadcasted_iota(jnp.int32, rows.shape, 1)
    owner = lax.rem(lane // width, GROUP)
    return jnp.concatenate(
        [jnp.where(owner == s, rows, jnp.zeros_like(rows)) for s in range(GROUP)], axis=0
    )


def natural(flipped, at, source):
    part = lax.broadcasted_iota(jnp.int32, (ROWS, LANES), 1) // FINE
    result = None
    for g in range(4):
        piece = flipped[at + g * ROWS:at + (g + 1) * ROWS]
        if source is not None and g != source:
            piece = pltpu.roll(piece, ((g - source) % 4) * FINE, 1)
        result = piece if g == 0 else jnp.where(part == g, piece, result)
    return result


def bank_kernel(devices, *refs):
    blocks = refs[:devices]
    cutoff, bank, gathered = refs[devices:]
    rank = lax.axis_index("tm")
    _, count, width = blocks[0].shape
    shape = (count, count)
    same = lax.broadcasted_iota(jnp.int32, shape, 0) == lax.broadcasted_iota(jnp.int32, shape, 1)
    column = jnp.sum(jnp.where(same, cutoff[...], 0), axis=1, keepdims=True)
    lane = lax.broadcasted_iota(jnp.int32, (count, LANES), 1)
    for other, block in enumerate(blocks):
        first = (rank ^ other) * (width // LANES)
        for at in range(width // LANES):
            lanes = slice(at * LANES, (at + 1) * LANES)
            keep = lane + (first + at) * LANES < column
            both = [jnp.where(keep, block[i, :, lanes].astype(jnp.float32), 0.0) for i in range(2)]
            gathered[first + at] = jnp.concatenate(both, axis=1).astype(jnp.bfloat16)
    shape = (count * ROWS, count * ROWS)
    to, source = lax.broadcasted_iota(jnp.int32, shape, 0), lax.broadcasted_iota(jnp.int32, shape, 1)
    order = (source == (to % ROWS) * count + to // ROWS).astype(jnp.float32).astype(jnp.bfloat16)
    value = dot(order, gathered[...].reshape(ROWS * count, 2 * LANES))
    bank[0] = value[:, :LANES].reshape(count, ROWS, LANES)
    bank[1] = value[:, LANES:].reshape(count, ROWS, LANES)


def filter_kernel(energy, mine, others, bank, narrow, broad, out, spec, halves):
    core = lax.rem(lax.axis_index("tmpl"), 2)
    halves[:, core] = mine[...]
    halves[:, 1 - core] = others[...]
    segs = 2 * mine.shape[0] * mine.shape[1] // ROWS
    record = halves.reshape(segs, ROWS, LANES)
    own, count = out.shape
    half = GROUP * FINE
    w_low, w_high = broad[:ROWS][None], broad[ROWS:FINE][None]
    fwd_cos, fwd_sin = broad[FINE:2 * FINE][None], broad[2 * FINE:3 * FINE][None]
    inv_cos, inv_sin = broad[3 * FINE:4 * FINE][None], broad[4 * FINE:5 * FINE][None]
    high, low = narrow[:2 * FINE], narrow[2 * FINE:4 * FINE]
    spread = lambda part: jnp.concatenate(
        [block_diagonal(part[:FINE], part.shape[1] // GROUP), block_diagonal(part[FINE:], part.shape[1] // GROUP)]
    )
    first_high = spread(high)
    first = jnp.concatenate([first_high, first_high, spread(low)], axis=1)
    third_rows = narrow[4 * FINE:6 * FINE]
    third = jnp.concatenate([block_diagonal(third_rows[:FINE], ROWS), block_diagonal(third_rows[FINE:], ROWS)])
    second = slice(6 * FINE, 6 * FINE + 2 * LANES)
    fourth = slice(6 * FINE + 2 * LANES, 6 * FINE + 4 * LANES)

    def frames(start, last):
        here = record[pl.ds(start, GROUP)]
        if last:
            after = jnp.concatenate([record[pl.ds(start + 1, GROUP - 1)], record[pl.ds(0, 1)]], axis=0)
        else:
            after = record[pl.ds(start + 1, GROUP)]
        both = jnp.concatenate([here * w_low, after * w_high], axis=1)
        return both.reshape(half, LANES)

    def first_product(start, last):
        pair = jnp.concatenate([frames(start, False), frames(start + GROUP, last)], axis=1)
        high, low = split(pair)
        return dot(first, jnp.concatenate([high, low, high], axis=0))

    def second_product(step, h):
        re = step[:half, h * LANES:(h + 1) * LANES].reshape(GROUP, FINE, LANES)
        im = step[half:, h * LANES:(h + 1) * LANES].reshape(GROUP, FINE, LANES)
        turned = jnp.concatenate([re * fwd_cos + im * fwd_sin, im * fwd_cos - re * fwd_sin], axis=2)
        high, low = split(turned.reshape(half, 2 * LANES))
        return dot(jnp.concatenate([high, low], axis=1), jnp.concatenate([narrow[second]] * 2, axis=0))

    def add_power(both, at, power):
        value = both[:, :LANES] + both[:, LANES:]
        spec[pl.ds(at * FINE, half)] = value
        return power + jnp.sum((value * value).reshape(GROUP, FINE, LANES), axis=0)

    def whole(start, last, power):
        step = first_product(start, last)
        for h in range(2):
            power = add_power(second_product(step, h), start + h * GROUP, power)
        return power

    power = jnp.zeros((FINE, LANES), jnp.float32)
    pairs = segs // (2 * GROUP)
    stride = 2 * GROUP
    if pairs <= 4:
        steps = [first_product(i * stride, i == pairs - 1) for i in range(pairs)]
        waiting = None
        for i, step in enumerate(steps):
            for h in range(2):
                both = second_product(step, h)
                if waiting is not None:
                    power = add_power(*waiting, power)
                waiting = (both, i * stride + h * GROUP)
        power = add_power(*waiting, power)
    else:
        power = lax.fori_loop(0, pairs - 1, lambda i, p: whole(i * stride, False, p), power)
        power = whole((pairs - 1) * stride, True, power)
    power = power + pltpu.roll(power, LANES // 2, 1)
    density = power / (segs * energy) + FLOOR
    inverse_density = natural((1.0 / jnp.concatenate([density] * 4, axis=0)).T, 0, None)

    place = lax.axis_index("tm") * own
    column = lax.broadcasted_iota(jnp.int32, (GROUP, LANES), 1)

    def block(number, carry):
        at = pl.multiple_of((place + number * GROUP) * FINE, half)
        white = spec[pl.ds(at, half)].reshape(GROUP, FINE, LANES) / density[None]
        white = white.astype(jnp.bfloat16).astype(jnp.float32).reshape(2, 4 * FINE, LANES)
        re_parts, im_parts = [], []
        for side in range(2):
            flipped = white[side].T
            for s in range(4):
                re_parts.append(natural(flipped, 0, s))
                im_parts.append(natural(flipped, LANES // 2, s))
        white_re, white_im = jnp.stack(re_parts), jnp.stack(im_parts)

        def section_of(step):
            sides, norms = [], []
            for m in (2 * step, 2 * step + 1):
                h_re, h_im = bank[0, m], bank[1, m]
                norms.append(jnp.sum((h_re * h_re + h_im * h_im) * inverse_density, keepdims=True))
                c_re = h_re[None] * white_re + h_im[None] * white_im
                c_im = h_re[None] * white_im - h_im[None] * white_re
                both = jnp.concatenate([c_re, c_im], axis=0).reshape(2 * GROUP * ROWS, LANES)
                sides.append(both.astype(jnp.bfloat16))
            return dot(third, jnp.concatenate(sides, axis=1)), norms

        def wave_of(section, side):
            re = section[:half, side * LANES:(side + 1) * LANES].reshape(GROUP, FINE, LANES)
            im = section[half:, side * LANES:(side + 1) * LANES].reshape(GROUP, FINE, LANES)
            turned = jnp.concatenate([re * inv_cos - im * inv_sin, re * inv_sin + im * inv_cos], axis=2)
            return dot(turned.reshape(half, 2 * LANES).astype(jnp.bfloat16), narrow[fourth])

        def peak_of(m, wave, norm, result):
            square = wave[:, :LANES] * wave[:, :LANES] + wave[:, LANES:] * wave[:, LANES:]
            top = jnp.max(jnp.max(square.reshape(GROUP, FINE, LANES), axis=1), axis=1, keepdims=True)
            value = jnp.sqrt(top) / (jnp.sqrt(norm) * math.sqrt(energy))
            return jnp.where(column == m, value, result)

        result = jnp.zeros((GROUP, LANES), jnp.float32)
        ready, waiting = section_of(0), None
        for step in range(count // 2):
            section, norms = ready
            if step + 1 < count // 2:
                ready = section_of(step + 1)
            for side in range(2):
                wave = wave_of(section, side)
                if waiting is not None:
                    result = peak_of(*waiting, result)
                waiting = (2 * step + side, wave, norms[side])
        result = peak_of(*waiting, result)
        out[pl.ds(number * GROUP, GROUP)] = result[:, :count]
        return carry

    repeat(own // GROUP, block, 0)


def swap(array, axis, bits):
    return lax.ppermute(array, axis, [(i, i ^ bits) for i in range(lax.axis_size(axis))])


def on_device(strain, templates, cutoff):
    tm, devices = lax.axis_size("tm"), lax.axis_size("tm") * lax.axis_size("tmpl")
    size = strain.shape[0] // HOP
    segs = devices * size
    own = segs // tm
    count = templates.shape[1]
    vmem = pl.BlockSpec(memory_space=pltpu.VMEM)
    params = pltpu.CompilerParams(vmem_limit_bytes=40 * 1024 * 1024)
    f32 = jnp.float32

    chunk = strain.reshape(1, size * ROWS, LANES)
    copies = jnp.broadcast_to(chunk, (devices // 2, size * ROWS, LANES))
    copies, held = lax.optimization_barrier((copies, templates))
    copies = copies.reshape(devices, size * ROWS // 2, LANES)
    mine = lax.all_to_all(copies, ("tm", "tmpl"), split_axis=0, concat_axis=0, tiled=True)
    blocks = [swap(held, "tm", other) for other in range(1, tm)]
    others = swap(mine, "tmpl", 1)
    blocks = [held] + blocks
    bank = pl.pallas_call(
        functools.partial(bank_kernel, tm),
        out_shape=jax.ShapeDtypeStruct((2, count, ROWS, LANES), f32),
        in_specs=[vmem] * (tm + 1),
        out_specs=vmem,
        scratch_shapes=[pltpu.VMEM((ROWS, count, 2 * LANES), jnp.bfloat16)],
        compiler_params=params,
        cost_estimate=pl.CostEstimate(flops=0, bytes_accessed=2500000, transcendentals=0),
        name="bank",
    )(*blocks, cutoff.reshape(1, count))
    narrow, broad, energy = tables()
    return pl.pallas_call(
        functools.partial(filter_kernel, energy),
        out_shape=jax.ShapeDtypeStruct((own, count), f32),
        in_specs=[vmem] * 5,
        out_specs=vmem,
        scratch_shapes=[
            pltpu.VMEM((segs * FINE, LANES), f32),
            pltpu.VMEM((devices, 2, size * ROWS // 2, LANES), f32),
        ],
        compiler_params=params,
        name="matched_filter",
    )(mine, others, bank, jnp.asarray(narrow), jnp.asarray(broad))


def solution(mesh):
    in_specs = (P(("tm", "tmpl")), P(None, "tmpl", "tm"), P("tmpl"))
    out_specs = P("tm", "tmpl")
    return jax.shard_map(
        on_device, mesh=mesh, in_specs=in_specs, out_specs=out_specs, check_vma=False
    )
```

```python
import functools
import math

import jax
import jax.numpy as jnp
import ml_dtypes
import numpy as np
from jax import lax
from jax.experimental import pallas as pl
from jax.experimental.pallas import tpu as pltpu
from jax.sharding import PartitionSpec as P

NFFT = 4096
BINS = 2048
HOP = 2048
LANES = 128
ROWS = HOP // LANES
FINE = 32
GROUP = 8
FLOOR = 1e-6

ROOT_SCALE = {128: 1.66575, 64: 1.66575, 32: 1.6245, 16: 1.6245, 8: 1.6245}


def root_order(index, period):
    return period // math.gcd(int(index), period)


def row_scale(count, period):
    return np.array([ROOT_SCALE.get(root_order(i, period), 1.0) for i in range(count)])


def as_bf16(table):
    return np.asarray(table, np.float32).astype(ml_dtypes.bfloat16)


def two_parts(table):
    high = as_bf16(table)
    low = as_bf16(np.asarray(table, np.float64) - high.astype(np.float64))
    return high, low


def turn(left, right, period):
    angle = 2.0 * np.pi * (np.outer(left, right) % period) / period
    return np.cos(angle), np.sin(angle)


@functools.lru_cache(maxsize=None)
def tables():
    fine, wide, rows = np.arange(FINE), np.arange(LANES), np.arange(ROWS)
    window = 0.5 - 0.5 * np.cos(2.0 * np.pi * np.arange(NFFT) / NFFT)
    cos, sin = turn(fine, fine, FINE)
    first_high, first_low = two_parts(np.tile(np.concatenate([cos, -sin]), (1, GROUP)))
    fwd_cos, fwd_sin = turn(fine, wide, NFFT)
    f_order = np.array([4 * d + g for g in range(4) for d in range(ROWS)])
    cos, sin = turn(wide, f_order, LANES)
    second_high, second_low = two_parts(np.block([[cos, -sin], [sin, cos]]))
    scale_q, scale_c = row_scale(FINE, FINE), row_scale(LANES, LANES)
    cos, sin = turn(fine, rows, FINE)
    cos, sin = np.tile(cos * scale_q[:, None], (1, GROUP)), np.tile(sin * scale_q[:, None], (1, GROUP))
    third = np.block([[cos, -sin], [sin, cos]])
    inv_cos, inv_sin = turn(fine, wide, NFFT)
    undo = 1.0 / (scale_q[:, None] * scale_c[None, :])
    cos, sin = turn(wide, wide, LANES)
    cos, sin = cos * scale_c[:, None], sin * scale_c[:, None]
    fourth = np.block([[cos, sin], [-sin, cos]])
    narrow = np.concatenate(
        [first_high, first_low, as_bf16(third), np.concatenate([second_high, second_low], axis=1), as_bf16(fourth)]
    )
    broad = np.concatenate([window.reshape(FINE, LANES), fwd_cos, fwd_sin, inv_cos * undo, inv_sin * undo])
    return narrow, np.asarray(broad, np.float32), float((window * window).sum())


def dot(left, right):
    return jnp.dot(left, right, preferred_element_type=jnp.float32)


def split(value):
    high = value.astype(jnp.bfloat16)
    return high, (value - high.astype(jnp.float32)).astype(jnp.bfloat16)


def repeat(count, body, carry):
    if count <= 8:
        for step in range(count):
            carry = body(step, carry)
        return carry
    return lax.fori_loop(0, count, body, carry)


def block_diagonal(rows, width):
    lane = lax.broadcasted_iota(jnp.int32, rows.shape, 1)
    owner = lax.rem(lane // width, GROUP)
    return jnp.concatenate(
        [jnp.where(owner == s, rows, jnp.zeros_like(rows)) for s in range(GROUP)], axis=0
    )


def natural(flipped, at, source):
    part = lax.broadcasted_iota(jnp.int32, (ROWS, LANES), 1) // FINE
    result = None
    for g in range(4):
        piece = flipped[at + g * ROWS:at + (g + 1) * ROWS]
        if source is not None and g != source:
            piece = pltpu.roll(piece, ((g - source) % 4) * FINE, 1)
        result = piece if g == 0 else jnp.where(part == g, piece, result)
    return result


def bank_kernel(*refs):
    *stacks, cutoff, bank, gathered = refs
    rank = lax.axis_index("tm")
    _, _, count, width = stacks[0].shape
    blocks = [stack.at[i] for stack in stacks for i in range(stack.shape[0])]
    shape = (count, count)
    same = lax.broadcasted_iota(jnp.int32, shape, 0) == lax.broadcasted_iota(jnp.int32, shape, 1)
    column = jnp.sum(jnp.where(same, cutoff[...], 0), axis=1, keepdims=True)
    lane = lax.broadcasted_iota(jnp.int32, (count, LANES), 1)
    for other, block in enumerate(blocks):
        first = (rank ^ other) * (width // LANES)
        for at in range(width // LANES):
            lanes = slice(at * LANES, (at + 1) * LANES)
            keep = lane + (first + at) * LANES < column
            both = [jnp.where(keep, block[i, :, lanes].astype(jnp.float32), 0.0) for i in range(2)]
            gathered[first + at] = jnp.concatenate(both, axis=1).astype(jnp.bfloat16)
    shape = (count * ROWS, count * ROWS)
    to, source = lax.broadcasted_iota(jnp.int32, shape, 0), lax.broadcasted_iota(jnp.int32, shape, 1)
    order = (source == (to % ROWS) * count + to // ROWS).astype(jnp.float32).astype(jnp.bfloat16)
    value = dot(order, gathered[...].reshape(ROWS * count, 2 * LANES))
    bank[0] = value[:, :LANES].reshape(count, ROWS, LANES)
    bank[1] = value[:, LANES:].reshape(count, ROWS, LANES)


def filter_kernel(energy, mine, others, bank, narrow, broad, out, spec, halves):
    core = lax.rem(lax.axis_index("tmpl"), 2)
    halves[:, core] = mine[...]
    halves[:, 1 - core] = others[...]
    segs = 2 * mine.shape[0] * mine.shape[1] // ROWS
    record = halves.reshape(segs, ROWS, LANES)
    own, count = out.shape
    half = GROUP * FINE
    w_low, w_high = broad[:ROWS][None], broad[ROWS:FINE][None]
    fwd_cos, fwd_sin = broad[FINE:2 * FINE][None], broad[2 * FINE:3 * FINE][None]
    inv_cos, inv_sin = broad[3 * FINE:4 * FINE][None], broad[4 * FINE:5 * FINE][None]
    high, low = narrow[:2 * FINE], narrow[2 * FINE:4 * FINE]
    spread = lambda part: jnp.concatenate(
        [block_diagonal(part[:FINE], part.shape[1] // GROUP), block_diagonal(part[FINE:], part.shape[1] // GROUP)]
    )
    first_high = spread(high)
    first = jnp.concatenate([first_high, first_high, spread(low)], axis=1)
    third_rows = narrow[4 * FINE:6 * FINE]
    third = jnp.concatenate([block_diagonal(third_rows[:FINE], ROWS), block_diagonal(third_rows[FINE:], ROWS)])
    second = slice(6 * FINE, 6 * FINE + 2 * LANES)
    fourth = slice(6 * FINE + 2 * LANES, 6 * FINE + 4 * LANES)

    def frames(start, last):
        here = record[pl.ds(start, GROUP)]
        if last:
            after = jnp.concatenate([record[pl.ds(start + 1, GROUP - 1)], record[pl.ds(0, 1)]], axis=0)
        else:
            after = record[pl.ds(start + 1, GROUP)]
        both = jnp.concatenate([here * w_low, after * w_high], axis=1)
        return both.reshape(half, LANES)

    def first_product(start, last):
        pair = jnp.concatenate([frames(start, False), frames(start + GROUP, last)], axis=1)
        high, low = split(pair)
        return dot(first, jnp.concatenate([high, low, high], axis=0))

    def second_product(step, h):
        re = step[:half, h * LANES:(h + 1) * LANES].reshape(GROUP, FINE, LANES)
        im = step[half:, h * LANES:(h + 1) * LANES].reshape(GROUP, FINE, LANES)
        turned = jnp.concatenate([re * fwd_cos + im * fwd_sin, im * fwd_cos - re * fwd_sin], axis=2)
        high, low = split(turned.reshape(half, 2 * LANES))
        return dot(jnp.concatenate([high, low], axis=1), jnp.concatenate([narrow[second]] * 2, axis=0))

    def add_power(both, at, power):
        value = both[:, :LANES] + both[:, LANES:]
        spec[pl.ds(at * FINE, half)] = value
        return power + jnp.sum((value * value).reshape(GROUP, FINE, LANES), axis=0)

    def whole(start, last, power):
        step = first_product(start, last)
        for h in range(2):
            power = add_power(second_product(step, h), start + h * GROUP, power)
        return power

    power = jnp.zeros((FINE, LANES), jnp.float32)
    pairs = segs // (2 * GROUP)
    stride = 2 * GROUP
    if pairs <= 4:
        steps = [first_product(i * stride, i == pairs - 1) for i in range(pairs)]
        waiting = None
        for i, step in enumerate(steps):
            for h in range(2):
                both = second_product(step, h)
                if waiting is not None:
                    power = add_power(*waiting, power)
                waiting = (both, i * stride + h * GROUP)
        power = add_power(*waiting, power)
    else:
        power = lax.fori_loop(0, pairs - 1, lambda i, p: whole(i * stride, False, p), power)
        power = whole((pairs - 1) * stride, True, power)
    power = power + pltpu.roll(power, LANES // 2, 1)
    density = power / (segs * energy) + FLOOR
    inverse_density = natural((1.0 / jnp.concatenate([density] * 4, axis=0)).T, 0, None)

    place = lax.axis_index("tm") * own
    column = lax.broadcasted_iota(jnp.int32, (GROUP, LANES), 1)

    def block(number, carry):
        at = pl.multiple_of((place + number * GROUP) * FINE, half)
        white = spec[pl.ds(at, half)].reshape(GROUP, FINE, LANES) / density[None]
        white = white.astype(jnp.bfloat16).astype(jnp.float32).reshape(2, 4 * FINE, LANES)
        re_parts, im_parts = [], []
        for side in range(2):
            flipped = white[side].T
            for s in range(4):
                re_parts.append(natural(flipped, 0, s))
                im_parts.append(natural(flipped, LANES // 2, s))
        white_re, white_im = jnp.stack(re_parts), jnp.stack(im_parts)

        def section_of(step):
            sides, norms = [], []
            for m in (2 * step, 2 * step + 1):
                h_re, h_im = bank[0, m], bank[1, m]
                norms.append(jnp.sum((h_re * h_re + h_im * h_im) * inverse_density, keepdims=True))
                c_re = h_re[None] * white_re + h_im[None] * white_im
                c_im = h_re[None] * white_im - h_im[None] * white_re
                both = jnp.concatenate([c_re, c_im], axis=0).reshape(2 * GROUP * ROWS, LANES)
                sides.append(both.astype(jnp.bfloat16))
            return dot(third, jnp.concatenate(sides, axis=1)), norms

        def wave_of(section, side):
            re = section[:half, side * LANES:(side + 1) * LANES].reshape(GROUP, FINE, LANES)
            im = section[half:, side * LANES:(side + 1) * LANES].reshape(GROUP, FINE, LANES)
            turned = jnp.concatenate([re * inv_cos - im * inv_sin, re * inv_sin + im * inv_cos], axis=2)
            return dot(turned.reshape(half, 2 * LANES).astype(jnp.bfloat16), narrow[fourth])

        def peak_of(m, wave, norm, result):
            square = wave[:, :LANES] * wave[:, :LANES] + wave[:, LANES:] * wave[:, LANES:]
            top = jnp.max(jnp.max(square.reshape(GROUP, FINE, LANES), axis=1), axis=1, keepdims=True)
            value = jnp.sqrt(top) / (jnp.sqrt(norm) * math.sqrt(energy))
            return jnp.where(column == m, value, result)

        result = jnp.zeros((GROUP, LANES), jnp.float32)
        ready, waiting = section_of(0), None
        for step in range(count // 2):
            section, norms = ready
            if step + 1 < count // 2:
                ready = section_of(step + 1)
            for side in range(2):
                wave = wave_of(section, side)
                if waiting is not None:
                    result = peak_of(*waiting, result)
                waiting = (2 * step + side, wave, norms[side])
        result = peak_of(*waiting, result)
        out[pl.ds(number * GROUP, GROUP)] = result[:, :count]
        return carry

    repeat(own // GROUP, block, 0)


def swap(array, axis, bits):
    return lax.ppermute(array, axis, [(i, i ^ bits) for i in range(lax.axis_size(axis))])


def on_device(strain, templates, cutoff):
    tm, devices = lax.axis_size("tm"), lax.axis_size("tm") * lax.axis_size("tmpl")
    size = strain.shape[0] // HOP
    segs = devices * size
    own = segs // tm
    count = templates.shape[1]
    vmem = pl.BlockSpec(memory_space=pltpu.VMEM)
    params = pltpu.CompilerParams(vmem_limit_bytes=40 * 1024 * 1024)
    f32 = jnp.float32

    chunk = strain.reshape(1, size * ROWS, LANES)
    copies = jnp.broadcast_to(chunk, (devices // 2, size * ROWS, LANES))
    copies = copies.reshape(devices, size * ROWS // 2, LANES)
    mine = lax.all_to_all(copies, ("tm", "tmpl"), split_axis=0, concat_axis=0, tiled=True)
    blocks, bits = [templates[None]], 1
    while bits < tm:
        known = blocks[0] if bits == 1 else jnp.concatenate(blocks, axis=0)
        blocks.append(swap(known, "tm", bits))
        bits *= 2
    mine, *blocks = lax.optimization_barrier((mine, *blocks))
    others = swap(mine, "tmpl", 1)
    bank = pl.pallas_call(
        bank_kernel,
        out_shape=jax.ShapeDtypeStruct((2, count, ROWS, LANES), f32),
        in_specs=[vmem] * (len(blocks) + 1),
        out_specs=vmem,
        scratch_shapes=[pltpu.VMEM((ROWS, count, 2 * LANES), jnp.bfloat16)],
        compiler_params=params,
        cost_estimate=pl.CostEstimate(flops=0, bytes_accessed=2500000, transcendentals=0),
        name="bank",
    )(*blocks, cutoff.reshape(1, count))
    narrow, broad, energy = tables()
    return pl.pallas_call(
        functools.partial(filter_kernel, energy),
        out_shape=jax.ShapeDtypeStruct((own, count), f32),
        in_specs=[vmem] * 5,
        out_specs=vmem,
        scratch_shapes=[
            pltpu.VMEM((segs * FINE, LANES), f32),
            pltpu.VMEM((devices, 2, size * ROWS // 2, LANES), f32),
        ],
        compiler_params=params,
        name="matched_filter",
    )(mine, others, bank, jnp.asarray(narrow), jnp.asarray(broad))


def solution(mesh):
    in_specs = (P(("tm", "tmpl")), P(None, "tmpl", "tm"), P("tmpl"))
    out_specs = P("tm", "tmpl")
    return jax.shard_map(
        on_device, mesh=mesh, in_specs=in_specs, out_specs=out_specs, check_vma=False
    )
```

```python
import functools
import math

import jax
import jax.numpy as jnp
import ml_dtypes
import numpy as np
from jax import lax
from jax.experimental import pallas as pl
from jax.experimental.pallas import tpu as pltpu
from jax.sharding import PartitionSpec as P

NFFT = 4096
BINS = 2048
HOP = 2048
LANES = 128
ROWS = HOP // LANES
FINE = 32
GROUP = 8
FLOOR = 1e-6

ROOT_SCALE = {128: 1.66575, 64: 1.66575, 32: 1.6245, 16: 1.6245, 8: 1.6245}


def root_order(index, period):
    return period // math.gcd(int(index), period)


def row_scale(count, period):
    return np.array([ROOT_SCALE.get(root_order(i, period), 1.0) for i in range(count)])


def as_bf16(table):
    return np.asarray(table, np.float32).astype(ml_dtypes.bfloat16)


def two_parts(table):
    high = as_bf16(table)
    low = as_bf16(np.asarray(table, np.float64) - high.astype(np.float64))
    return high, low


def turn(left, right, period):
    angle = 2.0 * np.pi * (np.outer(left, right) % period) / period
    return np.cos(angle), np.sin(angle)


@functools.lru_cache(maxsize=None)
def tables():
    fine, wide, rows = np.arange(FINE), np.arange(LANES), np.arange(ROWS)
    window = 0.5 - 0.5 * np.cos(2.0 * np.pi * np.arange(NFFT) / NFFT)
    cos, sin = turn(fine, fine, FINE)
    first_high, first_low = two_parts(np.tile(np.concatenate([cos, -sin]), (1, GROUP)))
    fwd_cos, fwd_sin = turn(fine, wide, NFFT)
    f_order = np.array([4 * d + g for g in range(4) for d in range(ROWS)])
    cos, sin = turn(wide, f_order, LANES)
    second_high, second_low = two_parts(np.block([[cos, -sin], [sin, cos]]))
    scale_q, scale_c = row_scale(FINE, FINE), row_scale(LANES, LANES)
    cos, sin = turn(fine, rows, FINE)
    cos, sin = np.tile(cos * scale_q[:, None], (1, GROUP)), np.tile(sin * scale_q[:, None], (1, GROUP))
    third = np.block([[cos, -sin], [sin, cos]])
    inv_cos, inv_sin = turn(fine, wide, NFFT)
    undo = 1.0 / (scale_q[:, None] * scale_c[None, :])
    cos, sin = turn(wide, wide, LANES)
    cos, sin = cos * scale_c[:, None], sin * scale_c[:, None]
    fourth = np.block([[cos, sin], [-sin, cos]])
    narrow = np.concatenate(
        [first_high, first_low, as_bf16(third), np.concatenate([second_high, second_low], axis=1), as_bf16(fourth)]
    )
    broad = np.concatenate([window.reshape(FINE, LANES), fwd_cos, fwd_sin, inv_cos * undo, inv_sin * undo])
    return narrow, np.asarray(broad, np.float32), float((window * window).sum())


def dot(left, right):
    return jnp.dot(left, right, preferred_element_type=jnp.float32)


def split(value):
    high = value.astype(jnp.bfloat16)
    return high, (value - high.astype(jnp.float32)).astype(jnp.bfloat16)


def repeat(count, body, carry):
    if count <= 8:
        for step in range(count):
            carry = body(step, carry)
        return carry
    return lax.fori_loop(0, count, body, carry)


def block_diagonal(rows, width):
    lane = lax.broadcasted_iota(jnp.int32, rows.shape, 1)
    owner = lax.rem(lane // width, GROUP)
    return jnp.concatenate(
        [jnp.where(owner == s, rows, jnp.zeros_like(rows)) for s in range(GROUP)], axis=0
    )


def natural(flipped, at, source):
    part = lax.broadcasted_iota(jnp.int32, (ROWS, LANES), 1) // FINE
    result = None
    for g in range(4):
        piece = flipped[at + g * ROWS:at + (g + 1) * ROWS]
        if source is not None and g != source:
            piece = pltpu.roll(piece, ((g - source) % 4) * FINE, 1)
        result = piece if g == 0 else jnp.where(part == g, piece, result)
    return result


def bank_kernel(devices, *refs):
    blocks = refs[:devices]
    cutoff, bank, gathered = refs[devices:]
    rank = lax.axis_index("tm")
    _, count, width = blocks[0].shape
    shape = (count, count)
    same = lax.broadcasted_iota(jnp.int32, shape, 0) == lax.broadcasted_iota(jnp.int32, shape, 1)
    column = jnp.sum(jnp.where(same, cutoff[...], 0), axis=1, keepdims=True)
    lane = lax.broadcasted_iota(jnp.int32, (count, LANES), 1)
    for other, block in enumerate(blocks):
        first = (rank ^ other) * (width // LANES)
        for at in range(width // LANES):
            lanes = slice(at * LANES, (at + 1) * LANES)
            keep = lane + (first + at) * LANES < column
            both = [jnp.where(keep, block[i, :, lanes].astype(jnp.float32), 0.0) for i in range(2)]
            gathered[first + at] = jnp.concatenate(both, axis=1).astype(jnp.bfloat16)
    shape = (count * ROWS, count * ROWS)
    to, source = lax.broadcasted_iota(jnp.int32, shape, 0), lax.broadcasted_iota(jnp.int32, shape, 1)
    order = (source == (to % ROWS) * count + to // ROWS).astype(jnp.float32).astype(jnp.bfloat16)
    value = dot(order, gathered[...].reshape(ROWS * count, 2 * LANES))
    bank[0] = value[:, :LANES].reshape(count, ROWS, LANES)
    bank[1] = value[:, LANES:].reshape(count, ROWS, LANES)


def filter_kernel(energy, mine, others, bank, narrow, broad, out, spec, halves):
    core = lax.rem(lax.axis_index("tmpl"), 2)
    halves[:, core] = mine[...]
    halves[:, 1 - core] = others[...]
    segs = 2 * mine.shape[0] * mine.shape[1] // ROWS
    record = halves.reshape(segs, ROWS, LANES)
    own, count = out.shape
    half = GROUP * FINE
    w_low, w_high = broad[:ROWS][None], broad[ROWS:FINE][None]
    fwd_cos, fwd_sin = broad[FINE:2 * FINE][None], broad[2 * FINE:3 * FINE][None]
    inv_cos, inv_sin = broad[3 * FINE:4 * FINE][None], broad[4 * FINE:5 * FINE][None]
    high, low = narrow[:2 * FINE], narrow[2 * FINE:4 * FINE]
    spread = lambda part: jnp.concatenate(
        [block_diagonal(part[:FINE], part.shape[1] // GROUP), block_diagonal(part[FINE:], part.shape[1] // GROUP)]
    )
    first_high = spread(high)
    first = jnp.concatenate([first_high, first_high, spread(low)], axis=1)
    third_rows = narrow[4 * FINE:6 * FINE]
    third = jnp.concatenate([block_diagonal(third_rows[:FINE], ROWS), block_diagonal(third_rows[FINE:], ROWS)])
    second = slice(6 * FINE, 6 * FINE + 2 * LANES)
    fourth = slice(6 * FINE + 2 * LANES, 6 * FINE + 4 * LANES)

    def frames(start, last):
        here = record[pl.ds(start, GROUP)]
        if last:
            after = jnp.concatenate([record[pl.ds(start + 1, GROUP - 1)], record[pl.ds(0, 1)]], axis=0)
        else:
            after = record[pl.ds(start + 1, GROUP)]
        both = jnp.concatenate([here * w_low, after * w_high], axis=1)
        return both.reshape(half, LANES)

    def first_product(start, last):
        pair = jnp.concatenate([frames(start, False), frames(start + GROUP, last)], axis=1)
        high, low = split(pair)
        return dot(first, jnp.concatenate([high, low, high], axis=0))

    def second_product(step, h):
        re = step[:half, h * LANES:(h + 1) * LANES].reshape(GROUP, FINE, LANES)
        im = step[half:, h * LANES:(h + 1) * LANES].reshape(GROUP, FINE, LANES)
        turned = jnp.concatenate([re * fwd_cos + im * fwd_sin, im * fwd_cos - re * fwd_sin], axis=2)
        high, low = split(turned.reshape(half, 2 * LANES))
        return dot(jnp.concatenate([high, low], axis=1), jnp.concatenate([narrow[second]] * 2, axis=0))

    def add_power(both, at, power):
        value = both[:, :LANES] + both[:, LANES:]
        spec[pl.ds(at * FINE, half)] = value
        return power + jnp.sum((value * value).reshape(GROUP, FINE, LANES), axis=0)

    def whole(start, last, power):
        step = first_product(start, last)
        for h in range(2):
            power = add_power(second_product(step, h), start + h * GROUP, power)
        return power

    power = jnp.zeros((FINE, LANES), jnp.float32)
    pairs = segs // (2 * GROUP)
    stride = 2 * GROUP
    if pairs <= 4:
        steps = [first_product(i * stride, i == pairs - 1) for i in range(pairs)]
        waiting = None
        for i, step in enumerate(steps):
            for h in range(2):
                both = second_product(step, h)
                if waiting is not None:
                    power = add_power(*waiting, power)
                waiting = (both, i * stride + h * GROUP)
        power = add_power(*waiting, power)
    else:
        power = lax.fori_loop(0, pairs - 1, lambda i, p: whole(i * stride, False, p), power)
        power = whole((pairs - 1) * stride, True, power)
    power = power + pltpu.roll(power, LANES // 2, 1)
    density = power / (segs * energy) + FLOOR
    density = natural(jnp.concatenate([density] * 4, axis=0).T, 0, None)
    inverse_density = 1.0 / density

    place = lax.axis_index("tm") * own
    column = lax.broadcasted_iota(jnp.int32, (GROUP, LANES), 1)

    def block(number, carry):
        at = pl.multiple_of((place + number * GROUP) * FINE, half)
        values = spec[pl.ds(at, half)].reshape(2, 4 * FINE, LANES)
        re_parts, im_parts = [], []
        for side in range(2):
            flipped = values[side].T
            for s in range(4):
                re_parts.append(natural(flipped, 0, s))
                im_parts.append(natural(flipped, LANES // 2, s))
        white_re, white_im = (
            (jnp.stack(parts) / density[None]).astype(jnp.bfloat16).astype(jnp.float32)
            for parts in (re_parts, im_parts)
        )

        def section_of(step):
            sides, norms = [], []
            for m in (2 * step, 2 * step + 1):
                h_re, h_im = bank[0, m], bank[1, m]
                norms.append(jnp.sum((h_re * h_re + h_im * h_im) * inverse_density, keepdims=True))
                c_re = h_re[None] * white_re + h_im[None] * white_im
                c_im = h_re[None] * white_im - h_im[None] * white_re
                both = jnp.concatenate([c_re, c_im], axis=0).reshape(2 * GROUP * ROWS, LANES)
                sides.append(both.astype(jnp.bfloat16))
            return dot(third, jnp.concatenate(sides, axis=1)), norms

        def wave_of(section, side):
            re = section[:half, side * LANES:(side + 1) * LANES].reshape(GROUP, FINE, LANES)
            im = section[half:, side * LANES:(side + 1) * LANES].reshape(GROUP, FINE, LANES)
            turned = jnp.concatenate([re * inv_cos - im * inv_sin, re * inv_sin + im * inv_cos], axis=2)
            return dot(turned.reshape(half, 2 * LANES).astype(jnp.bfloat16), narrow[fourth])

        def peak_of(m, wave, norm, result):
            square = wave[:, :LANES] * wave[:, :LANES] + wave[:, LANES:] * wave[:, LANES:]
            top = jnp.max(jnp.max(square.reshape(GROUP, FINE, LANES), axis=1), axis=1, keepdims=True)
            value = jnp.sqrt(top) / (jnp.sqrt(norm) * math.sqrt(energy))
            return jnp.where(column == m, value, result)

        result = jnp.zeros((GROUP, LANES), jnp.float32)
        ready, waiting = section_of(0), None
        for step in range(count // 2):
            section, norms = ready
            if step + 1 < count // 2:
                ready = section_of(step + 1)
            for side in range(2):
                wave = wave_of(section, side)
                if waiting is not None:
                    result = peak_of(*waiting, result)
                waiting = (2 * step + side, wave, norms[side])
        result = peak_of(*waiting, result)
        out[pl.ds(number * GROUP, GROUP)] = result[:, :count]
        return carry

    repeat(own // GROUP, block, 0)


def swap(array, axis, bits):
    return lax.ppermute(array, axis, [(i, i ^ bits) for i in range(lax.axis_size(axis))])


def on_device(strain, templates, cutoff):
    tm, devices = lax.axis_size("tm"), lax.axis_size("tm") * lax.axis_size("tmpl")
    size = strain.shape[0] // HOP
    segs = devices * size
    own = segs // tm
    count = templates.shape[1]
    vmem = pl.BlockSpec(memory_space=pltpu.VMEM)
    params = pltpu.CompilerParams(vmem_limit_bytes=40 * 1024 * 1024)
    f32 = jnp.float32

    chunk = strain.reshape(1, size * ROWS, LANES)
    copies = jnp.broadcast_to(chunk, (devices // 2, size * ROWS, LANES))
    copies, held = lax.optimization_barrier((copies, templates))
    copies = copies.reshape(devices, size * ROWS // 2, LANES)
    mine = lax.all_to_all(copies, ("tm", "tmpl"), split_axis=0, concat_axis=0, tiled=True)
    blocks = [swap(held, "tm", other) for other in range(1, tm)]
    mine, *blocks = lax.optimization_barrier((mine, *blocks))
    others = swap(mine, "tmpl", 1)
    blocks = [held] + blocks
    bank = pl.pallas_call(
        functools.partial(bank_kernel, tm),
        out_shape=jax.ShapeDtypeStruct((2, count, ROWS, LANES), f32),
        in_specs=[vmem] * (tm + 1),
        out_specs=vmem,
        scratch_shapes=[pltpu.VMEM((ROWS, count, 2 * LANES), jnp.bfloat16)],
        compiler_params=params,
        cost_estimate=pl.CostEstimate(flops=0, bytes_accessed=2500000, transcendentals=0),
        name="bank",
    )(*blocks, cutoff.reshape(1, count))
    narrow, broad, energy = tables()
    return pl.pallas_call(
        functools.partial(filter_kernel, energy),
        out_shape=jax.ShapeDtypeStruct((own, count), f32),
        in_specs=[vmem] * 5,
        out_specs=vmem,
        scratch_shapes=[
            pltpu.VMEM((segs * FINE, LANES), f32),
            pltpu.VMEM((devices, 2, size * ROWS // 2, LANES), f32),
        ],
        compiler_params=params,
        name="matched_filter",
    )(mine, others, bank, jnp.asarray(narrow), jnp.asarray(broad))


def solution(mesh):
    in_specs = (P(("tm", "tmpl")), P(None, "tmpl", "tm"), P("tmpl"))
    out_specs = P("tm", "tmpl")
    return jax.shard_map(
        on_device, mesh=mesh, in_specs=in_specs, out_specs=out_specs, check_vma=False
    )
```

```python
import functools
import math

import jax
import jax.numpy as jnp
import ml_dtypes
import numpy as np
from jax import lax
from jax.experimental import pallas as pl
from jax.experimental.pallas import tpu as pltpu
from jax.sharding import PartitionSpec as P

NFFT = 4096
BINS = 2048
HOP = 2048
LANES = 128
ROWS = HOP // LANES
FINE = 32
GROUP = 8
FLOOR = 1e-6

ROOT_SCALE = {128: 1.66575, 64: 1.66575, 32: 1.6245, 16: 1.6245, 8: 1.6245}


def root_order(index, period):
    return period // math.gcd(int(index), period)


def row_scale(count, period):
    return np.array([ROOT_SCALE.get(root_order(i, period), 1.0) for i in range(count)])


def as_bf16(table):
    return np.asarray(table, np.float32).astype(ml_dtypes.bfloat16)


def two_parts(table):
    high = as_bf16(table)
    low = as_bf16(np.asarray(table, np.float64) - high.astype(np.float64))
    return high, low


def turn(left, right, period):
    angle = 2.0 * np.pi * (np.outer(left, right) % period) / period
    return np.cos(angle), np.sin(angle)


@functools.lru_cache(maxsize=None)
def tables():
    fine, wide, rows = np.arange(FINE), np.arange(LANES), np.arange(ROWS)
    window = 0.5 - 0.5 * np.cos(2.0 * np.pi * np.arange(NFFT) / NFFT)
    cos, sin = turn(fine, fine, FINE)
    first_high, first_low = two_parts(np.tile(np.concatenate([cos, -sin]), (1, GROUP)))
    fwd_cos, fwd_sin = turn(fine, wide, NFFT)
    f_order = np.array([4 * d + g for g in range(4) for d in range(ROWS)])
    cos, sin = turn(wide, f_order, LANES)
    second_high, second_low = two_parts(np.block([[cos, -sin], [sin, cos]]))
    scale_q, scale_c = row_scale(FINE, FINE), row_scale(LANES, LANES)
    cos, sin = turn(fine, rows, FINE)
    cos, sin = np.tile(cos * scale_q[:, None], (1, GROUP)), np.tile(sin * scale_q[:, None], (1, GROUP))
    third = np.block([[cos, -sin], [sin, cos]])
    inv_cos, inv_sin = turn(fine, wide, NFFT)
    undo = 1.0 / (scale_q[:, None] * scale_c[None, :])
    cos, sin = turn(wide, wide, LANES)
    cos, sin = cos * scale_c[:, None], sin * scale_c[:, None]
    fourth = np.block([[cos, sin], [-sin, cos]])
    narrow = np.concatenate(
        [first_high, first_low, as_bf16(third), np.concatenate([second_high, second_low], axis=1), as_bf16(fourth)]
    )
    broad = np.concatenate([window.reshape(FINE, LANES), fwd_cos, fwd_sin, inv_cos * undo, inv_sin * undo])
    return narrow, np.asarray(broad, np.float32), float((window * window).sum())


def dot(left, right):
    return jnp.dot(left, right, preferred_element_type=jnp.float32)


def split(value):
    high = value.astype(jnp.bfloat16)
    return high, (value - high.astype(jnp.float32)).astype(jnp.bfloat16)


def repeat(count, body, carry):
    if count <= 8:
        for step in range(count):
            carry = body(step, carry)
        return carry
    return lax.fori_loop(0, count, body, carry)


def block_diagonal(rows, width):
    lane = lax.broadcasted_iota(jnp.int32, rows.shape, 1)
    owner = lax.rem(lane // width, GROUP)
    return jnp.concatenate(
        [jnp.where(owner == s, rows, jnp.zeros_like(rows)) for s in range(GROUP)], axis=0
    )


def natural(flipped, at, source):
    part = lax.broadcasted_iota(jnp.int32, (ROWS, LANES), 1) // FINE
    result = None
    for g in range(4):
        piece = flipped[at + g * ROWS:at + (g + 1) * ROWS]
        if source is not None and g != source:
            piece = pltpu.roll(piece, ((g - source) % 4) * FINE, 1)
        result = piece if g == 0 else jnp.where(part == g, piece, result)
    return result


def spread(part, width):
    return jnp.concatenate([block_diagonal(part[:FINE], width), block_diagonal(part[FINE:], width)])


def bank_kernel(devices, *refs):
    blocks = refs[:devices]
    cutoff, narrow, bank, first, third, gathered = refs[devices:]
    first[0] = spread(narrow[:2 * FINE], FINE)
    first[1] = spread(narrow[2 * FINE:4 * FINE], FINE)
    third[...] = spread(narrow[4 * FINE:6 * FINE], ROWS)
    rank = lax.axis_index("tm")
    _, count, width = blocks[0].shape
    shape = (count, count)
    same = lax.broadcasted_iota(jnp.int32, shape, 0) == lax.broadcasted_iota(jnp.int32, shape, 1)
    column = jnp.sum(jnp.where(same, cutoff[...], 0), axis=1, keepdims=True)
    lane = lax.broadcasted_iota(jnp.int32, (count, LANES), 1)
    for other, block in enumerate(blocks):
        first = (rank ^ other) * (width // LANES)
        for at in range(width // LANES):
            lanes = slice(at * LANES, (at + 1) * LANES)
            keep = lane + (first + at) * LANES < column
            both = [jnp.where(keep, block[i, :, lanes].astype(jnp.float32), 0.0) for i in range(2)]
            gathered[first + at] = jnp.concatenate(both, axis=1).astype(jnp.bfloat16)
    shape = (count * ROWS, count * ROWS)
    to, source = lax.broadcasted_iota(jnp.int32, shape, 0), lax.broadcasted_iota(jnp.int32, shape, 1)
    order = (source == (to % ROWS) * count + to // ROWS).astype(jnp.float32).astype(jnp.bfloat16)
    value = dot(order, gathered[...].reshape(ROWS * count, 2 * LANES))
    bank[0] = value[:, :LANES].reshape(count, ROWS, LANES)
    bank[1] = value[:, LANES:].reshape(count, ROWS, LANES)


def filter_kernel(energy, mine, others, bank, tables, third, narrow, broad, out, spec, halves):
    core = lax.rem(lax.axis_index("tmpl"), 2)
    halves[:, core] = mine[...]
    halves[:, 1 - core] = others[...]
    segs = 2 * mine.shape[0] * mine.shape[1] // ROWS
    record = halves.reshape(segs, ROWS, LANES)
    own, count = out.shape
    half = GROUP * FINE
    w_low, w_high = broad[:ROWS][None], broad[ROWS:FINE][None]
    fwd_cos, fwd_sin = broad[FINE:2 * FINE][None], broad[2 * FINE:3 * FINE][None]
    inv_cos, inv_sin = broad[3 * FINE:4 * FINE][None], broad[4 * FINE:5 * FINE][None]
    first = jnp.concatenate([tables[0], tables[0], tables[1]], axis=1)
    second = slice(6 * FINE, 6 * FINE + 2 * LANES)
    fourth = slice(6 * FINE + 2 * LANES, 6 * FINE + 4 * LANES)

    def frames(start, last):
        here = record[pl.ds(start, GROUP)]
        if last:
            after = jnp.concatenate([record[pl.ds(start + 1, GROUP - 1)], record[pl.ds(0, 1)]], axis=0)
        else:
            after = record[pl.ds(start + 1, GROUP)]
        both = jnp.concatenate([here * w_low, after * w_high], axis=1)
        return both.reshape(half, LANES)

    def first_product(start, last):
        pair = jnp.concatenate([frames(start, False), frames(start + GROUP, last)], axis=1)
        high, low = split(pair)
        return dot(first, jnp.concatenate([high, low, high], axis=0))

    def second_product(step, h):
        re = step[:half, h * LANES:(h + 1) * LANES].reshape(GROUP, FINE, LANES)
        im = step[half:, h * LANES:(h + 1) * LANES].reshape(GROUP, FINE, LANES)
        turned = jnp.concatenate([re * fwd_cos + im * fwd_sin, im * fwd_cos - re * fwd_sin], axis=2)
        high, low = split(turned.reshape(half, 2 * LANES))
        return dot(jnp.concatenate([high, low], axis=1), jnp.concatenate([narrow[second]] * 2, axis=0))

    def add_power(both, at, power):
        value = both[:, :LANES] + both[:, LANES:]
        spec[pl.ds(at * FINE, half)] = value
        return power + jnp.sum((value * value).reshape(GROUP, FINE, LANES), axis=0)

    def whole(start, last, power):
        step = first_product(start, last)
        for h in range(2):
            power = add_power(second_product(step, h), start + h * GROUP, power)
        return power

    power = jnp.zeros((FINE, LANES), jnp.float32)
    pairs = segs // (2 * GROUP)
    stride = 2 * GROUP
    if pairs <= 4:
        steps = [first_product(i * stride, i == pairs - 1) for i in range(pairs)]
        waiting = None
        for i, step in enumerate(steps):
            for h in range(2):
                both = second_product(step, h)
                if waiting is not None:
                    power = add_power(*waiting, power)
                waiting = (both, i * stride + h * GROUP)
        power = add_power(*waiting, power)
    else:
        power = lax.fori_loop(0, pairs - 1, lambda i, p: whole(i * stride, False, p), power)
        power = whole((pairs - 1) * stride, True, power)
    power = power + pltpu.roll(power, LANES // 2, 1)
    density = power / (segs * energy) + FLOOR
    density = natural(jnp.concatenate([density] * 4, axis=0).T, 0, None)
    inverse_density = 1.0 / density

    place = lax.axis_index("tm") * own
    column = lax.broadcasted_iota(jnp.int32, (GROUP, LANES), 1)

    def block(number, carry):
        at = pl.multiple_of((place + number * GROUP) * FINE, half)
        values = spec[pl.ds(at, half)].reshape(2, 4 * FINE, LANES)
        re_parts, im_parts = [], []
        for side in range(2):
            flipped = values[side].T
            for s in range(4):
                re_parts.append(natural(flipped, 0, s))
                im_parts.append(natural(flipped, LANES // 2, s))
        white_re, white_im = (
            (jnp.stack(parts) / density[None]).astype(jnp.bfloat16).astype(jnp.float32)
            for parts in (re_parts, im_parts)
        )

        def section_of(step):
            sides, norms = [], []
            for m in (2 * step, 2 * step + 1):
                h_re, h_im = bank[0, m], bank[1, m]
                norms.append(jnp.sum((h_re * h_re + h_im * h_im) * inverse_density, keepdims=True))
                c_re = h_re[None] * white_re + h_im[None] * white_im
                c_im = h_re[None] * white_im - h_im[None] * white_re
                both = jnp.concatenate([c_re, c_im], axis=0).reshape(2 * GROUP * ROWS, LANES)
                sides.append(both.astype(jnp.bfloat16))
            return dot(third[...], jnp.concatenate(sides, axis=1)), norms

        def wave_of(section, side):
            re = section[:half, side * LANES:(side + 1) * LANES].reshape(GROUP, FINE, LANES)
            im = section[half:, side * LANES:(side + 1) * LANES].reshape(GROUP, FINE, LANES)
            turned = jnp.concatenate([re * inv_cos - im * inv_sin, re * inv_sin + im * inv_cos], axis=2)
            return dot(turned.reshape(half, 2 * LANES).astype(jnp.bfloat16), narrow[fourth])

        def peak_of(m, wave, norm, result):
            square = wave[:, :LANES] * wave[:, :LANES] + wave[:, LANES:] * wave[:, LANES:]
            top = jnp.max(jnp.max(square.reshape(GROUP, FINE, LANES), axis=1), axis=1, keepdims=True)
            value = jnp.sqrt(top) / (jnp.sqrt(norm) * math.sqrt(energy))
            return jnp.where(column == m, value, result)

        result = jnp.zeros((GROUP, LANES), jnp.float32)
        ready, waiting = section_of(0), None
        for step in range(count // 2):
            section, norms = ready
            if step + 1 < count // 2:
                ready = section_of(step + 1)
            for side in range(2):
                wave = wave_of(section, side)
                if waiting is not None:
                    result = peak_of(*waiting, result)
                waiting = (2 * step + side, wave, norms[side])
        result = peak_of(*waiting, result)
        out[pl.ds(number * GROUP, GROUP)] = result[:, :count]
        return carry

    repeat(own // GROUP, block, 0)


def swap(array, axis, bits):
    return lax.ppermute(array, axis, [(i, i ^ bits) for i in range(lax.axis_size(axis))])


def on_device(strain, templates, cutoff):
    tm, devices = lax.axis_size("tm"), lax.axis_size("tm") * lax.axis_size("tmpl")
    size = strain.shape[0] // HOP
    segs = devices * size
    own = segs // tm
    count = templates.shape[1]
    vmem = pl.BlockSpec(memory_space=pltpu.VMEM)
    params = pltpu.CompilerParams(vmem_limit_bytes=40 * 1024 * 1024)
    f32 = jnp.float32

    chunk = strain.reshape(1, size * ROWS, LANES)
    copies = jnp.broadcast_to(chunk, (devices // 2, size * ROWS, LANES))
    copies, held = lax.optimization_barrier((copies, templates))
    copies = copies.reshape(devices, size * ROWS // 2, LANES)
    mine = lax.all_to_all(copies, ("tm", "tmpl"), split_axis=0, concat_axis=0, tiled=True)
    blocks = [swap(held, "tm", other) for other in range(1, tm)]
    mine, *blocks = lax.optimization_barrier((mine, *blocks))
    others = swap(mine, "tmpl", 1)
    blocks = [held] + blocks
    narrow, broad, energy = tables()
    narrow, broad = jnp.asarray(narrow), jnp.asarray(broad)
    square = (2 * GROUP * FINE, 2 * GROUP * ROWS)
    bank, first, third = pl.pallas_call(
        functools.partial(bank_kernel, tm),
        out_shape=(
            jax.ShapeDtypeStruct((2, count, ROWS, LANES), f32),
            jax.ShapeDtypeStruct((2,) + square, jnp.bfloat16),
            jax.ShapeDtypeStruct(square, jnp.bfloat16),
        ),
        in_specs=[vmem] * (tm + 2),
        out_specs=(vmem,) * 3,
        scratch_shapes=[pltpu.VMEM((ROWS, count, 2 * LANES), jnp.bfloat16)],
        compiler_params=params,
        cost_estimate=pl.CostEstimate(flops=0, bytes_accessed=2500000, transcendentals=0),
        name="bank",
    )(*blocks, cutoff.reshape(1, count), narrow)
    return pl.pallas_call(
        functools.partial(filter_kernel, energy),
        out_shape=jax.ShapeDtypeStruct((own, count), f32),
        in_specs=[vmem] * 7,
        out_specs=vmem,
        scratch_shapes=[
            pltpu.VMEM((segs * FINE, LANES), f32),
            pltpu.VMEM((devices, 2, size * ROWS // 2, LANES), f32),
        ],
        compiler_params=params,
        name="matched_filter",
    )(mine, others, bank, first, third, narrow, broad)


def solution(mesh):
    in_specs = (P(("tm", "tmpl")), P(None, "tmpl", "tm"), P("tmpl"))
    out_specs = P("tm", "tmpl")
    return jax.shard_map(
        on_device, mesh=mesh, in_specs=in_specs, out_specs=out_specs, check_vma=False
    )
```

```python
import functools
import math

import jax
import jax.numpy as jnp
import ml_dtypes
import numpy as np
from jax import lax
from jax.experimental import pallas as pl
from jax.experimental.pallas import tpu as pltpu
from jax.sharding import PartitionSpec as P

NFFT = 4096
BINS = 2048
HOP = 2048
LANES = 128
ROWS = HOP // LANES
FINE = 32
GROUP = 8
FLOOR = 1e-6

ROOT_SCALE = {128: 1.66575, 64: 1.66575, 32: 1.6245, 16: 1.6245, 8: 1.6245}


def root_order(index, period):
    return period // math.gcd(int(index), period)


def row_scale(count, period):
    return np.array([ROOT_SCALE.get(root_order(i, period), 1.0) for i in range(count)])


def as_bf16(table):
    return np.asarray(table, np.float32).astype(ml_dtypes.bfloat16)


def two_parts(table):
    high = as_bf16(table)
    low = as_bf16(np.asarray(table, np.float64) - high.astype(np.float64))
    return high, low


def turn(left, right, period):
    angle = 2.0 * np.pi * (np.outer(left, right) % period) / period
    return np.cos(angle), np.sin(angle)


@functools.lru_cache(maxsize=None)
def tables():
    fine, wide, rows = np.arange(FINE), np.arange(LANES), np.arange(ROWS)
    window = 0.5 - 0.5 * np.cos(2.0 * np.pi * np.arange(NFFT) / NFFT)
    cos, sin = turn(fine, fine, FINE)
    first_high, first_low = two_parts(np.tile(np.concatenate([cos, -sin]), (1, GROUP)))
    fwd_cos, fwd_sin = turn(fine, wide, NFFT)
    f_order = np.array([4 * d + g for g in range(4) for d in range(ROWS)])
    cos, sin = turn(wide, f_order, LANES)
    second_high, second_low = two_parts(np.block([[cos, -sin], [sin, cos]]))
    scale_q, scale_c = row_scale(FINE, FINE), row_scale(LANES, LANES)
    cos, sin = turn(fine, rows, FINE)
    cos, sin = np.tile(cos * scale_q[:, None], (1, GROUP)), np.tile(sin * scale_q[:, None], (1, GROUP))
    third = np.block([[cos, -sin], [sin, cos]])
    inv_cos, inv_sin = turn(fine, wide, NFFT)
    undo = 1.0 / (scale_q[:, None] * scale_c[None, :])
    cos, sin = turn(wide, wide, LANES)
    cos, sin = cos * scale_c[:, None], sin * scale_c[:, None]
    fourth = np.block([[cos, sin], [-sin, cos]])
    narrow = np.concatenate(
        [first_high, first_low, as_bf16(third), np.concatenate([second_high, second_low], axis=1), as_bf16(fourth)]
    )
    broad = np.concatenate([window.reshape(FINE, LANES), fwd_cos, fwd_sin, inv_cos * undo, inv_sin * undo])
    return narrow, np.asarray(broad, np.float32), float((window * window).sum())


def dot(left, right):
    return jnp.dot(left, right, preferred_element_type=jnp.float32)


def split(value):
    high = value.astype(jnp.bfloat16)
    return high, (value - high.astype(jnp.float32)).astype(jnp.bfloat16)


def repeat(count, body, carry):
    if count <= 8:
        for step in range(count):
            carry = body(step, carry)
        return carry
    return lax.fori_loop(0, count, body, carry)


def block_diagonal(rows, width):
    lane = lax.broadcasted_iota(jnp.int32, rows.shape, 1)
    owner = lax.rem(lane // width, GROUP)
    return jnp.concatenate(
        [jnp.where(owner == s, rows, jnp.zeros_like(rows)) for s in range(GROUP)], axis=0
    )


def natural(flipped, at, source):
    part = lax.broadcasted_iota(jnp.int32, (ROWS, LANES), 1) // FINE
    result = None
    for g in range(4):
        piece = flipped[at + g * ROWS:at + (g + 1) * ROWS]
        if source is not None and g != source:
            piece = pltpu.roll(piece, ((g - source) % 4) * FINE, 1)
        result = piece if g == 0 else jnp.where(part == g, piece, result)
    return result


def bank_kernel(devices, *refs):
    blocks = refs[:devices]
    cutoff, bank, gathered = refs[devices:]
    rank = lax.axis_index("tm")
    _, count, width = blocks[0].shape
    shape = (count, count)
    same = lax.broadcasted_iota(jnp.int32, shape, 0) == lax.broadcasted_iota(jnp.int32, shape, 1)
    column = jnp.sum(jnp.where(same, cutoff[...], 0), axis=1, keepdims=True)
    lane = lax.broadcasted_iota(jnp.int32, (count, LANES), 1)
    for other, block in enumerate(blocks):
        first = (rank ^ other) * (width // LANES)
        for at in range(width // LANES):
            lanes = slice(at * LANES, (at + 1) * LANES)
            keep = lane + (first + at) * LANES < column
            both = [jnp.where(keep, block[i, :, lanes].astype(jnp.float32), 0.0) for i in range(2)]
            gathered[first + at] = jnp.concatenate(both, axis=1).astype(jnp.bfloat16)
    shape = (count * ROWS, count * ROWS)
    to, source = lax.broadcasted_iota(jnp.int32, shape, 0), lax.broadcasted_iota(jnp.int32, shape, 1)
    order = (source == (to % ROWS) * count + to // ROWS).astype(jnp.float32).astype(jnp.bfloat16)
    value = dot(order, gathered[...].reshape(ROWS * count, 2 * LANES))
    bank[0] = value[:, :LANES].reshape(count, ROWS, LANES)
    bank[1] = value[:, LANES:].reshape(count, ROWS, LANES)


def filter_kernel(energy, mine, others, bank, narrow, broad, out, spec, halves):
    core = lax.rem(lax.axis_index("tmpl"), 2)
    halves[:, core] = mine[...]
    halves[:, 1 - core] = others[...]
    segs = 2 * mine.shape[0] * mine.shape[1] // ROWS
    record = halves.reshape(segs, ROWS, LANES)
    own, count = out.shape
    half = GROUP * FINE
    w_low, w_high = broad[:ROWS][None], broad[ROWS:FINE][None]
    fwd_cos, fwd_sin = broad[FINE:2 * FINE][None], broad[2 * FINE:3 * FINE][None]
    inv_cos, inv_sin = broad[3 * FINE:4 * FINE][None], broad[4 * FINE:5 * FINE][None]
    high, low = narrow[:2 * FINE], narrow[2 * FINE:4 * FINE]
    spread = lambda part: jnp.concatenate(
        [block_diagonal(part[:FINE], part.shape[1] // GROUP), block_diagonal(part[FINE:], part.shape[1] // GROUP)]
    )
    first_high = spread(high)
    first = jnp.concatenate([first_high, first_high, spread(low)], axis=1)
    third_rows = narrow[4 * FINE:6 * FINE]
    third = jnp.concatenate([block_diagonal(third_rows[:FINE], ROWS), block_diagonal(third_rows[FINE:], ROWS)])
    second = slice(6 * FINE, 6 * FINE + 2 * LANES)
    fourth = slice(6 * FINE + 2 * LANES, 6 * FINE + 4 * LANES)

    def frames(start, last):
        here = record[pl.ds(start, GROUP)]
        if last:
            after = jnp.concatenate([record[pl.ds(start + 1, GROUP - 1)], record[pl.ds(0, 1)]], axis=0)
        else:
            after = record[pl.ds(start + 1, GROUP)]
        both = jnp.concatenate([here * w_low, after * w_high], axis=1)
        return both.reshape(half, LANES)

    def first_product(start, last):
        pair = jnp.concatenate([frames(start, False), frames(start + GROUP, last)], axis=1)
        high, low = split(pair)
        return dot(first, jnp.concatenate([high, low, high], axis=0))

    def second_product(step, h):
        re = step[:half, h * LANES:(h + 1) * LANES].reshape(GROUP, FINE, LANES)
        im = step[half:, h * LANES:(h + 1) * LANES].reshape(GROUP, FINE, LANES)
        turned = jnp.concatenate([re * fwd_cos + im * fwd_sin, im * fwd_cos - re * fwd_sin], axis=2)
        high, low = split(turned.reshape(half, 2 * LANES))
        return dot(jnp.concatenate([high, low], axis=1), jnp.concatenate([narrow[second]] * 2, axis=0))

    def add_power(both, at, power):
        value = both[:, :LANES] + both[:, LANES:]
        spec[pl.ds(at * FINE, half)] = value
        return power + jnp.sum((value * value).reshape(GROUP, FINE, LANES), axis=0)

    def whole(start, last, power):
        step = first_product(start, last)
        for h in range(2):
            power = add_power(second_product(step, h), start + h * GROUP, power)
        return power

    power = jnp.zeros((FINE, LANES), jnp.float32)
    pairs = segs // (2 * GROUP)
    stride = 2 * GROUP
    if pairs <= 4:
        steps = [first_product(i * stride, i == pairs - 1) for i in range(pairs)]
        waiting = None
        for i, step in enumerate(steps):
            for h in range(2):
                both = second_product(step, h)
                if waiting is not None:
                    power = add_power(*waiting, power)
                waiting = (both, i * stride + h * GROUP)
        power = add_power(*waiting, power)
    else:
        power = lax.fori_loop(0, pairs - 1, lambda i, p: whole(i * stride, False, p), power)
        power = whole((pairs - 1) * stride, True, power)
    power = power + pltpu.roll(power, LANES // 2, 1)
    density = power / (segs * energy) + FLOOR
    density = natural(jnp.concatenate([density] * 4, axis=0).T, 0, None)
    inverse_density = 1.0 / density

    place = lax.axis_index("tm") * own
    column = lax.broadcasted_iota(jnp.int32, (GROUP, LANES), 1)

    def block(number, carry):
        at = pl.multiple_of((place + number * GROUP) * FINE, half)
        values = spec[pl.ds(at, half)].reshape(2, 4 * FINE, LANES)
        re_parts, im_parts = [], []
        for side in range(2):
            flipped = values[side].T
            for s in range(4):
                re_parts.append(natural(flipped, 0, s))
                im_parts.append(natural(flipped, LANES // 2, s))
        white_re, white_im = (
            (jnp.stack(parts) / density[None]).astype(jnp.bfloat16).astype(jnp.float32)
            for parts in (re_parts, im_parts)
        )

        def products_of(step):
            sides, norms = [], []
            for m in (2 * step, 2 * step + 1):
                h_re, h_im = bank[0, m], bank[1, m]
                norms.append(jnp.sum((h_re * h_re + h_im * h_im) * inverse_density, keepdims=True))
                c_re = h_re[None] * white_re + h_im[None] * white_im
                c_im = h_re[None] * white_im - h_im[None] * white_re
                both = jnp.concatenate([c_re, c_im], axis=0).reshape(2 * GROUP * ROWS, LANES)
                sides.append(both.astype(jnp.bfloat16))
            return jnp.concatenate(sides, axis=1), norms

        def wave_of(section, side):
            re = section[:half, side * LANES:(side + 1) * LANES].reshape(GROUP, FINE, LANES)
            im = section[half:, side * LANES:(side + 1) * LANES].reshape(GROUP, FINE, LANES)
            turned = jnp.concatenate([re * inv_cos - im * inv_sin, re * inv_sin + im * inv_cos], axis=2)
            return dot(turned.reshape(half, 2 * LANES).astype(jnp.bfloat16), narrow[fourth])

        def peak_of(m, wave, norm, result):
            square = wave[:, :LANES] * wave[:, :LANES] + wave[:, LANES:] * wave[:, LANES:]
            top = jnp.max(jnp.max(square.reshape(GROUP, FINE, LANES), axis=1), axis=1, keepdims=True)
            value = jnp.sqrt(top) / (jnp.sqrt(norm) * math.sqrt(energy))
            return jnp.where(column == m, value, result)

        result = jnp.zeros((GROUP, LANES), jnp.float32)
        steps = count // 2
        made = [products_of(step) for step in range(min(2, steps))]
        ready, waiting = dot(third, made[0][0]), None
        for step in range(steps):
            section, norms = ready, made[step][1]
            if step + 2 < steps:
                made.append(products_of(step + 2))
            if step + 1 < steps:
                ready = dot(third, made[step + 1][0])
            for side in range(2):
                wave = wave_of(section, side)
                if waiting is not None:
                    result = peak_of(*waiting, result)
                waiting = (2 * step + side, wave, norms[side])
        result = peak_of(*waiting, result)
        out[pl.ds(number * GROUP, GROUP)] = result[:, :count]
        return carry

    repeat(own // GROUP, block, 0)


def swap(array, axis, bits):
    return lax.ppermute(array, axis, [(i, i ^ bits) for i in range(lax.axis_size(axis))])


def on_device(strain, templates, cutoff):
    tm, devices = lax.axis_size("tm"), lax.axis_size("tm") * lax.axis_size("tmpl")
    size = strain.shape[0] // HOP
    segs = devices * size
    own = segs // tm
    count = templates.shape[1]
    vmem = pl.BlockSpec(memory_space=pltpu.VMEM)
    params = pltpu.CompilerParams(vmem_limit_bytes=40 * 1024 * 1024)
    f32 = jnp.float32

    chunk = strain.reshape(1, size * ROWS, LANES)
    copies = jnp.broadcast_to(chunk, (devices // 2, size * ROWS, LANES))
    copies, held = lax.optimization_barrier((copies, templates))
    copies = copies.reshape(devices, size * ROWS // 2, LANES)
    mine = lax.all_to_all(copies, ("tm", "tmpl"), split_axis=0, concat_axis=0, tiled=True)
    blocks = [swap(held, "tm", other) for other in range(1, tm)]
    mine, *blocks = lax.optimization_barrier((mine, *blocks))
    others = swap(mine, "tmpl", 1)
    blocks = [held] + blocks
    bank = pl.pallas_call(
        functools.partial(bank_kernel, tm),
        out_shape=jax.ShapeDtypeStruct((2, count, ROWS, LANES), f32),
        in_specs=[vmem] * (tm + 1),
        out_specs=vmem,
        scratch_shapes=[pltpu.VMEM((ROWS, count, 2 * LANES), jnp.bfloat16)],
        compiler_params=params,
        cost_estimate=pl.CostEstimate(flops=0, bytes_accessed=2500000, transcendentals=0),
        name="bank",
    )(*blocks, cutoff.reshape(1, count))
    narrow, broad, energy = tables()
    return pl.pallas_call(
        functools.partial(filter_kernel, energy),
        out_shape=jax.ShapeDtypeStruct((own, count), f32),
        in_specs=[vmem] * 5,
        out_specs=vmem,
        scratch_shapes=[
            pltpu.VMEM((segs * FINE, LANES), f32),
            pltpu.VMEM((devices, 2, size * ROWS // 2, LANES), f32),
        ],
        compiler_params=params,
        name="matched_filter",
    )(mine, others, bank, jnp.asarray(narrow), jnp.asarray(broad))


def solution(mesh):
    in_specs = (P(("tm", "tmpl")), P(None, "tmpl", "tm"), P("tmpl"))
    out_specs = P("tm", "tmpl")
    return jax.shard_map(
        on_device, mesh=mesh, in_specs=in_specs, out_specs=out_specs, check_vma=False
    )
```

```python
import functools
import math

import jax
import jax.numpy as jnp
import ml_dtypes
import numpy as np
from jax import lax
from jax.experimental import pallas as pl
from jax.experimental.pallas import tpu as pltpu
from jax.sharding import PartitionSpec as P

NFFT = 4096
BINS = 2048
HOP = 2048
LANES = 128
ROWS = HOP // LANES
FINE = 32
GROUP = 8
FLOOR = 1e-6

ROOT_SCALE = {128: 1.66575, 64: 1.66575, 32: 1.6245, 16: 1.6245, 8: 1.6245}


def root_order(index, period):
    return period // math.gcd(int(index), period)


def row_scale(count, period):
    return np.array([ROOT_SCALE.get(root_order(i, period), 1.0) for i in range(count)])


def as_bf16(table):
    return np.asarray(table, np.float32).astype(ml_dtypes.bfloat16)


def two_parts(table):
    high = as_bf16(table)
    low = as_bf16(np.asarray(table, np.float64) - high.astype(np.float64))
    return high, low


def turn(left, right, period):
    angle = 2.0 * np.pi * (np.outer(left, right) % period) / period
    return np.cos(angle), np.sin(angle)


@functools.lru_cache(maxsize=None)
def tables():
    fine, wide, rows = np.arange(FINE), np.arange(LANES), np.arange(ROWS)
    window = 0.5 - 0.5 * np.cos(2.0 * np.pi * np.arange(NFFT) / NFFT)
    cos, sin = turn(fine, fine, FINE)
    first_high, first_low = two_parts(np.tile(np.concatenate([cos, -sin]), (1, GROUP)))
    fwd_cos, fwd_sin = turn(fine, wide, NFFT)
    f_order = np.array([4 * d + g for g in range(4) for d in range(ROWS)])
    cos, sin = turn(wide, f_order, LANES)
    second_high, second_low = two_parts(np.block([[cos, -sin], [sin, cos]]))
    scale_q, scale_c = row_scale(FINE, FINE), row_scale(LANES, LANES)
    cos, sin = turn(fine, rows, FINE)
    cos, sin = np.tile(cos * scale_q[:, None], (1, GROUP)), np.tile(sin * scale_q[:, None], (1, GROUP))
    third = np.block([[cos, -sin], [sin, cos]])
    inv_cos, inv_sin = turn(fine, wide, NFFT)
    undo = 1.0 / (scale_q[:, None] * scale_c[None, :])
    cos, sin = turn(wide, wide, LANES)
    cos, sin = cos * scale_c[:, None], sin * scale_c[:, None]
    fourth = np.block([[cos, sin], [-sin, cos]])
    narrow = np.concatenate(
        [first_high, first_low, as_bf16(third), np.concatenate([second_high, second_low], axis=1), as_bf16(fourth)]
    )
    broad = np.concatenate([window.reshape(FINE, LANES), fwd_cos, fwd_sin, inv_cos * undo, inv_sin * undo])
    return narrow, np.asarray(broad, np.float32), float((window * window).sum())


def dot(left, right):
    return jnp.dot(left, right, preferred_element_type=jnp.float32)


def split(value):
    high = value.astype(jnp.bfloat16)
    return high, (value - high.astype(jnp.float32)).astype(jnp.bfloat16)


def repeat(count, body, carry):
    if count <= 8:
        for step in range(count):
            carry = body(step, carry)
        return carry
    return lax.fori_loop(0, count, body, carry)


def block_diagonal(rows, width):
    lane = lax.broadcasted_iota(jnp.int32, rows.shape, 1)
    owner = lax.rem(lane // width, GROUP)
    return jnp.concatenate(
        [jnp.where(owner == s, rows, jnp.zeros_like(rows)) for s in range(GROUP)], axis=0
    )


def natural(flipped, at, source):
    part = lax.broadcasted_iota(jnp.int32, (ROWS, LANES), 1) // FINE
    result = None
    for g in range(4):
        piece = flipped[at + g * ROWS:at + (g + 1) * ROWS]
        if source is not None and g != source:
            piece = pltpu.roll(piece, ((g - source) % 4) * FINE, 1)
        result = piece if g == 0 else jnp.where(part == g, piece, result)
    return result


def bank_kernel(devices, *refs):
    blocks = refs[:devices]
    cutoff, bank, gathered = refs[devices:]
    rank = lax.axis_index("tm")
    _, count, width = blocks[0].shape
    shape = (count, count)
    same = lax.broadcasted_iota(jnp.int32, shape, 0) == lax.broadcasted_iota(jnp.int32, shape, 1)
    column = jnp.sum(jnp.where(same, cutoff[...], 0), axis=1, keepdims=True)
    lane = lax.broadcasted_iota(jnp.int32, (count, LANES), 1)
    for other, block in enumerate(blocks):
        first = (rank ^ other) * (width // LANES)
        for at in range(width // LANES):
            lanes = slice(at * LANES, (at + 1) * LANES)
            keep = lane + (first + at) * LANES < column
            both = [jnp.where(keep, block[i, :, lanes].astype(jnp.float32), 0.0) for i in range(2)]
            gathered[first + at] = jnp.concatenate(both, axis=1).astype(jnp.bfloat16)
    shape = (count * ROWS, count * ROWS)
    to, source = lax.broadcasted_iota(jnp.int32, shape, 0), lax.broadcasted_iota(jnp.int32, shape, 1)
    order = (source == (to % ROWS) * count + to // ROWS).astype(jnp.float32).astype(jnp.bfloat16)
    value = dot(order, gathered[...].reshape(ROWS * count, 2 * LANES))
    bank[0] = value[:, :LANES].reshape(count, ROWS, LANES)
    bank[1] = value[:, LANES:].reshape(count, ROWS, LANES)


def filter_kernel(energy, mine, others, bank, narrow, broad, out, spec, halves):
    core = lax.rem(lax.axis_index("tmpl"), 2)
    halves[:, core] = mine[...]
    halves[:, 1 - core] = others[...]
    segs = 2 * mine.shape[0] * mine.shape[1] // ROWS
    record = halves.reshape(segs, ROWS, LANES)
    own, count = out.shape
    half = GROUP * FINE
    w_low, w_high = broad[:ROWS][None], broad[ROWS:FINE][None]
    fwd_cos, fwd_sin = broad[FINE:2 * FINE][None], broad[2 * FINE:3 * FINE][None]
    inv_cos, inv_sin = broad[3 * FINE:4 * FINE][None], broad[4 * FINE:5 * FINE][None]
    high, low = narrow[:2 * FINE], narrow[2 * FINE:4 * FINE]
    spread = lambda part: jnp.concatenate(
        [block_diagonal(part[:FINE], part.shape[1] // GROUP), block_diagonal(part[FINE:], part.shape[1] // GROUP)]
    )
    first_high = spread(high)
    first = jnp.concatenate([first_high, first_high, spread(low)], axis=1)
    third_rows = narrow[4 * FINE:6 * FINE]
    third = jnp.concatenate([block_diagonal(third_rows[:FINE], ROWS), block_diagonal(third_rows[FINE:], ROWS)])
    second = slice(6 * FINE, 6 * FINE + 2 * LANES)
    fourth = slice(6 * FINE + 2 * LANES, 6 * FINE + 4 * LANES)

    def frames(start, last):
        here = record[pl.ds(start, GROUP)]
        if last:
            after = jnp.concatenate([record[pl.ds(start + 1, GROUP - 1)], record[pl.ds(0, 1)]], axis=0)
        else:
            after = record[pl.ds(start + 1, GROUP)]
        both = jnp.concatenate([here * w_low, after * w_high], axis=1)
        return both.reshape(half, LANES)

    def first_product(start, last):
        pair = jnp.concatenate([frames(start, False), frames(start + GROUP, last)], axis=1)
        high, low = split(pair)
        return dot(first, jnp.concatenate([high, low, high], axis=0))

    def second_product(step, h):
        re = step[:half, h * LANES:(h + 1) * LANES].reshape(GROUP, FINE, LANES)
        im = step[half:, h * LANES:(h + 1) * LANES].reshape(GROUP, FINE, LANES)
        turned = jnp.concatenate([re * fwd_cos + im * fwd_sin, im * fwd_cos - re * fwd_sin], axis=2)
        high, low = split(turned.reshape(half, 2 * LANES))
        return dot(jnp.concatenate([high, low], axis=1), jnp.concatenate([narrow[second]] * 2, axis=0))

    def add_power(both, at, power):
        value = both[:, :LANES] + both[:, LANES:]
        spec[pl.ds(at * FINE, half)] = value
        return power + jnp.sum((value * value).reshape(GROUP, FINE, LANES), axis=0)

    def whole(start, last, power):
        step = first_product(start, last)
        for h in range(2):
            power = add_power(second_product(step, h), start + h * GROUP, power)
        return power

    power = jnp.zeros((FINE, LANES), jnp.float32)
    pairs = segs // (2 * GROUP)
    stride = 2 * GROUP
    if pairs <= 4:
        steps = [first_product(i * stride, i == pairs - 1) for i in range(pairs)]
        waiting = None
        for i, step in enumerate(steps):
            for h in range(2):
                both = second_product(step, h)
                if waiting is not None:
                    power = add_power(*waiting, power)
                waiting = (both, i * stride + h * GROUP)
        power = add_power(*waiting, power)
    else:
        power = lax.fori_loop(0, pairs - 1, lambda i, p: whole(i * stride, False, p), power)
        power = whole((pairs - 1) * stride, True, power)
    power = power + pltpu.roll(power, LANES // 2, 1)
    density = power / (segs * energy) + FLOOR
    density = natural(jnp.concatenate([density] * 4, axis=0).T, 0, None)
    inverse_density = 1.0 / density

    place = lax.axis_index("tm") * own
    column = lax.broadcasted_iota(jnp.int32, (GROUP, LANES), 1)

    def block(number, carry):
        at = pl.multiple_of((place + number * GROUP) * FINE, half)
        values = spec[pl.ds(at, half)].reshape(2, 4 * FINE, LANES)
        re_parts, im_parts = [], []
        for side in range(2):
            flipped = values[side].T
            for s in range(4):
                re_parts.append(natural(flipped, 0, s))
                im_parts.append(natural(flipped, LANES // 2, s))
        white_re, white_im = (
            (jnp.stack(parts) / density[None]).astype(jnp.bfloat16).astype(jnp.float32)
            for parts in (re_parts, im_parts)
        )

        def section_of(step):
            sides, norms = [], []
            for m in (2 * step, 2 * step + 1):
                h_re, h_im = bank[0, m], bank[1, m]
                norms.append(jnp.sum((h_re * h_re + h_im * h_im) * inverse_density, keepdims=True))
                c_re = h_re[None] * white_re + h_im[None] * white_im
                c_im = h_re[None] * white_im - h_im[None] * white_re
                both = jnp.concatenate([c_re, c_im], axis=0).reshape(2 * GROUP * ROWS, LANES)
                sides.append(both.astype(jnp.bfloat16))
            return dot(third, jnp.concatenate(sides, axis=1)), norms

        def waves_of(section):
            sides = []
            for side in range(2):
                re = section[:half, side * LANES:(side + 1) * LANES].reshape(GROUP, FINE, LANES)
                im = section[half:, side * LANES:(side + 1) * LANES].reshape(GROUP, FINE, LANES)
                turned = jnp.concatenate([re * inv_cos - im * inv_sin, re * inv_sin + im * inv_cos], axis=2)
                sides.append(turned.reshape(half, 2 * LANES).astype(jnp.bfloat16))
            return dot(jnp.concatenate(sides, axis=0), narrow[fourth])

        def peak_of(m, wave, norm, result):
            square = wave[:, :LANES] * wave[:, :LANES] + wave[:, LANES:] * wave[:, LANES:]
            top = jnp.max(jnp.max(square.reshape(GROUP, FINE, LANES), axis=1), axis=1, keepdims=True)
            value = jnp.sqrt(top) / (jnp.sqrt(norm) * math.sqrt(energy))
            return jnp.where(column == m, value, result)

        result = jnp.zeros((GROUP, LANES), jnp.float32)
        ready, waiting = section_of(0), None
        for step in range(count // 2):
            section, norms = ready
            if step + 1 < count // 2:
                ready = section_of(step + 1)
            waves = waves_of(section)
            if waiting is not None:
                for ready_peak in waiting:
                    result = peak_of(*ready_peak, result)
            waiting = [(2 * step + i, waves[i * half:(i + 1) * half], norms[i]) for i in range(2)]
        for ready_peak in waiting:
            result = peak_of(*ready_peak, result)
        out[pl.ds(number * GROUP, GROUP)] = result[:, :count]
        return carry

    repeat(own // GROUP, block, 0)


def swap(array, axis, bits):
    return lax.ppermute(array, axis, [(i, i ^ bits) for i in range(lax.axis_size(axis))])


def on_device(strain, templates, cutoff):
    tm, devices = lax.axis_size("tm"), lax.axis_size("tm") * lax.axis_size("tmpl")
    size = strain.shape[0] // HOP
    segs = devices * size
    own = segs // tm
    count = templates.shape[1]
    vmem = pl.BlockSpec(memory_space=pltpu.VMEM)
    params = pltpu.CompilerParams(vmem_limit_bytes=40 * 1024 * 1024)
    f32 = jnp.float32

    chunk = strain.reshape(1, size * ROWS, LANES)
    copies = jnp.broadcast_to(chunk, (devices // 2, size * ROWS, LANES))
    copies, held = lax.optimization_barrier((copies, templates))
    copies = copies.reshape(devices, size * ROWS // 2, LANES)
    mine = lax.all_to_all(copies, ("tm", "tmpl"), split_axis=0, concat_axis=0, tiled=True)
    blocks = [swap(held, "tm", other) for other in range(1, tm)]
    mine, *blocks = lax.optimization_barrier((mine, *blocks))
    others = swap(mine, "tmpl", 1)
    blocks = [held] + blocks
    bank = pl.pallas_call(
        functools.partial(bank_kernel, tm),
        out_shape=jax.ShapeDtypeStruct((2, count, ROWS, LANES), f32),
        in_specs=[vmem] * (tm + 1),
        out_specs=vmem,
        scratch_shapes=[pltpu.VMEM((ROWS, count, 2 * LANES), jnp.bfloat16)],
        compiler_params=params,
        cost_estimate=pl.CostEstimate(flops=0, bytes_accessed=2500000, transcendentals=0),
        name="bank",
    )(*blocks, cutoff.reshape(1, count))
    narrow, broad, energy = tables()
    return pl.pallas_call(
        functools.partial(filter_kernel, energy),
        out_shape=jax.ShapeDtypeStruct((own, count), f32),
        in_specs=[vmem] * 5,
        out_specs=vmem,
        scratch_shapes=[
            pltpu.VMEM((segs * FINE, LANES), f32),
            pltpu.VMEM((devices, 2, size * ROWS // 2, LANES), f32),
        ],
        compiler_params=params,
        name="matched_filter",
    )(mine, others, bank, jnp.asarray(narrow), jnp.asarray(broad))


def solution(mesh):
    in_specs = (P(("tm", "tmpl")), P(None, "tmpl", "tm"), P("tmpl"))
    out_specs = P("tm", "tmpl")
    return jax.shard_map(
        on_device, mesh=mesh, in_specs=in_specs, out_specs=out_specs, check_vma=False
    )
```

```python
import functools
import math

import jax
import jax.numpy as jnp
import ml_dtypes
import numpy as np
from jax import lax
from jax.experimental import pallas as pl
from jax.experimental.pallas import tpu as pltpu
from jax.sharding import PartitionSpec as P

NFFT = 4096
BINS = 2048
HOP = 2048
LANES = 128
ROWS = HOP // LANES
FINE = 32
GROUP = 8
FLOOR = 1e-6

ROOT_SCALE = {128: 1.66575, 64: 1.66575, 32: 1.6245, 16: 1.6245, 8: 1.6245}


def root_order(index, period):
    return period // math.gcd(int(index), period)


def row_scale(count, period):
    return np.array([ROOT_SCALE.get(root_order(i, period), 1.0) for i in range(count)])


def as_bf16(table):
    return np.asarray(table, np.float32).astype(ml_dtypes.bfloat16)


def two_parts(table):
    high = as_bf16(table)
    low = as_bf16(np.asarray(table, np.float64) - high.astype(np.float64))
    return high, low


def turn(left, right, period):
    angle = 2.0 * np.pi * (np.outer(left, right) % period) / period
    return np.cos(angle), np.sin(angle)


@functools.lru_cache(maxsize=None)
def tables():
    fine, wide, rows = np.arange(FINE), np.arange(LANES), np.arange(ROWS)
    window = 0.5 - 0.5 * np.cos(2.0 * np.pi * np.arange(NFFT) / NFFT)
    cos, sin = turn(fine, fine, FINE)
    first_high, first_low = two_parts(np.tile(np.concatenate([cos, -sin]), (1, GROUP)))
    fwd_cos, fwd_sin = turn(fine, wide, NFFT)
    f_order = np.array([4 * d + g for g in range(4) for d in range(ROWS)])
    cos, sin = turn(wide, f_order, LANES)
    second_high, second_low = two_parts(np.block([[cos, -sin], [sin, cos]]))
    scale_q, scale_c = row_scale(FINE, FINE), row_scale(LANES, LANES)
    cos, sin = turn(fine, rows, FINE)
    cos, sin = np.tile(cos * scale_q[:, None], (1, GROUP)), np.tile(sin * scale_q[:, None], (1, GROUP))
    third = np.block([[cos, -sin], [sin, cos]])
    inv_cos, inv_sin = turn(fine, wide, NFFT)
    undo = 1.0 / (scale_q[:, None] * scale_c[None, :])
    cos, sin = turn(wide, wide, LANES)
    cos, sin = cos * scale_c[:, None], sin * scale_c[:, None]
    fourth = np.block([[cos, sin], [-sin, cos]])
    narrow = np.concatenate(
        [first_high, first_low, as_bf16(third), np.concatenate([second_high, second_low], axis=1), as_bf16(fourth)]
    )
    broad = np.concatenate([window.reshape(FINE, LANES), fwd_cos, fwd_sin, inv_cos * undo, inv_sin * undo])
    return narrow, np.asarray(broad, np.float32), float((window * window).sum())


def dot(left, right):
    return jnp.dot(left, right, preferred_element_type=jnp.float32)


def split(value):
    high = value.astype(jnp.bfloat16)
    return high, (value - high.astype(jnp.float32)).astype(jnp.bfloat16)


def repeat(count, body, carry):
    if count <= 8:
        for step in range(count):
            carry = body(step, carry)
        return carry
    return lax.fori_loop(0, count, body, carry)


def block_diagonal(rows, width):
    lane = lax.broadcasted_iota(jnp.int32, rows.shape, 1)
    owner = lax.rem(lane // width, GROUP)
    return jnp.concatenate(
        [jnp.where(owner == s, rows, jnp.zeros_like(rows)) for s in range(GROUP)], axis=0
    )


def natural(flipped, at, source):
    part = lax.broadcasted_iota(jnp.int32, (ROWS, LANES), 1) // FINE
    result = None
    for g in range(4):
        piece = flipped[at + g * ROWS:at + (g + 1) * ROWS]
        if source is not None and g != source:
            piece = pltpu.roll(piece, ((g - source) % 4) * FINE, 1)
        result = piece if g == 0 else jnp.where(part == g, piece, result)
    return result


def bank_kernel(devices, *refs):
    blocks = refs[:devices]
    cutoff, bank, gathered = refs[devices:]
    rank = lax.axis_index("tm")
    _, count, width = blocks[0].shape
    shape = (count, count)
    same = lax.broadcasted_iota(jnp.int32, shape, 0) == lax.broadcasted_iota(jnp.int32, shape, 1)
    column = jnp.sum(jnp.where(same, cutoff[...], 0), axis=1, keepdims=True)
    lane = lax.broadcasted_iota(jnp.int32, (count, LANES), 1)
    for other, block in enumerate(blocks):
        first = (rank ^ other) * (width // LANES)
        for at in range(width // LANES):
            lanes = slice(at * LANES, (at + 1) * LANES)
            keep = lane + (first + at) * LANES < column
            both = [jnp.where(keep, block[i, :, lanes].astype(jnp.float32), 0.0) for i in range(2)]
            gathered[first + at] = jnp.concatenate(both, axis=1).astype(jnp.bfloat16)
    shape = (count * ROWS, count * ROWS)
    to, source = lax.broadcasted_iota(jnp.int32, shape, 0), lax.broadcasted_iota(jnp.int32, shape, 1)
    order = (source == (to % ROWS) * count + to // ROWS).astype(jnp.float32).astype(jnp.bfloat16)
    value = dot(order, gathered[...].reshape(ROWS * count, 2 * LANES))
    bank[0] = value[:, :LANES].reshape(count, ROWS, LANES)
    bank[1] = value[:, LANES:].reshape(count, ROWS, LANES)


def filter_kernel(energy, mine, others, bank, narrow, broad, out, spec, halves):
    core = lax.rem(lax.axis_index("tmpl"), 2)
    halves[:, core] = mine[...]
    halves[:, 1 - core] = others[...]
    segs = 2 * mine.shape[0] * mine.shape[1] // ROWS
    record = halves.reshape(segs, ROWS, LANES)
    own, count = out.shape
    half = GROUP * FINE
    w_low, w_high = broad[:ROWS][None], broad[ROWS:FINE][None]
    fwd_cos, fwd_sin = broad[FINE:2 * FINE][None], broad[2 * FINE:3 * FINE][None]
    inv_cos, inv_sin = broad[3 * FINE:4 * FINE][None], broad[4 * FINE:5 * FINE][None]
    high, low = narrow[:2 * FINE], narrow[2 * FINE:4 * FINE]
    spread = lambda part: jnp.concatenate(
        [block_diagonal(part[:FINE], part.shape[1] // GROUP), block_diagonal(part[FINE:], part.shape[1] // GROUP)]
    )
    first_high = spread(high)
    first = jnp.concatenate([first_high, first_high, spread(low)], axis=1)
    third_rows = narrow[4 * FINE:6 * FINE]
    third = jnp.concatenate([block_diagonal(third_rows[:FINE], ROWS), block_diagonal(third_rows[FINE:], ROWS)])
    second = slice(6 * FINE, 6 * FINE + 2 * LANES)
    fourth = slice(6 * FINE + 2 * LANES, 6 * FINE + 4 * LANES)

    def frames(start, last):
        here = record[pl.ds(start, GROUP)]
        if last:
            after = jnp.concatenate([record[pl.ds(start + 1, GROUP - 1)], record[pl.ds(0, 1)]], axis=0)
        else:
            after = record[pl.ds(start + 1, GROUP)]
        both = jnp.concatenate([here * w_low, after * w_high], axis=1)
        return both.reshape(half, LANES)

    def first_product(start, last):
        pair = jnp.concatenate([frames(start, False), frames(start + GROUP, last)], axis=1)
        high, low = split(pair)
        return dot(first, jnp.concatenate([high, low, high], axis=0))

    def second_product(step):
        sides = []
        for h in range(2):
            re = step[:half, h * LANES:(h + 1) * LANES].reshape(GROUP, FINE, LANES)
            im = step[half:, h * LANES:(h + 1) * LANES].reshape(GROUP, FINE, LANES)
            turned = jnp.concatenate([re * fwd_cos + im * fwd_sin, im * fwd_cos - re * fwd_sin], axis=2)
            high, low = split(turned.reshape(half, 2 * LANES))
            sides.append(jnp.concatenate([high, low], axis=1))
        return dot(jnp.concatenate(sides, axis=0), jnp.concatenate([narrow[second]] * 2, axis=0))

    def add_power(both, at, power):
        value = both[:, :LANES] + both[:, LANES:]
        spec[pl.ds(at * FINE, 2 * half)] = value
        return power + jnp.sum((value * value).reshape(2 * GROUP, FINE, LANES), axis=0)

    def whole(start, last, power):
        return add_power(second_product(first_product(start, last)), start, power)

    power = jnp.zeros((FINE, LANES), jnp.float32)
    pairs = segs // (2 * GROUP)
    stride = 2 * GROUP
    if pairs <= 4:
        steps = [first_product(i * stride, i == pairs - 1) for i in range(pairs)]
        waiting = None
        for i, step in enumerate(steps):
            both = second_product(step)
            if waiting is not None:
                power = add_power(*waiting, power)
            waiting = (both, i * stride)
        power = add_power(*waiting, power)
    else:
        power = lax.fori_loop(0, pairs - 1, lambda i, p: whole(i * stride, False, p), power)
        power = whole((pairs - 1) * stride, True, power)
    power = power + pltpu.roll(power, LANES // 2, 1)
    density = power / (segs * energy) + FLOOR
    density = natural(jnp.concatenate([density] * 4, axis=0).T, 0, None)
    inverse_density = 1.0 / density

    place = lax.axis_index("tm") * own
    column = lax.broadcasted_iota(jnp.int32, (GROUP, LANES), 1)

    def block(number, carry):
        at = pl.multiple_of((place + number * GROUP) * FINE, half)
        values = spec[pl.ds(at, half)].reshape(2, 4 * FINE, LANES)
        re_parts, im_parts = [], []
        for side in range(2):
            flipped = values[side].T
            for s in range(4):
                re_parts.append(natural(flipped, 0, s))
                im_parts.append(natural(flipped, LANES // 2, s))
        white_re, white_im = (
            (jnp.stack(parts) / density[None]).astype(jnp.bfloat16).astype(jnp.float32)
            for parts in (re_parts, im_parts)
        )

        def section_of(step):
            sides, norms = [], []
            for m in (2 * step, 2 * step + 1):
                h_re, h_im = bank[0, m], bank[1, m]
                norms.append(jnp.sum((h_re * h_re + h_im * h_im) * inverse_density, keepdims=True))
                c_re = h_re[None] * white_re + h_im[None] * white_im
                c_im = h_re[None] * white_im - h_im[None] * white_re
                both = jnp.concatenate([c_re, c_im], axis=0).reshape(2 * GROUP * ROWS, LANES)
                sides.append(both.astype(jnp.bfloat16))
            return dot(third, jnp.concatenate(sides, axis=1)), norms

        def waves_of(section):
            sides = []
            for side in range(2):
                re = section[:half, side * LANES:(side + 1) * LANES].reshape(GROUP, FINE, LANES)
                im = section[half:, side * LANES:(side + 1) * LANES].reshape(GROUP, FINE, LANES)
                turned = jnp.concatenate([re * inv_cos - im * inv_sin, re * inv_sin + im * inv_cos], axis=2)
                sides.append(turned.reshape(half, 2 * LANES).astype(jnp.bfloat16))
            return dot(jnp.concatenate(sides, axis=0), narrow[fourth])

        def peak_of(m, wave, norm, result):
            square = wave[:, :LANES] * wave[:, :LANES] + wave[:, LANES:] * wave[:, LANES:]
            top = jnp.max(jnp.max(square.reshape(GROUP, FINE, LANES), axis=1), axis=1, keepdims=True)
            value = jnp.sqrt(top) / (jnp.sqrt(norm) * math.sqrt(energy))
            return jnp.where(column == m, value, result)

        result = jnp.zeros((GROUP, LANES), jnp.float32)
        ready, waiting = section_of(0), None
        for step in range(count // 2):
            section, norms = ready
            if step + 1 < count // 2:
                ready = section_of(step + 1)
            waves = waves_of(section)
            if waiting is not None:
                for ready_peak in waiting:
                    result = peak_of(*ready_peak, result)
            waiting = [(2 * step + i, waves[i * half:(i + 1) * half], norms[i]) for i in range(2)]
        for ready_peak in waiting:
            result = peak_of(*ready_peak, result)
        out[pl.ds(number * GROUP, GROUP)] = result[:, :count]
        return carry

    repeat(own // GROUP, block, 0)


def swap(array, axis, bits):
    return lax.ppermute(array, axis, [(i, i ^ bits) for i in range(lax.axis_size(axis))])


def on_device(strain, templates, cutoff):
    tm, devices = lax.axis_size("tm"), lax.axis_size("tm") * lax.axis_size("tmpl")
    size = strain.shape[0] // HOP
    segs = devices * size
    own = segs // tm
    count = templates.shape[1]
    vmem = pl.BlockSpec(memory_space=pltpu.VMEM)
    params = pltpu.CompilerParams(vmem_limit_bytes=40 * 1024 * 1024)
    f32 = jnp.float32

    chunk = strain.reshape(1, size * ROWS, LANES)
    copies = jnp.broadcast_to(chunk, (devices // 2, size * ROWS, LANES))
    copies, held = lax.optimization_barrier((copies, templates))
    copies = copies.reshape(devices, size * ROWS // 2, LANES)
    mine = lax.all_to_all(copies, ("tm", "tmpl"), split_axis=0, concat_axis=0, tiled=True)
    blocks = [swap(held, "tm", other) for other in range(1, tm)]
    mine, *blocks = lax.optimization_barrier((mine, *blocks))
    others = swap(mine, "tmpl", 1)
    blocks = [held] + blocks
    bank = pl.pallas_call(
        functools.partial(bank_kernel, tm),
        out_shape=jax.ShapeDtypeStruct((2, count, ROWS, LANES), f32),
        in_specs=[vmem] * (tm + 1),
        out_specs=vmem,
        scratch_shapes=[pltpu.VMEM((ROWS, count, 2 * LANES), jnp.bfloat16)],
        compiler_params=params,
        cost_estimate=pl.CostEstimate(flops=0, bytes_accessed=2500000, transcendentals=0),
        name="bank",
    )(*blocks, cutoff.reshape(1, count))
    narrow, broad, energy = tables()
    return pl.pallas_call(
        functools.partial(filter_kernel, energy),
        out_shape=jax.ShapeDtypeStruct((own, count), f32),
        in_specs=[vmem] * 5,
        out_specs=vmem,
        scratch_shapes=[
            pltpu.VMEM((segs * FINE, LANES), f32),
            pltpu.VMEM((devices, 2, size * ROWS // 2, LANES), f32),
        ],
        compiler_params=params,
        name="matched_filter",
    )(mine, others, bank, jnp.asarray(narrow), jnp.asarray(broad))


def solution(mesh):
    in_specs = (P(("tm", "tmpl")), P(None, "tmpl", "tm"), P("tmpl"))
    out_specs = P("tm", "tmpl")
    return jax.shard_map(
        on_device, mesh=mesh, in_specs=in_specs, out_specs=out_specs, check_vma=False
    )
```

```python
import functools
import math

import jax
import jax.numpy as jnp
import ml_dtypes
import numpy as np
from jax import lax
from jax.experimental import pallas as pl
from jax.experimental.pallas import tpu as pltpu
from jax.sharding import PartitionSpec as P

NFFT = 4096
BINS = 2048
HOP = 2048
LANES = 128
ROWS = HOP // LANES
FINE = 32
GROUP = 8
FLOOR = 1e-6

ROOT_SCALE = {128: 1.66575, 64: 1.66575, 32: 1.6245, 16: 1.6245, 8: 1.6245}


def root_order(index, period):
    return period // math.gcd(int(index), period)


def row_scale(count, period):
    return np.array([ROOT_SCALE.get(root_order(i, period), 1.0) for i in range(count)])


def as_bf16(table):
    return np.asarray(table, np.float32).astype(ml_dtypes.bfloat16)


def two_parts(table):
    high = as_bf16(table)
    low = as_bf16(np.asarray(table, np.float64) - high.astype(np.float64))
    return high, low


def turn(left, right, period):
    angle = 2.0 * np.pi * (np.outer(left, right) % period) / period
    return np.cos(angle), np.sin(angle)


@functools.lru_cache(maxsize=None)
def tables():
    fine, wide, rows = np.arange(FINE), np.arange(LANES), np.arange(ROWS)
    window = 0.5 - 0.5 * np.cos(2.0 * np.pi * np.arange(NFFT) / NFFT)
    cos, sin = turn(fine, fine, FINE)
    first_high, first_low = two_parts(np.tile(np.concatenate([cos, -sin]), (1, GROUP)))
    fwd_cos, fwd_sin = turn(fine, wide, NFFT)
    f_order = np.array([4 * d + g for g in range(4) for d in range(ROWS)])
    cos, sin = turn(wide, f_order, LANES)
    second_high, second_low = two_parts(np.block([[cos, -sin], [sin, cos]]))
    scale_q, scale_c = row_scale(FINE, FINE), row_scale(LANES, LANES)
    cos, sin = turn(fine, rows, FINE)
    cos, sin = np.tile(cos * scale_q[:, None], (1, GROUP)), np.tile(sin * scale_q[:, None], (1, GROUP))
    third = np.block([[cos, -sin], [sin, cos]])
    inv_cos, inv_sin = turn(fine, wide, NFFT)
    undo = 1.0 / (scale_q[:, None] * scale_c[None, :])
    cos, sin = turn(wide, wide, LANES)
    cos, sin = cos * scale_c[:, None], sin * scale_c[:, None]
    fourth = np.block([[cos, sin], [-sin, cos]])
    narrow = np.concatenate(
        [first_high, first_low, as_bf16(third), np.concatenate([second_high, second_low], axis=1), as_bf16(fourth)]
    )
    broad = np.concatenate([window.reshape(FINE, LANES), fwd_cos, fwd_sin, inv_cos * undo, inv_sin * undo])
    return narrow, np.asarray(broad, np.float32), float((window * window).sum())


def dot(left, right):
    return jnp.dot(left, right, preferred_element_type=jnp.float32)


def split(value):
    high = value.astype(jnp.bfloat16)
    return high, (value - high.astype(jnp.float32)).astype(jnp.bfloat16)


def repeat(count, body, carry):
    if count <= 8:
        for step in range(count):
            carry = body(step, carry)
        return carry
    return lax.fori_loop(0, count, body, carry)


def block_diagonal(rows, width):
    lane = lax.broadcasted_iota(jnp.int32, rows.shape, 1)
    owner = lax.rem(lane // width, GROUP)
    return jnp.concatenate(
        [jnp.where(owner == s, rows, jnp.zeros_like(rows)) for s in range(GROUP)], axis=0
    )


def natural(flipped, at, source):
    part = lax.broadcasted_iota(jnp.int32, (ROWS, LANES), 1) // FINE
    result = None
    for g in range(4):
        piece = flipped[at + g * ROWS:at + (g + 1) * ROWS]
        if source is not None and g != source:
            piece = pltpu.roll(piece, ((g - source) % 4) * FINE, 1)
        result = piece if g == 0 else jnp.where(part == g, piece, result)
    return result


def bank_kernel(devices, *refs):
    blocks = refs[:devices]
    cutoff, bank, gathered = refs[devices:]
    rank = lax.axis_index("tm")
    _, count, width = blocks[0].shape
    shape = (count, count)
    same = lax.broadcasted_iota(jnp.int32, shape, 0) == lax.broadcasted_iota(jnp.int32, shape, 1)
    column = jnp.sum(jnp.where(same, cutoff[...], 0), axis=1, keepdims=True)
    lane = lax.broadcasted_iota(jnp.int32, (count, LANES), 1)
    for other, block in enumerate(blocks):
        first = (rank ^ other) * (width // LANES)
        for at in range(width // LANES):
            lanes = slice(at * LANES, (at + 1) * LANES)
            keep = lane + (first + at) * LANES < column
            both = [jnp.where(keep, block[i, :, lanes].astype(jnp.float32), 0.0) for i in range(2)]
            gathered[first + at] = jnp.concatenate(both, axis=1).astype(jnp.bfloat16)
    shape = (count * ROWS, count * ROWS)
    to, source = lax.broadcasted_iota(jnp.int32, shape, 0), lax.broadcasted_iota(jnp.int32, shape, 1)
    order = (source == (to % ROWS) * count + to // ROWS).astype(jnp.float32).astype(jnp.bfloat16)
    value = dot(order, gathered[...].reshape(ROWS * count, 2 * LANES))
    bank[0] = value[:, :LANES].reshape(count, ROWS, LANES)
    bank[1] = value[:, LANES:].reshape(count, ROWS, LANES)


def filter_kernel(energy, mine, others, bank, narrow, broad, out, spec, halves):
    core = lax.rem(lax.axis_index("tmpl"), 2)
    halves[:, core] = mine[...]
    halves[:, 1 - core] = others[...]
    segs = 2 * mine.shape[0] * mine.shape[1] // ROWS
    record = halves.reshape(segs, ROWS, LANES)
    own, count = out.shape
    half = GROUP * FINE
    w_low, w_high = broad[:ROWS][None], broad[ROWS:FINE][None]
    fwd_cos, fwd_sin = broad[FINE:2 * FINE][None], broad[2 * FINE:3 * FINE][None]
    inv_cos, inv_sin = broad[3 * FINE:4 * FINE][None], broad[4 * FINE:5 * FINE][None]
    high, low = narrow[:2 * FINE], narrow[2 * FINE:4 * FINE]
    spread = lambda part: jnp.concatenate(
        [block_diagonal(part[:FINE], part.shape[1] // GROUP), block_diagonal(part[FINE:], part.shape[1] // GROUP)]
    )
    first_high = spread(high)
    first = jnp.concatenate([first_high, first_high, spread(low)], axis=1)
    third_rows = narrow[4 * FINE:6 * FINE]
    third = jnp.concatenate([block_diagonal(third_rows[:FINE], ROWS), block_diagonal(third_rows[FINE:], ROWS)])
    second = slice(6 * FINE, 6 * FINE + 2 * LANES)
    fourth = slice(6 * FINE + 2 * LANES, 6 * FINE + 4 * LANES)

    def frames(start, last):
        here = record[pl.ds(start, GROUP)]
        if last:
            after = jnp.concatenate([record[pl.ds(start + 1, GROUP - 1)], record[pl.ds(0, 1)]], axis=0)
        else:
            after = record[pl.ds(start + 1, GROUP)]
        both = jnp.concatenate([here * w_low, after * w_high], axis=1)
        return both.reshape(half, LANES)

    def first_product(start, last):
        pair = jnp.concatenate([frames(start, False), frames(start + GROUP, last)], axis=1)
        high, low = split(pair)
        return dot(first, jnp.concatenate([high, low, high], axis=0))

    def second_product(step):
        sides = []
        for h in range(2):
            re = step[:half, h * LANES:(h + 1) * LANES].reshape(GROUP, FINE, LANES)
            im = step[half:, h * LANES:(h + 1) * LANES].reshape(GROUP, FINE, LANES)
            turned = jnp.concatenate([re * fwd_cos + im * fwd_sin, im * fwd_cos - re * fwd_sin], axis=2)
            high, low = split(turned.reshape(half, 2 * LANES))
            sides.append(jnp.concatenate([high, low], axis=1))
        return dot(jnp.concatenate(sides, axis=0), jnp.concatenate([narrow[second]] * 2, axis=0))

    def add_power(both, at, power):
        value = both[:, :LANES] + both[:, LANES:]
        spec[pl.ds(at * FINE, 2 * half)] = value
        return power + jnp.sum((value * value).reshape(2 * GROUP, FINE, LANES), axis=0)

    def whole(start, last, power):
        return add_power(second_product(first_product(start, last)), start, power)

    power = jnp.zeros((FINE, LANES), jnp.float32)
    pairs = segs // (2 * GROUP)
    stride = 2 * GROUP
    if pairs <= 4:
        steps = [first_product(i * stride, i == pairs - 1) for i in range(pairs)]
        waiting = None
        for i, step in enumerate(steps):
            both = second_product(step)
            if waiting is not None:
                power = add_power(*waiting, power)
            waiting = (both, i * stride)
        power = add_power(*waiting, power)
    else:
        power = lax.fori_loop(0, pairs - 1, lambda i, p: whole(i * stride, False, p), power)
        power = whole((pairs - 1) * stride, True, power)
    power = power + pltpu.roll(power, LANES // 2, 1)
    density = power / (segs * energy) + FLOOR
    density = natural(jnp.concatenate([density] * 4, axis=0).T, 0, None)
    inverse_density = 1.0 / density

    place = lax.axis_index("tm") * own
    column = lax.broadcasted_iota(jnp.int32, (GROUP, LANES), 1)

    def block(number, carry):
        at = pl.multiple_of((place + number * GROUP) * FINE, half)
        values = spec[pl.ds(at, half)].reshape(2, 4 * FINE, LANES)
        re_parts, im_parts = [], []
        for side in range(2):
            flipped = values[side].T
            for s in range(4):
                re_parts.append(natural(flipped, 0, s))
                im_parts.append(natural(flipped, LANES // 2, s))
        white_re, white_im = (
            (jnp.stack(parts) / density[None]).astype(jnp.bfloat16).astype(jnp.float32)
            for parts in (re_parts, im_parts)
        )

        def section_of(step):
            sides = []
            for m in (2 * step, 2 * step + 1):
                h_re, h_im = bank[0, m], bank[1, m]
                c_re = h_re[None] * white_re + h_im[None] * white_im
                c_im = h_re[None] * white_im - h_im[None] * white_re
                both = jnp.concatenate([c_re, c_im], axis=0).reshape(2 * GROUP * ROWS, LANES)
                sides.append(both.astype(jnp.bfloat16))
            return dot(third, jnp.concatenate(sides, axis=1))

        def waves_of(section):
            sides = []
            for side in range(2):
                re = section[:half, side * LANES:(side + 1) * LANES].reshape(GROUP, FINE, LANES)
                im = section[half:, side * LANES:(side + 1) * LANES].reshape(GROUP, FINE, LANES)
                turned = jnp.concatenate([re * inv_cos - im * inv_sin, re * inv_sin + im * inv_cos], axis=2)
                sides.append(turned.reshape(half, 2 * LANES).astype(jnp.bfloat16))
            return dot(jnp.concatenate(sides, axis=0), narrow[fourth])

        def peak_of(m, wave, result):
            square = wave[:, :LANES] * wave[:, :LANES] + wave[:, LANES:] * wave[:, LANES:]
            top = jnp.max(jnp.max(square.reshape(GROUP, FINE, LANES), axis=1), axis=1, keepdims=True)
            return jnp.where(column == m, top, result)

        result = jnp.zeros((GROUP, LANES), jnp.float32)
        ready, waiting = section_of(0), None
        for step in range(count // 2):
            section = ready
            if step + 1 < count // 2:
                ready = section_of(step + 1)
            waves = waves_of(section)
            if waiting is not None:
                for ready_peak in waiting:
                    result = peak_of(*ready_peak, result)
            waiting = [(2 * step + i, waves[i * half:(i + 1) * half]) for i in range(2)]
        for ready_peak in waiting:
            result = peak_of(*ready_peak, result)
        weight = jnp.sum((bank[0] * bank[0] + bank[1] * bank[1]) * inverse_density[None], axis=1)
        norm = jnp.sum(weight, axis=1, keepdims=True)
        spot = lax.broadcasted_iota(jnp.int32, (count, LANES), 0) == lax.broadcasted_iota(jnp.int32, (count, LANES), 1)
        norm = jnp.sum(jnp.where(spot, norm, 0.0), axis=0, keepdims=True)
        result = jnp.sqrt(result) / (jnp.sqrt(norm) * math.sqrt(energy))
        out[pl.ds(number * GROUP, GROUP)] = result[:, :count]
        return carry

    repeat(own // GROUP, block, 0)


def swap(array, axis, bits):
    return lax.ppermute(array, axis, [(i, i ^ bits) for i in range(lax.axis_size(axis))])


def on_device(strain, templates, cutoff):
    tm, devices = lax.axis_size("tm"), lax.axis_size("tm") * lax.axis_size("tmpl")
    size = strain.shape[0] // HOP
    segs = devices * size
    own = segs // tm
    count = templates.shape[1]
    vmem = pl.BlockSpec(memory_space=pltpu.VMEM)
    params = pltpu.CompilerParams(vmem_limit_bytes=40 * 1024 * 1024)
    f32 = jnp.float32

    chunk = strain.reshape(1, size * ROWS, LANES)
    copies = jnp.broadcast_to(chunk, (devices // 2, size * ROWS, LANES))
    copies, held = lax.optimization_barrier((copies, templates))
    copies = copies.reshape(devices, size * ROWS // 2, LANES)
    mine = lax.all_to_all(copies, ("tm", "tmpl"), split_axis=0, concat_axis=0, tiled=True)
    blocks = [swap(held, "tm", other) for other in range(1, tm)]
    mine, *blocks = lax.optimization_barrier((mine, *blocks))
    others = swap(mine, "tmpl", 1)
    blocks = [held] + blocks
    bank = pl.pallas_call(
        functools.partial(bank_kernel, tm),
        out_shape=jax.ShapeDtypeStruct((2, count, ROWS, LANES), f32),
        in_specs=[vmem] * (tm + 1),
        out_specs=vmem,
        scratch_shapes=[pltpu.VMEM((ROWS, count, 2 * LANES), jnp.bfloat16)],
        compiler_params=params,
        cost_estimate=pl.CostEstimate(flops=0, bytes_accessed=2500000, transcendentals=0),
        name="bank",
    )(*blocks, cutoff.reshape(1, count))
    narrow, broad, energy = tables()
    return pl.pallas_call(
        functools.partial(filter_kernel, energy),
        out_shape=jax.ShapeDtypeStruct((own, count), f32),
        in_specs=[vmem] * 5,
        out_specs=vmem,
        scratch_shapes=[
            pltpu.VMEM((segs * FINE, LANES), f32),
            pltpu.VMEM((devices, 2, size * ROWS // 2, LANES), f32),
        ],
        compiler_params=params,
        name="matched_filter",
    )(mine, others, bank, jnp.asarray(narrow), jnp.asarray(broad))


def solution(mesh):
    in_specs = (P(("tm", "tmpl")), P(None, "tmpl", "tm"), P("tmpl"))
    out_specs = P("tm", "tmpl")
    return jax.shard_map(
        on_device, mesh=mesh, in_specs=in_specs, out_specs=out_specs, check_vma=False
    )
```
